32 devices in a mesh: dp: 16 (over z, y, x), fsdp: 2 (over core).
Axes of the slice: x: 2, y: 2, z: 4, core: 2. Of those that a mesh axis runs over, the one named last changes fastest.
Arguments:
- block_input: bfloat16 [32, 576, 1024], P(('dp', 'fsdp')), may hold values from -6 to 6
- cotangent: bfloat16 [32, 576, 1024], P(('dp', 'fsdp')), may hold values from -6 to 6
- seg_ids: int32 [32, 576], P(('dp', 'fsdp')), may hold values from 0 to 3, never falling along the last dimension, each value on 1 to 288 neighbouring positions
- slot_valid: int32 [32, 576], P(('dp', 'fsdp')), may hold values from 0 to 1, as said below
- rel_buckets: int32 [32, 3, 576, 576], P(('dp', 'fsdp')), may hold values from 0 to 127
- w_qkv: bfloat16 [1024, 3072], P(('dp', 'fsdp')), may hold values from -0.1875 to 0.1875
- w_out: bfloat16 [1024, 1024], P(('dp', 'fsdp')), may hold values from -1.5 to 1.5
- w_in: bfloat16 [1024, 4096], P(('dp', 'fsdp')), may hold values from -0.1875 to 0.1875
- w_down: bfloat16 [4096, 1024], P(('dp', 'fsdp')), may hold values from -0.09375 to 0.09375
- vec_bias: bfloat16 [6, 1024], P(None, ('dp', 'fsdp')), may hold values from -3 to 3
- norm_gain: bfloat16 [2, 1024], P(None, ('dp', 'fsdp')), may hold values from 0.25 to 1.75
- bias_hidden: bfloat16 [4096], P(('dp', 'fsdp')), may hold values from -3 to 3
- rel_tables: bfloat16 [6144], P(('dp', 'fsdp')), may hold values from -3 to 3
Outputs:
- block_output: bfloat16 [32, 576, 1024], P(('dp', 'fsdp'))
- grad_input: float32 [32, 576, 1024], P(('dp', 'fsdp'))
- grad_w_qkv: float32 [1024, 3072], P(('dp', 'fsdp'))
- grad_w_out: float32 [1024, 1024], P(('dp', 'fsdp'))
- grad_w_in: float32 [1024, 4096], P(('dp', 'fsdp'))
- grad_w_down: float32 [4096, 1024], P(('dp', 'fsdp'))
- grad_vec_bias: float32 [6, 1024], P(None, ('dp', 'fsdp'))
- grad_norm_gain: float32 [2, 1024], P(None, ('dp', 'fsdp'))
- grad_bias_hidden: float32 [4096], P(('dp', 'fsdp'))
- grad_rel_tables: float32 [6144], P(('dp', 'fsdp'))
The draws below stay inside these ranges and needn't reach their ends.
Inputs may be any that keep to these rules, and one draw needn't show every extreme that they name: `seg_ids`: document numbers never fall along a row; a document holds 1 to 288 slots. `slot_valid`: in each row the used slots come first and number at least 432; row 0 is full.
All inputs are finite; a program needn't handle non-finite values.
Results may differ from the reference program's by a relative error of at most 0.013.
The reference program's roundings to bfloat16 on the way count: a program that leaves them out, or rounds other values in their place, can miss the bound.
Values may be sent and summed in bfloat16 or wider, within the bound.
A program may use at most 192 MiB of HBM per device.

```python
import math
import jax
import jax.numpy as jnp
import numpy as np
from jax import lax

D = 1024
H = 16
FF = 4096
NB = 128
ROW_LEN = 576
SEGS = 4
SEG_MOST = 288
ROWS = 32


def draw_slot_valid(key, part):
    padding = jax.random.randint(key, (ROWS,), 0, ROW_LEN // 4 + 1, dtype=jnp.int32)
    filled = ROW_LEN - padding.at[0].set(0)
    position = jnp.arange(ROW_LEN, dtype=jnp.int32)
    return (position[None, :] < filled[:, None]).astype(jnp.int32)


def touch_ends(values, rng, least, largest):
    longest = values.shape.index(max(values.shape))
    spots = []
    for shift in (0, 1):
        where = [jax.random.randint(jax.random.fold_in(rng, axis), (), 0, length) for axis, length in enumerate(values.shape)]
        where[longest] = (where[longest] + shift) % values.shape[longest]
        spots.append(tuple(where))
    return values.at[spots[0]].set(least).at[spots[1]].set(largest)


def strengthened(values, rng, source, target, blocks, factor):
    def block_of(axis_at):
        return (jnp.arange(values.shape[axis_at]) // (values.shape[axis_at] // blocks)).reshape((-1,) + (1,) * (values.ndim - 1 - axis_at))

    one_side = jax.random.permutation(rng, blocks)[block_of(target)]
    second = (block_of(target) + blocks // 2) % blocks
    return jnp.where((block_of(source) == one_side) | (block_of(source) == second), factor * values, values)


def block_levels(key, dims, shards, smallest, top_value):
    level = 1.0
    for axis_at, shards_of in shards:
        heights = jax.random.uniform(jax.random.fold_in(jax.random.fold_in(key, 6), axis_at), (shards_of,), jnp.float32, smallest / len(shards), top_value / len(shards))
        level = level * jnp.repeat(jnp.exp(heights), dims[axis_at] // shards_of).reshape((-1,) + (1,) * (len(dims) - 1 - axis_at))
    return level


def length_profile(amount, total, bound, skew):
    weights = [(1 << 20) // math.isqrt(rank ** skew) + 1 for rank in range(2, amount + 1)]
    rest, holding = total - bound - (amount - 1), [1] * (amount - 1)
    while rest > 0:
        candidates = [i for i in range(amount - 1) if holding[i] < bound]
        mass, remaining = sum([weights[i] for i in candidates]), rest
        for i in candidates:
            addition = min(bound - holding[i], max(1, remaining * weights[i] // mass), rest)
            holding[i] = holding[i] + addition
            rest = rest - addition
    return np.array([bound] + holding)


def uneven(key, count, total, limit, skew):
    if count == 2:
        one = jax.random.randint(key, (), max(1, total - limit), min(limit, total - 1) + 1)
        return jnp.stack([one, total - one])
    lengths = jnp.asarray(length_profile(count, total, limit, skew), jnp.int32)
    twos = (count - 1) // 2
    source_of, receiver = lengths[1:1 + 2 * twos:2], lengths[2:2 + 2 * twos:2]
    margin = jnp.minimum(source_of - 1, limit - receiver)
    shifted = jax.random.randint(jax.random.fold_in(key, 1), (twos,), 0, 1 << 20) % (margin + 1)
    lengths = lengths.at[1:1 + 2 * twos:2].set(source_of - shifted).at[2:2 + 2 * twos:2].set(receiver + shifted)
    return lengths[jax.random.permutation(jax.random.fold_in(key, 2), count)]


def noise(own_key, dims, deviation, reach, shards=(), held_as=jnp.bfloat16):
    array = jax.random.normal(own_key, dims, jnp.float32) * deviation
    if len(shards) > 0:
        array = block_levels(own_key, dims, shards, -0.22, 0.18) * array
    return jnp.clip(array, min=-reach, max=reach).astype(held_as)


def heavy_noise(own_key, extent, spread, reach, split, heavy, kind=jnp.bfloat16):
    entries = spread * jax.random.normal(own_key, extent, jnp.float32)
    if split:
        entries = entries * block_levels(own_key, extent, split, -0.22, 0.18)
    return jnp.clip(strengthened(entries, jax.random.fold_in(own_key, 3), *heavy), -reach, reach).astype(kind)


def setup_inputs(seed: int = 0) -> dict:
    key_list = jax.random.split(jax.random.key(seed), 14)
    return {
        "block_input": heavy_noise(key_list[0], (ROWS, ROW_LEN, D), 1.0, 6.0, ((0, 32),), (0, 2, 32, 2.75)),
        "cotangent": noise(key_list[1], (ROWS, ROW_LEN, D), 1.0, 6.0, ((0, 32),)),
        "seg_ids": jax.vmap(lambda own: jnp.searchsorted(jnp.cumsum(uneven(own, SEGS, ROW_LEN, SEG_MOST, 2)), jnp.arange(ROW_LEN), side="right"))(jax.random.split(key_list[2], ROWS)).reshape((ROWS, ROW_LEN)).astype(jnp.int32),
        "slot_valid": draw_slot_valid(jax.random.fold_in(key_list[13], 71), 0),
        "rel_buckets": touch_ends(jax.random.randint(key_list[4], (ROWS, 3, ROW_LEN, ROW_LEN), 0, NB), jax.random.fold_in(key_list[4], 1), 0, NB - 1).astype(jnp.int32),
        "w_qkv": noise(key_list[5], (D, 3 * D), D ** -0.5, 0.1875, ((0, 32),)),
        "w_out": noise(key_list[6], (D, D), (D // 64) ** -0.5, 1.5, ((0, 32),)),
        "w_in": noise(key_list[7], (D, FF), D ** -0.5, 0.1875, ((0, 32),)),
        "w_down": noise(key_list[8], (FF, D), FF ** -0.5, 0.09375, ((0, 32),)),
        "vec_bias": noise(key_list[9], (6, D), 0.5, 3.0, ((1, 32),)),
        "norm_gain": jnp.clip(1.0 + 0.15 * jax.random.normal(key_list[10], (2, D), jnp.float32), 0.25, 1.75).astype(jnp.bfloat16),
        "bias_hidden": noise(key_list[11], (FF,), 0.5, 3.0, ((0, 32),)),
        "rel_tables": noise(key_list[12], (3 * NB * H,), 0.5, 3.0, ((0, 32),)),
    }


@jax.custom_vjp
def low(v):
    return lax.optimization_barrier(v.astype(jnp.bfloat16)).astype(jnp.float32)

@jax.custom_vjp
def low_back(v):
    return v

def low_keep(v):
    return (low(v), None)

def low_pass(kept, grad):
    return (grad,)

def back_keep(v):
    return (v, None)

def back_low(kept, grad):
    return (low(grad),)
low.defvjp(low_keep, low_pass)
low_back.defvjp(back_keep, back_low)
EPSILON = 1e-05
MASK_FILL = -1e+30
HIGHEST_MODE = lax.Precision.HIGHEST

def rounded_both(value):
    return low(low_back(value))

def layer_norm(inputs, gain_row, shift_row):
    average = lax.optimization_barrier(jnp.mean(inputs, axis=-1, keepdims=True))
    centered = inputs - average
    variance = lax.optimization_barrier(jnp.mean(centered * centered, axis=-1, keepdims=True))
    return centered * lax.rsqrt(variance + EPSILON) * gain_row + shift_row

def row_forward(weights, row_in, segments, validity, buckets):
    w_qkv, w_out, w_in, w_down, vec_bias, norm_gain, bias_hidden, tables = weights
    length = row_in.shape[0]
    model_width = w_out.shape[0]
    head_size = model_width // H
    scale = head_size ** (-0.5)
    mixed = jnp.dot(row_in, w_qkv, precision=HIGHEST_MODE)
    queries = rounded_both(mixed[:, :model_width] + vec_bias[0]).reshape(length, H, head_size)
    key_rows = rounded_both(mixed[:, model_width:2 * model_width]).reshape(length, H, head_size)
    value_rows = rounded_both(mixed[:, 2 * model_width:] + vec_bias[1]).reshape(length, H, head_size)
    spatial = tables[0][buckets[0]] + tables[1][buckets[1]] + tables[2][buckets[2]]
    raw_scores = jnp.einsum('qhd,khd->hqk', queries, key_rows, precision=HIGHEST_MODE) * scale
    scores = low_back(raw_scores + jnp.moveaxis(spatial, 2, 0))
    position = jnp.arange(length)
    allowed = (segments[:, None] == segments[None, :]) & ((validity[None, :] > 0) | (position[:, None] == position[None, :]))
    masked = jnp.where(allowed[None], scores, MASK_FILL)
    top_score = lax.optimization_barrier(jnp.max(masked, axis=-1, keepdims=True))
    exponent = jnp.exp(masked - top_score)
    probability = low(exponent / lax.optimization_barrier(jnp.sum(exponent, axis=-1, keepdims=True)))
    context = rounded_both(jnp.einsum('hqk,khd->qhd', probability, value_rows, precision=HIGHEST_MODE).reshape(length, model_width))
    branch = low_back(jnp.dot(context, w_out, precision=HIGHEST_MODE) + vec_bias[2])
    normed_first = layer_norm(row_in + branch, norm_gain[0], vec_bias[4])
    hidden = low_back(jnp.dot(low(normed_first), w_in, precision=HIGHEST_MODE) + bias_hidden)
    active = low(jax.nn.gelu(hidden, approximate=False))
    down_out = low_back(jnp.dot(active, w_down, precision=HIGHEST_MODE) + vec_bias[3])
    return layer_norm(normed_first + down_out, norm_gain[1], vec_bias[5])

def reference(block_input, cotangent, seg_ids, slot_valid, rel_buckets, w_qkv, w_out, w_in, w_down, vec_bias, norm_gain, bias_hidden, rel_tables):
    weights = (w_qkv.astype(jnp.float32), w_out.astype(jnp.float32), w_in.astype(jnp.float32), w_down.astype(jnp.float32), vec_bias.astype(jnp.float32), norm_gain.astype(jnp.float32), bias_hidden.astype(jnp.float32), rel_tables.astype(jnp.float32).reshape(3, NB, H))

    def row_step(totals, row_data):
        row_in, row_cot, segments, validity, buckets = row_data

        def forward(inputs, layer_weights):
            return row_forward(layer_weights, inputs, segments, validity, buckets)
        result, pullback = jax.vjp(forward, row_in.astype(jnp.float32), weights)
        grad_in, grad_weights = pullback(row_cot.astype(jnp.float32))
        return (jax.tree.map(jnp.add, totals, grad_weights), (result.astype(jnp.bfloat16), grad_in))
    initial = jax.tree.map(jnp.zeros_like, weights)
    totals, (outputs, grad_input) = lax.scan(row_step, initial, (block_input, cotangent, seg_ids, slot_valid, rel_buckets))
    return (outputs, grad_input, totals[0], totals[1], totals[2], totals[3], totals[4], totals[5], totals[6], totals[7].reshape(-1))
```

```python
import functools
import itertools

import jax
import jax.numpy as jnp
from jax import lax
from jax.experimental import pallas as pl
from jax.experimental.pallas import tpu as pltpu
from jax.sharding import PartitionSpec as P

H = 16
NB = 128
LANES = 128
EPSILON = 1e-05
MASK_FILL = -1e30
TABLE_STEP = 8192.0
VMEM_BYTES = 60 << 20
BOTH = ("dp", "fsdp")
MESH = pl.DeviceIdType.MESH
DIMS = (4, 2, 2)
GATHER_ORDERS = ((0, 2, 1), (0, 1, 2), (2, 1, 0))
STEPS = 5
LAG = 2
SMALL_ROWS = 16
SMALL_GRAD_ROWS = 8
GRAD_TILE = 64
HIGH_PARTS = 4
LOW_PARTS = NB // HIGH_PARTS


def dot_plain(left, right):
    return jnp.dot(left, right, preferred_element_type=jnp.float32)


def dot_first(left, right):
    return lax.dot_general(
        left, right, (((0,), (0,)), ((), ())), preferred_element_type=jnp.float32
    )


def dot_last(left, right):
    return lax.dot_general(
        left, right, (((1,), (1,)), ((), ())), preferred_element_type=jnp.float32
    )


def layer_norm(inputs, gain_row, shift_row):
    average = jnp.mean(inputs, axis=-1, keepdims=True)
    centered = inputs - average
    variance = jnp.mean(centered * centered, axis=-1, keepdims=True)
    return centered * lax.rsqrt(variance + EPSILON) * gain_row + shift_row


def gelu_exact(inputs):
    return jax.nn.gelu(inputs, approximate=False)


def coordinates():
    chip = lax.axis_index("dp")
    core = lax.axis_index("fsdp")
    planes, rows, columns = DIMS
    place = (
        chip // (rows * columns),
        lax.rem(chip // columns, rows),
        lax.rem(chip, columns),
    )
    return place, core


def device_at(place, core):
    return ((place[0] * DIMS[1] + place[1]) * DIMS[2] + place[2], core)


def shifted(place, axis, distance):
    moved = list(place)
    moved[axis] = lax.rem(moved[axis] + distance, DIMS[axis])
    return tuple(moved)


def greet(place, core):
    barrier = pltpu.get_barrier_semaphore()
    peers = [
        device_at(shifted(place, axis, distance), core)
        for axis in range(3)
        for distance in range(1, DIMS[axis])
    ]
    peers.append(device_at(place, 1 - core))
    for peer in peers:
        pl.semaphore_signal(barrier, inc=1, device_id=peer, device_id_type=MESH)
    pl.semaphore_wait(barrier, len(peers))


def schedule(waves, lag):
    events = []
    for wave in range(waves):
        for step in range(STEPS):
            events.append((wave + lag * step, wave, step))
    return [(wave, step) for slot, wave, step in sorted(events)]


def wave_of(array, row, rows, column, *tiles):
    bounds = [column]
    for count in tiles:
        bounds.append(bounds[-1] + count * LANES)
    return (array, row, rows, tuple(bounds))


def hops_before(order, phase):
    return sum(DIMS[axis] - 1 for axis in order[:phase])


def gather_steps(wave, number, full, send, recv, place, core):
    array, row, rows, bounds = wave
    whole = full[array]
    routes = [r for r in range(len(GATHER_ORDERS)) if bounds[r + 1] > bounds[r]]
    total_hops = hops_before(GATHER_ORDERS[0], 3)
    started = []
    arriving = {}
    from_core = []

    def copy(route, slot, index, target):
        part = whole.at[
            index[0], index[1], index[2], core,
            pl.ds(row, rows), pl.ds(bounds[route], bounds[route + 1] - bounds[route]),
        ]
        made = pltpu.make_async_remote_copy(
            part, part, send.at[number, route, slot], recv.at[number, route, slot],
            device_id=target, device_id_type=MESH,
        )
        made.start()
        started.append(made)
        return made

    def to_core(route, slot, index):
        from_core.append(copy(route, total_hops + slot, index, device_at(place, 1 - core)))

    def launch(phase):
        for route in routes:
            order = GATHER_ORDERS[route]
            index = list(place)
            for axis in order[:phase]:
                index[axis] = slice(None)
            for distance in range(1, DIMS[order[phase]]):
                arriving[route, phase, distance] = copy(
                    route, hops_before(order, phase) + distance - 1, index,
                    device_at(shifted(place, order[phase], distance), core),
                )

    def land(phase):
        for route in routes:
            order = GATHER_ORDERS[route]
            axis = order[phase]
            for distance in range(1, DIMS[axis]):
                arriving[route, phase, distance].wait_recv()
                index = list(place)
                for done in order[:phase]:
                    index[done] = slice(None)
                index[axis] = lax.rem(place[axis] + DIMS[axis] - distance, DIMS[axis])
                to_core(route, 1 + hops_before(order, phase) + distance - 1, index)

    def first():
        for route in routes:
            to_core(route, 0, list(place))
        launch(0)

    def second():
        land(0)
        launch(1)

    def third():
        land(1)
        launch(2)

    def fourth():
        land(2)

    def fifth():
        for made in from_core:
            made.wait_recv()
        for made in started:
            made.wait_send()

    return [first, second, third, fourth, fifth]


def gather_kernel(waves, arrays, *refs):
    shards = refs[:arrays]
    outs = refs[arrays : 2 * arrays]
    local_sem, send, recv, out_sem = refs[2 * arrays : 2 * arrays + 4]
    full = refs[2 * arrays + 4 :]
    place, core = coordinates()
    own = [
        pltpu.make_async_copy(
            shards[i], full[i].at[place[0], place[1], place[2], core], local_sem.at[i]
        )
        for i in range(arrays)
    ]
    for copy in own:
        copy.start()
    greet(place, core)
    steps = [
        gather_steps(wave, number, full, send, recv, place, core)
        for number, wave in enumerate(waves)
    ]
    for copy in own:
        copy.wait()
    leaving = []
    for number, step in schedule(len(waves), LAG):
        steps[number][step]()
        if step == STEPS - 1:
            array, row, rows, bounds = waves[number]
            part = (slice(None),) * 4 + (
                pl.ds(row, rows), pl.ds(bounds[0], bounds[-1] - bounds[0]),
            )
            out = pltpu.make_async_copy(
                full[array].at[part], outs[array].at[part], out_sem.at[number]
            )
            out.start()
            leaving.append(out)
    for out in leaving:
        out.wait()


def gather_all(shards, waves, collective):
    arrays = len(shards)
    routes = len(GATHER_ORDERS)
    hops = 2 * hops_before(GATHER_ORDERS[0], 3) + 1
    return pl.pallas_call(
        functools.partial(gather_kernel, waves, arrays),
        in_specs=[pl.BlockSpec(memory_space=pl.ANY)] * arrays,
        out_specs=[pl.BlockSpec(memory_space=pl.ANY)] * arrays,
        out_shape=[
            jax.ShapeDtypeStruct(DIMS + (2,) + shard.shape, shard.dtype) for shard in shards
        ],
        scratch_shapes=[
            pltpu.SemaphoreType.DMA((arrays,)),
            pltpu.SemaphoreType.DMA((len(waves), routes, hops)),
            pltpu.SemaphoreType.DMA((len(waves), routes, hops)),
            pltpu.SemaphoreType.DMA((len(waves),)),
        ]
        + [pltpu.VMEM(DIMS + (2,) + shard.shape, shard.dtype) for shard in shards],
        compiler_params=pltpu.CompilerParams(
            collective_id=collective, has_side_effects=True, vmem_limit_bytes=VMEM_BYTES
        ),
    )(*shards)


def reduce_orders():
    return [tuple(reversed(order)) for order in GATHER_ORDERS]


def axes_left(order, phase):
    return [axis for axis in range(3) if axis not in order[: phase + 1]]


def scatter_scratch(waves, dtypes):
    shapes = []
    for array, row, rows, bounds in waves:
        dtype = dtypes[array]
        block = DIMS + (rows, bounds[-1] - bounds[0])
        shapes += [pltpu.VMEM(block, dtype), pltpu.VMEM(block, dtype)]
        for route, order in enumerate(reduce_orders()):
            width = bounds[route + 1] - bounds[route]
            for phase in range(3 if width else 0):
                left = tuple(DIMS[axis] for axis in axes_left(order, phase))
                shapes.append(
                    pltpu.VMEM((DIMS[order[phase]] - 1,) + left + (rows, width), dtype)
                )
    return shapes


def scatter_steps(wave, number, grads, outs, scratch, local_sem, send, recv, place, core):
    array, row, rows, bounds = wave
    grad = grads[array]
    base = bounds[0]
    width = bounds[-1] - base
    total = next(scratch)
    other = next(scratch)
    orders = reduce_orders()
    routes = [r for r in range(len(orders)) if bounds[r + 1] > bounds[r]]
    landing = {}
    for route in routes:
        for phase in range(3):
            landing[route, phase] = next(scratch)
    core_slot = hops_before(orders[0], 3)
    started = []
    arriving = {}
    every = slice(None)

    def half(which):
        return grad.at[:, :, :, which, pl.ds(row, rows), pl.ds(base, width)]

    def first():
        arriving["own"] = pltpu.make_async_copy(half(core), total, local_sem.at[number])
        arriving["own"].start()
        made = pltpu.make_async_remote_copy(
            half(1 - core), other, send.at[number, 0, core_slot], recv.at[number, 0, core_slot],
            device_id=device_at(place, 1 - core), device_id_type=MESH,
        )
        made.start()
        started.append(made)
        arriving["core"] = made

    def launch(phase):
        for route in routes:
            order = orders[route]
            axis = order[phase]
            for distance in range(1, DIMS[axis]):
                index = [every] * 3
                for done in order[:phase]:
                    index[done] = place[done]
                index[axis] = lax.rem(place[axis] + distance, DIMS[axis])
                slot = hops_before(order, phase) + distance - 1
                made = pltpu.make_async_remote_copy(
                    total.at[
                        index[0], index[1], index[2], :,
                        pl.ds(bounds[route] - base, bounds[route + 1] - bounds[route]),
                    ],
                    landing[route, phase].at[distance - 1],
                    send.at[number, route, slot], recv.at[number, route, slot],
                    device_id=device_at(shifted(place, axis, distance), core),
                    device_id_type=MESH,
                )
                made.start()
                started.append(made)
                arriving[route, phase, distance] = made

    def land(phase):
        for route in routes:
            order = orders[route]
            axis = order[phase]
            for distance in range(1, DIMS[axis]):
                arriving[route, phase, distance].wait_recv()
            left = axes_left(order, phase)
            columns = slice(bounds[route] - base, bounds[route + 1] - base)
            for spot in itertools.product(*[range(DIMS[a]) for a in left]):
                index = list(place)
                for a, value in zip(left, spot):
                    index[a] = value
                at = (index[0], index[1], index[2], every, columns)
                added = total[at].astype(jnp.float32)
                for distance in range(1, DIMS[axis]):
                    added += landing[route, phase][(distance - 1,) + spot].astype(jnp.float32)
                if phase == 2:
                    outs[array][pl.ds(row, rows), bounds[route] : bounds[route + 1]] = added
                else:
                    total[at] = added.astype(total.dtype)

    def second():
        arriving["own"].wait()
        arriving["core"].wait_recv()

        def one_plane(plane, carry):
            for y, x in itertools.product(range(DIMS[1]), range(DIMS[2])):
                total[plane, y, x] = total[plane, y, x] + other[plane, y, x]
            return carry

        lax.fori_loop(0, DIMS[0], one_plane, 0)
        launch(0)

    def third():
        land(0)
        launch(1)

    def fourth():
        land(1)
        launch(2)

    def fifth():
        land(2)
        for made in started:
            made.wait_send()

    return [first, second, third, fourth, fifth]


def scatter_kernel(waves, arrays, *refs):
    grads = refs[:arrays]
    outs = refs[arrays : 2 * arrays]
    local_sem, send, recv = refs[2 * arrays : 2 * arrays + 3]
    scratch = iter(refs[2 * arrays + 3 :])
    place, core = coordinates()
    greet(place, core)
    steps = [
        scatter_steps(wave, number, grads, outs, scratch, local_sem, send, recv, place, core)
        for number, wave in enumerate(waves)
    ]
    for number, step in schedule(len(waves), LAG):
        steps[number][step]()


def scatter_all(grads, waves, collective):
    arrays = len(grads)
    sems = (len(waves), len(GATHER_ORDERS), hops_before(GATHER_ORDERS[0], 3) + 1)
    return pl.pallas_call(
        functools.partial(scatter_kernel, waves, arrays),
        in_specs=[pl.BlockSpec(memory_space=pl.ANY)] * arrays,
        out_specs=[pl.BlockSpec(memory_space=pltpu.VMEM)] * arrays,
        out_shape=[jax.ShapeDtypeStruct(grad.shape[4:], jnp.float32) for grad in grads],
        scratch_shapes=[
            pltpu.SemaphoreType.DMA((len(waves),)),
            pltpu.SemaphoreType.DMA(sems),
            pltpu.SemaphoreType.DMA(sems),
        ]
        + scatter_scratch(waves, [grad.dtype for grad in grads]),
        compiler_params=pltpu.CompilerParams(
            collective_id=collective, has_side_effects=True, vmem_limit_bytes=VMEM_BYTES
        ),
    )(*grads)


def split_wave(array, row, rows, column, tiles, turn):
    edge = tiles // 8
    one = (tiles - edge + turn) // 2
    return wave_of(array, row, rows, column, one, tiles - edge - one, edge)


def weight_waves(array, rows, columns, row_step, tile_step):
    waves = []
    tiles = columns // LANES
    for row in range(0, rows, row_step):
        for tile in range(0, tiles, tile_step):
            size = min(tile_step, tiles - tile)
            waves.append(
                split_wave(array, row, row_step, tile * LANES, size, (len(waves) + array) % 2)
            )
    return waves


def attention_forward_kernel(
    key_ref, query_ref, value_ref, packed_ref, table_ref, mask_ref, probs_ref, context_ref,
    score_ref,
):
    length = key_ref.shape[0]
    padded = packed_ref.shape[1]
    pair = query_ref.shape[0]
    half = pair // 2
    feature = lax.broadcasted_iota(jnp.int32, (pair, padded), 0)
    queries = query_ref[...]
    zero = jnp.zeros_like(queries)
    score_ref[0] = dot_plain(key_ref[...], jnp.where(feature < half, queries, zero))
    score_ref[1] = dot_plain(key_ref[...], jnp.where(feature < half, zero, queries))
    for column in range(0, padded, LANES):
        lanes = slice(column, column + LANES)
        rows = [jnp.broadcast_to(table_ref[t, 0], (8, LANES)) for t in range(3)]
        tops = [jnp.full((8, LANES), 3.0 * MASK_FILL, jnp.float32) for side in range(2)]
        for start in range(0, length, 8):
            here = slice(start, start + 8)
            packed = packed_ref[here, lanes]
            sums = [None, None]
            for table in range(3):
                index = (packed >> (7 * table)) & (NB - 1)
                word = jnp.take_along_axis(rows[table], index, axis=1)
                for side, term in ((0, word >> 16), (1, (word << 16) >> 16)):
                    sums[side] = term if table == 0 else sums[side] + term
            mask = mask_ref[here, lanes]
            for side in range(2):
                scores = score_ref[side, here, lanes] + (
                    sums[side].astype(jnp.float32) * (1.0 / TABLE_STEP) + mask
                )
                score_ref[side, here, lanes] = scores
                tops[side] = jnp.maximum(tops[side], scores)
        for side in range(2):
            top = jnp.max(tops[side], axis=0, keepdims=True)
            exponent = jnp.exp(score_ref[side, :, lanes] - top)
            total = jnp.sum(exponent, axis=0, keepdims=True)
            probs_ref[side, :, lanes] = (exponent * (1.0 / total)).astype(jnp.bfloat16)
    for side in range(2):
        mine = slice(side * half, (side + 1) * half)
        context_ref[mine, :] = dot_plain(value_ref[mine, :], probs_ref[side]).astype(jnp.bfloat16)


def attention_forward(keys, queries_t, values_t, packed, tables, mask):
    length, width = keys.shape
    padded = packed.shape[1]
    pairs = H // 2
    pair = width // pairs
    whole = pl.BlockSpec((length, padded), lambda p: (0, 0))
    return pl.pallas_call(
        attention_forward_kernel,
        grid=(pairs,),
        in_specs=[
            pl.BlockSpec((length, pair), lambda p: (0, p)),
            pl.BlockSpec((pair, padded), lambda p: (p, 0)),
            pl.BlockSpec((pair, length), lambda p: (p, 0)),
            whole,
            pl.BlockSpec((3, 1, 1, NB), lambda p: (0, p, 0, 0)),
            whole,
        ],
        out_specs=[
            pl.BlockSpec((2, length, padded), lambda p: (p, 0, 0)),
            pl.BlockSpec((pair, padded), lambda p: (p, 0)),
        ],
        out_shape=[
            jax.ShapeDtypeStruct((H, length, padded), jnp.bfloat16),
            jax.ShapeDtypeStruct((width, padded), jnp.bfloat16),
        ],
        scratch_shapes=[pltpu.VMEM((2, length, padded), jnp.float32)],
        compiler_params=pltpu.CompilerParams(vmem_limit_bytes=VMEM_BYTES),
    )(keys, queries_t, values_t, packed, tables, mask)


def attention_backward_kernel(
    value_ref, context_grad_t_ref, context_grad_ref, query_ref, key_t_ref, probs_ref,
    grad_query_ref, grad_key_ref, grad_value_ref, score_grad_ref, prob_grad_ref, low_ref,
):
    length = value_ref.shape[0]
    pair, padded = context_grad_t_ref.shape
    half = pair // 2
    scale = half ** (-0.5)
    feature = lax.broadcasted_iota(jnp.int32, (pair, padded), 0)
    upstream = context_grad_t_ref[...]
    zero = jnp.zeros_like(upstream)
    prob_grad_ref[0] = dot_plain(value_ref[...], jnp.where(feature < half, upstream, zero))
    prob_grad_ref[1] = dot_plain(value_ref[...], jnp.where(feature < half, zero, upstream))
    for part in range(padded // LANES):
        lanes = slice(part * LANES, (part + 1) * LANES)
        for side in range(2):
            probs = probs_ref[side, :, lanes].astype(jnp.float32)
            prob_grad = prob_grad_ref[side, :, lanes]
            inner = jnp.sum(probs * prob_grad, axis=0, keepdims=True)
            score_grad = probs * (prob_grad - inner)
            score_grad_ref[part, side] = score_grad
            low_ref[side, :, lanes] = score_grad.astype(jnp.bfloat16)
    for side in range(2):
        mine = slice(side * half, (side + 1) * half)
        grad_query_ref[mine, :] = (dot_plain(key_t_ref[mine, :], low_ref[side]) * scale).astype(
            jnp.bfloat16
        )
    first_half = lax.broadcasted_iota(jnp.int32, (length, pair), 1) < half
    grad_key = [dot_plain(low_ref[side], query_ref[...]) for side in range(2)]
    grad_key_ref[...] = jnp.where(first_half, grad_key[0], grad_key[1]).astype(jnp.bfloat16)
    grad_value = [dot_plain(probs_ref[side], context_grad_ref[...]) for side in range(2)]
    grad_value_ref[...] = jnp.where(first_half, grad_value[0], grad_value[1]).astype(jnp.bfloat16)


def attention_backward(values, context_grad_t, context_grad, queries, keys_t, probs):
    length, width = values.shape
    padded = probs.shape[2]
    pairs = H // 2
    pair = width // pairs
    natural = pl.BlockSpec((length, pair), lambda p: (0, p))
    longer = pl.BlockSpec((padded, pair), lambda p: (0, p))
    flipped = pl.BlockSpec((pair, padded), lambda p: (p, 0))
    return pl.pallas_call(
        attention_backward_kernel,
        grid=(pairs,),
        in_specs=[
            natural,
            flipped,
            longer,
            longer,
            pl.BlockSpec((pair, length), lambda p: (p, 0)),
            pl.BlockSpec((2, length, padded), lambda p: (p, 0, 0)),
        ],
        out_specs=[
            flipped,
            natural,
            natural,
            pl.BlockSpec((padded // LANES, 2, length, LANES), lambda p: (0, p, 0, 0)),
        ],
        out_shape=[
            jax.ShapeDtypeStruct((width, padded), jnp.bfloat16),
            jax.ShapeDtypeStruct((length, width), jnp.bfloat16),
            jax.ShapeDtypeStruct((length, width), jnp.bfloat16),
            jax.ShapeDtypeStruct((padded // LANES, H, length, LANES), jnp.float32),
        ],
        scratch_shapes=[
            pltpu.VMEM((2, length, padded), jnp.float32),
            pltpu.VMEM((2, length, padded), jnp.bfloat16),
        ],
        compiler_params=pltpu.CompilerParams(vmem_limit_bytes=VMEM_BYTES),
    )(values, context_grad_t, context_grad, queries, keys_t, probs)


def table_grad_kernel(digit_ref, score_grad_ref, out_ref):
    padded = score_grad_ref.shape[0] * LANES

    @pl.when(pl.program_id(0) == 0)
    def start():
        out_ref[...] = jnp.zeros_like(out_ref)

    levels = lax.broadcasted_iota(jnp.int32, (LOW_PARTS, padded), 0).astype(jnp.bfloat16)
    one = jnp.ones((LOW_PARTS, padded), jnp.bfloat16)
    no_one = jnp.zeros((LOW_PARTS, padded), jnp.bfloat16)
    nothing = jnp.zeros((H, padded), jnp.bfloat16)
    flat_ref = score_grad_ref.reshape(padded // LANES * H * GRAD_TILE, LANES)

    def one_group(group, total):
        for offset in range(4):
            row = group * 4 + offset
            grads = jnp.concatenate(
                [
                    flat_ref[pl.ds(part * H * GRAD_TILE + row, H, stride=GRAD_TILE), :]
                    for part in range(padded // LANES)
                ],
                axis=1,
            ).astype(jnp.bfloat16)
            masked = []
            onehot = []
            for table in range(3):
                high = jnp.broadcast_to(digit_ref[row, table : table + 1, :], (H, padded))
                for part in range(HIGH_PARTS):
                    masked.append(jnp.where(high == jnp.bfloat16(part), grads, nothing))
                low = jnp.broadcast_to(digit_ref[row, 3 + table : 4 + table, :], (LOW_PARTS, padded))
                onehot.append(jnp.where(low == levels, one, no_one))
            total = total + dot_last(jnp.concatenate(masked, axis=0), jnp.concatenate(onehot, axis=0))
        return total

    out_ref[...] += lax.fori_loop(
        0, GRAD_TILE // 4, one_group, jnp.zeros(out_ref.shape, jnp.float32)
    )


def table_grads(digits, score_grad):
    length = score_grad.shape[2]
    padded = score_grad.shape[0] * LANES
    shape = (3 * HIGH_PARTS * H, 3 * LOW_PARTS)
    products = pl.pallas_call(
        table_grad_kernel,
        grid=(length // GRAD_TILE,),
        in_specs=[
            pl.BlockSpec((GRAD_TILE, 6, padded), lambda i: (i, 0, 0)),
            pl.BlockSpec((padded // LANES, H, GRAD_TILE, LANES), lambda i: (0, 0, i, 0)),
        ],
        out_specs=pl.BlockSpec(shape, lambda i: (0, 0)),
        out_shape=jax.ShapeDtypeStruct(shape, jnp.float32),
        compiler_params=pltpu.CompilerParams(vmem_limit_bytes=VMEM_BYTES),
    )(digits, score_grad)
    split = products.reshape(3, HIGH_PARTS, H, 3, LOW_PARTS)
    return jnp.stack(
        [jnp.transpose(split[t, :, :, t, :], (0, 2, 1)).reshape(NB, H) for t in range(3)]
    )


def norm_backward(inputs, gain_row, upstream):
    average = jnp.mean(inputs, axis=-1, keepdims=True)
    centered = inputs - average
    spread = lax.rsqrt(jnp.mean(centered * centered, axis=-1, keepdims=True) + EPSILON)
    normed = centered * spread
    scaled = upstream * gain_row
    grad = spread * (
        scaled
        - jnp.mean(scaled, axis=-1, keepdims=True)
        - normed * jnp.mean(scaled * normed, axis=-1, keepdims=True)
    )
    return grad, jnp.sum(upstream * normed, axis=0), jnp.sum(upstream, axis=0)


def small_piece(vec_bias, norm_gain, bias_hidden, rel_tables):
    return jnp.concatenate(
        [vec_bias.reshape(-1), norm_gain.reshape(-1), bias_hidden, rel_tables]
    )


def spread_small(everything, vec_rows, gain_rows, vec_size, gain_size, hidden_size):
    devices = everything.shape[0]
    vectors, gains, hidden, tables = jnp.split(
        everything, [vec_size, vec_size + gain_size, vec_size + gain_size + hidden_size], axis=1
    )
    vectors = jnp.transpose(vectors.reshape(devices, vec_rows, -1), (1, 0, 2))
    gains = jnp.transpose(gains.reshape(devices, gain_rows, -1), (1, 0, 2))
    return (
        vectors.reshape(vec_rows, -1).astype(jnp.float32),
        gains.reshape(gain_rows, -1).astype(jnp.float32),
        hidden.reshape(-1).astype(jnp.float32),
        tables.reshape(3, NB, H),
    )


def body(
    own_kernels, block_input, cotangent, seg_ids, slot_valid, rel_buckets, w_qkv, w_out, w_in,
    w_down, vec_bias, norm_gain, bias_hidden, rel_tables,
):
    row_in = block_input[0]
    row_cot = cotangent[0].astype(jnp.float32)
    segments = seg_ids[0]
    validity = slot_valid[0]
    buckets = rel_buckets[0]
    length, width = row_in.shape
    padded = -(-length // LANES) * LANES
    scale = (width // H) ** (-0.5)
    devices = lax.axis_size(BOTH)
    weights = [w_qkv, w_out, w_in, w_down]

    small = small_piece(vec_bias, norm_gain, bias_hidden, rel_tables)
    small_size = small.shape[0]
    weight_plan = [
        weight_waves(0, w_qkv.shape[0], w_qkv.shape[1], w_qkv.shape[0], 8),
        weight_waves(1, w_out.shape[0], w_out.shape[1], w_out.shape[0], 8),
        weight_waves(2, w_in.shape[0], w_in.shape[1], w_in.shape[0], 8),
        weight_waves(3, w_down.shape[0], w_down.shape[1], 32, 8),
    ]
    if own_kernels:
        pad_to = SMALL_ROWS * LANES
        small_block = jnp.pad(small, (0, pad_to - small_size)).reshape(SMALL_ROWS, LANES)
        plan = [wave_of(4, 0, SMALL_ROWS, 0, 1, 0, 0)] + sum(weight_plan, [])
        gathered = gather_all(weights + [small_block], plan, 1)
        full_qkv, full_out, full_in, full_down = [
            whole.reshape(-1, whole.shape[-1]) for whole in gathered[:4]
        ]
        everything = gathered[4].reshape(devices, pad_to)[:, :small_size]
    else:
        full_qkv, full_out, full_in, full_down = [
            lax.all_gather(weight, BOTH, axis=0, tiled=True) for weight in weights
        ]
        everything = lax.all_gather(small, BOTH, axis=0, tiled=False)
    vectors, gains, hidden_bias, tables = spread_small(
        everything, vec_bias.shape[0], norm_gain.shape[0], vec_bias.size, norm_gain.size,
        bias_hidden.size,
    )

    wide = ((0, 0), (0, padded - length))
    buckets = jnp.swapaxes(buckets, 1, 2)
    packed = jnp.pad(buckets[0] | (buckets[1] << 7) | (buckets[2] << 14), wide)
    digits = jnp.concatenate([buckets // LOW_PARTS, buckets % LOW_PARTS], axis=0)
    digits = jnp.pad(
        jnp.transpose(digits.astype(jnp.bfloat16), (1, 0, 2)), ((0, 0),) + wide
    )
    position = jnp.arange(length)
    allowed = (segments[:, None] == segments[None, :]) & (
        (validity[:, None] > 0) | (position[:, None] == position[None, :])
    )
    mask = jnp.pad(jnp.where(allowed, 0.0, MASK_FILL), wide)
    steps = jnp.round(tables.astype(jnp.float32) * TABLE_STEP).astype(jnp.int32)
    pair_tables = (steps[:, :, 0::2] << 16) | (steps[:, :, 1::2] & 0xFFFF)
    pair_tables = jnp.transpose(pair_tables, (0, 2, 1))[:, :, None, :]

    mixed = dot_plain(row_in, full_qkv)
    queries = (mixed[:, :width] + vectors[0]).astype(jnp.bfloat16) * jnp.bfloat16(scale)
    keys = mixed[:, width : 2 * width].astype(jnp.bfloat16)
    values = (mixed[:, 2 * width :] + vectors[1]).astype(jnp.bfloat16)
    taller = ((0, padded - length), (0, 0))
    queries = jnp.pad(queries, taller)
    probs, context_t = attention_forward(keys, queries.T, values.T, packed, pair_tables, mask)
    context_t = context_t[:, :length]
    first_sum = row_in.astype(jnp.float32) + dot_first(context_t, full_out) + vectors[2]
    normed_first = layer_norm(first_sum, gains[0], vectors[4])
    first_low = normed_first.astype(jnp.bfloat16)
    hidden = dot_plain(first_low, full_in) + hidden_bias
    active = gelu_exact(hidden).astype(jnp.bfloat16)
    second_sum = normed_first + dot_plain(active, full_down) + vectors[3]
    output = layer_norm(second_sum, gains[1], vectors[5]).astype(jnp.bfloat16)

    grad_second, grad_gain_two, grad_shift_two = norm_backward(second_sum, gains[1], row_cot)
    down_grad = grad_second.astype(jnp.bfloat16)
    grad_w_down = dot_first(active, down_grad).astype(jnp.bfloat16)
    unused, gelu_back = jax.vjp(gelu_exact, hidden)
    hidden_grad = gelu_back(dot_last(down_grad, full_down))[0].astype(jnp.bfloat16)
    grad_w_in = dot_first(first_low, hidden_grad).astype(jnp.bfloat16)
    grad_first = dot_last(hidden_grad, full_in) + grad_second
    grad_first_sum, grad_gain_one, grad_shift_one = norm_backward(first_sum, gains[0], grad_first)
    branch_grad = grad_first_sum.astype(jnp.bfloat16)
    grad_w_out = dot_plain(context_t, branch_grad).astype(jnp.bfloat16)
    context_grad = jnp.pad(dot_last(branch_grad, full_out).astype(jnp.bfloat16), taller)
    grad_queries_t, grad_keys, grad_values, score_grad = attention_backward(
        values, context_grad.T, context_grad, queries, keys.T, probs
    )
    grad_queries = grad_queries_t[:, :length].T
    grad_mixed = jnp.concatenate([grad_queries, grad_keys, grad_values], axis=1)
    grad_w_qkv = dot_first(row_in, grad_mixed).astype(jnp.bfloat16)
    grad_input = grad_first_sum + dot_last(grad_mixed, full_qkv)
    grad_tables = table_grads(digits, score_grad)

    grad_vectors = jnp.stack(
        [
            jnp.sum(grad_queries.astype(jnp.float32), axis=0),
            jnp.sum(grad_values.astype(jnp.float32), axis=0),
            jnp.sum(branch_grad.astype(jnp.float32), axis=0),
            jnp.sum(down_grad.astype(jnp.float32), axis=0),
            grad_shift_one,
            grad_shift_two,
        ]
    )
    grad_gains = jnp.stack([grad_gain_one, grad_gain_two])
    grad_hidden_bias = jnp.sum(hidden_grad.astype(jnp.float32), axis=0)

    def by_device(matrix):
        return jnp.transpose(matrix.reshape(matrix.shape[0], devices, -1), (1, 0, 2)).reshape(
            devices, -1
        )

    small_grads = jnp.concatenate(
        [
            by_device(grad_vectors),
            by_device(grad_gains),
            grad_hidden_bias.reshape(devices, -1),
            grad_tables.reshape(devices, -1),
        ],
        axis=1,
    )
    weight_grads = [grad_w_qkv, grad_w_out, grad_w_in, grad_w_down]
    if own_kernels:
        pad_to = SMALL_GRAD_ROWS * LANES
        small_block = jnp.pad(small_grads, ((0, 0), (0, pad_to - small_size)))
        blocks = [
            grad.reshape(DIMS + (2,) + weight.shape) for grad, weight in zip(weight_grads, weights)
        ] + [small_block.reshape(DIMS + (2, SMALL_GRAD_ROWS, LANES))]
        plan = (
            weight_plan[3] + weight_plan[2] + weight_plan[1] + weight_plan[0]
            + [wave_of(4, 0, SMALL_GRAD_ROWS, 0, 1, 0, 0)]
        )
        shards = scatter_all(blocks, plan, 2)
        small_shard = shards[4].reshape(-1)[:small_size]
    else:
        shards = [
            lax.psum_scatter(
                grad.astype(jnp.float32), BOTH, scatter_dimension=0, tiled=True
            )
            for grad in weight_grads
        ]
        small_shard = lax.psum_scatter(small_grads, BOTH, scatter_dimension=0, tiled=True)[0]
    shard_vectors, shard_gains, shard_hidden, shard_tables = jnp.split(
        small_shard,
        [
            vec_bias.size,
            vec_bias.size + norm_gain.size,
            vec_bias.size + norm_gain.size + bias_hidden.size,
        ],
    )
    return (
        output[None],
        grad_input[None],
        shards[0],
        shards[1],
        shards[2],
        shards[3],
        shard_vectors.reshape(vec_bias.shape),
        shard_gains.reshape(norm_gain.shape),
        shard_hidden,
        shard_tables,
    )


def solution(mesh):
    rows = P(BOTH)
    columns = P(None, BOTH)
    in_specs = (rows,) * 9 + (columns, columns, rows, rows)
    out_specs = (rows,) * 6 + (columns, columns, rows, rows)
    chips = DIMS[0] * DIMS[1] * DIMS[2]
    own_kernels = mesh.shape["dp"] == chips and mesh.shape["fsdp"] == 2
    return jax.shard_map(
        functools.partial(body, own_kernels),
        mesh=mesh,
        in_specs=in_specs,
        out_specs=out_specs,
        check_vma=False,
    )
```

```python
import functools
import itertools
import typing

import jax
import jax.numpy as jnp
from jax import lax
from jax.experimental import pallas as pl
from jax.experimental.pallas import tpu as pltpu
from jax.sharding import PartitionSpec as P

H = 16
NB = 128
LANES = 128
EPSILON = 1e-05
MASK_FILL = -1e30
TABLE_STEP = 8192.0
VMEM_BYTES = 60 << 20
BOTH = ("dp", "fsdp")
MESH = pl.DeviceIdType.MESH
DIMS = (4, 2, 2)
GATHER_ORDERS = ((0, 2, 1), (0, 1, 2), (2, 1, 0))
STEPS = 5
LAG = 2
GRAD_TILE = 64
ROWS_AT_ONCE = 16
WINDOW_TILES = 3
HIGH_PARTS = 4
LOW_PARTS = NB // HIGH_PARTS


def dot_plain(left, right):
    return jnp.dot(left, right, preferred_element_type=jnp.float32)


def dot_first(left, right):
    return lax.dot_general(
        left, right, (((0,), (0,)), ((), ())), preferred_element_type=jnp.float32
    )


def dot_last(left, right):
    return lax.dot_general(
        left, right, (((1,), (1,)), ((), ())), preferred_element_type=jnp.float32
    )


def layer_norm(inputs, gain_row, shift_row):
    average = jnp.mean(inputs, axis=-1, keepdims=True)
    centered = inputs - average
    variance = jnp.mean(centered * centered, axis=-1, keepdims=True)
    return centered * lax.rsqrt(variance + EPSILON) * gain_row + shift_row


def gelu_exact(inputs):
    return jax.nn.gelu(inputs, approximate=False)


def coordinates():
    chip = lax.axis_index("dp")
    core = lax.axis_index("fsdp")
    planes, rows, columns = DIMS
    place = (
        chip // (rows * columns),
        lax.rem(chip // columns, rows),
        lax.rem(chip, columns),
    )
    return place, core


def device_at(place, core):
    return ((place[0] * DIMS[1] + place[1]) * DIMS[2] + place[2], core)


def shifted(place, axis, distance):
    moved = list(place)
    moved[axis] = lax.rem(moved[axis] + distance, DIMS[axis])
    return tuple(moved)


def greet(place, core):
    barrier = pltpu.get_barrier_semaphore()
    peers = [
        device_at(shifted(place, axis, distance), core)
        for axis in range(3)
        for distance in range(1, DIMS[axis])
    ]
    peers.append(device_at(place, 1 - core))
    for peer in peers:
        pl.semaphore_signal(barrier, inc=1, device_id=peer, device_id_type=MESH)
    pl.semaphore_wait(barrier, len(peers))


def schedule(waves, lag):
    events = []
    for wave in range(waves):
        for step in range(STEPS):
            events.append((wave + lag * step, wave, step))
    return [(wave, step) for slot, wave, step in sorted(events)]


def wave_of(array, row, rows, column, *tiles):
    bounds = [column]
    for count in tiles:
        bounds.append(bounds[-1] + count * LANES)
    return (array, row, rows, tuple(bounds))


def hops_before(order, phase):
    return sum(DIMS[axis] - 1 for axis in order[:phase])


def gather_steps(wave, number, full, outs, send, recv, out_sem, place, core):
    array, row, rows, bounds = wave
    whole = full[array]
    routes = [r for r in range(len(GATHER_ORDERS)) if bounds[r + 1] > bounds[r]]
    total_hops = hops_before(GATHER_ORDERS[0], 3)

    def copy(route, slot, index, target):
        part = whole.at[
            index[0], index[1], index[2], core,
            pl.ds(row, rows), pl.ds(bounds[route], bounds[route + 1] - bounds[route]),
        ]
        return pltpu.make_async_remote_copy(
            part, part, send.at[number, route, slot], recv.at[number, route, slot],
            device_id=target, device_id_type=MESH,
        )

    def to_core(route, phase, distance):
        if phase is None:
            return copy(route, total_hops, list(place), device_at(place, 1 - core))
        order = GATHER_ORDERS[route]
        axis = order[phase]
        index = list(place)
        for done in order[:phase]:
            index[done] = slice(None)
        index[axis] = lax.rem(place[axis] + DIMS[axis] - distance, DIMS[axis])
        slot = total_hops + hops_before(order, phase) + distance
        return copy(route, slot, index, device_at(place, 1 - core))

    def hop(route, phase, distance):
        order = GATHER_ORDERS[route]
        index = list(place)
        for axis in order[:phase]:
            index[axis] = slice(None)
        return copy(
            route, hops_before(order, phase) + distance - 1, index,
            device_at(shifted(place, order[phase], distance), core),
        )

    def hops(phase):
        return [
            (route, phase, distance)
            for route in routes
            for distance in range(1, DIMS[GATHER_ORDERS[route][phase]])
        ]

    def launch(phase):
        for which in hops(phase):
            hop(*which).start()

    def land(phase):
        for which in hops(phase):
            hop(*which).wait_recv()
            to_core(*which).start()

    def out_copy():
        part = (slice(None),) * 4 + (
            pl.ds(row, rows), pl.ds(bounds[0], bounds[-1] - bounds[0]),
        )
        return pltpu.make_async_copy(
            full[array].at[part], outs[array].at[part], out_sem.at[number]
        )

    def first():
        for route in routes:
            to_core(route, None, 0).start()
        launch(0)

    def second():
        land(0)
        launch(1)

    def third():
        land(1)
        launch(2)

    def fourth():
        land(2)

    def fifth():
        for route in routes:
            to_core(route, None, 0).wait_recv()
        for phase in range(3):
            for which in hops(phase):
                to_core(*which).wait_recv()
        if array < len(outs):
            out_copy().start()

    def finish():
        for route in routes:
            to_core(route, None, 0).wait_send()
        for phase in range(3):
            for which in hops(phase):
                hop(*which).wait_send()
                to_core(*which).wait_send()
        if array < len(outs):
            out_copy().wait()

    return [first, second, third, fourth, fifth, finish]


def erf(values):
    clipped = jnp.clip(values, -3.832506856900711, 3.832506856900711)
    square = clipped * clipped
    top = jnp.full_like(square, 0.00022905065861350646)
    for term in (
        0.0034082910107109506, 0.050955695062380861, 0.18520832239976145, 1.128379143519084,
    ):
        top = top * square + term
    bottom = jnp.full_like(square, -1.1791602954361697e-7)
    for term in (
        0.000023547966471313185, 0.0010179625278914885, 0.014070470171167667,
        0.11098505178285362, 0.49746925110067538, 1.0,
    ):
        bottom = bottom * square + term
    return clipped * top / bottom


def gelu_and_slope(hidden):
    chance = 0.5 + 0.5 * erf(hidden * (0.5**0.5))
    density = jnp.exp(-0.5 * hidden * hidden) * 0.3989422804014327
    return hidden * chance, chance + hidden * density


def norm_rows(inputs, gain_row, shift_row):
    average = jnp.mean(inputs, axis=-1, keepdims=True)
    centered = inputs - average
    variance = jnp.mean(centered * centered, axis=-1, keepdims=True)
    return centered * lax.rsqrt(variance + EPSILON) * gain_row + shift_row


def attention_pair(pair_number, refs):
    (
        row_ref, qkv_ref, vector_ref, table_ref, packed_ref, mask_ref, score_ref, probs_ref,
        query_ref, key_t_ref, value_ref, context_ref, context_t_ref,
    ) = refs
    length, width = row_ref.shape
    padded = packed_ref.shape[1]
    pair = 2 * width // H
    half = pair // 2
    scale = half ** (-0.5)
    at = pl.multiple_of(pair_number * pair, pair)
    mine = pl.ds(at, pair)
    row_in = row_ref[...]

    def project(part):
        columns = pl.ds(pl.multiple_of(part * width + at, pair), pair)
        return dot_plain(row_in, qkv_ref[:, columns])

    queries = ((project(0) + vector_ref[0:1, mine]).astype(jnp.bfloat16)) * jnp.bfloat16(scale)
    keys = project(1).astype(jnp.bfloat16)
    values = (project(2) + vector_ref[1:2, mine]).astype(jnp.bfloat16)
    query_ref[0:length, mine] = queries
    query_ref[length:, mine] = jnp.zeros((padded - length, pair), jnp.bfloat16)
    value_ref[:, mine] = values
    queries_t = jnp.concatenate(
        [queries.T, jnp.zeros((pair, padded - length), jnp.bfloat16)], axis=1
    )
    key_t_ref[mine, :] = keys.T
    values_t = values.T
    feature = lax.broadcasted_iota(jnp.int32, (pair, padded), 0)
    zero = jnp.zeros_like(queries_t)
    score_ref[0] = dot_plain(keys, jnp.where(feature < half, queries_t, zero))
    score_ref[1] = dot_plain(keys, jnp.where(feature < half, zero, queries_t))
    for column in range(0, padded, LANES):
        lanes = slice(column, column + LANES)
        rows = [table_ref[t, pair_number] for t in range(3)]
        tops = [jnp.full((8, LANES), 3.0 * MASK_FILL, jnp.float32) for side in range(2)]
        for start in range(0, length, 8):
            here = slice(start, start + 8)
            packed = packed_ref[here, lanes]
            sums = [None, None]
            for table in range(3):
                index = (packed >> (7 * table)) & (NB - 1)
                word = jnp.take_along_axis(rows[table], index, axis=1)
                for side, term in ((0, word >> 16), (1, (word << 16) >> 16)):
                    sums[side] = term if table == 0 else sums[side] + term
            mask = mask_ref[here, lanes]
            for side in range(2):
                scores = score_ref[side, here, lanes] + (
                    sums[side].astype(jnp.float32) * (1.0 / TABLE_STEP) + mask
                )
                score_ref[side, here, lanes] = scores
                tops[side] = jnp.maximum(tops[side], scores)
        for side in range(2):
            top = jnp.max(tops[side], axis=0, keepdims=True)
            exponent = jnp.exp(score_ref[side, :, lanes] - top)
            total = jnp.sum(exponent, axis=0, keepdims=True)
            probs_ref[side, :, lanes] = (exponent * (1.0 / total)).astype(jnp.bfloat16)
    context_t = jnp.concatenate(
        [
            dot_plain(values_t[side * half : (side + 1) * half], probs_ref[side])
            for side in range(2)
        ],
        axis=0,
    ).astype(jnp.bfloat16)
    context_t_ref[mine, :] = context_t
    context_ref[:, mine] = context_t.T[0:length]


class ForwardRefs(typing.NamedTuple):
    w_qkv: typing.Any
    w_out: typing.Any
    w_in: typing.Any
    w_down: typing.Any
    small: typing.Any
    row: typing.Any
    buckets: typing.Any
    segments_down: typing.Any
    valid_down: typing.Any
    segments_across: typing.Any
    full_qkv: typing.Any
    full_out: typing.Any
    full_in: typing.Any
    full_down: typing.Any
    probs: typing.Any
    context_t: typing.Any
    queries: typing.Any
    keys_t: typing.Any
    values: typing.Any
    first_sum: typing.Any
    first_low: typing.Any
    active_t: typing.Any
    slope: typing.Any
    second_sum: typing.Any
    vectors: typing.Any
    packed_t: typing.Any
    h_qkv: typing.Any
    h_out: typing.Any
    h_in: typing.Any
    h_down: typing.Any
    h_small: typing.Any
    s_row: typing.Any
    s_buckets: typing.Any
    s_packed: typing.Any
    s_mask: typing.Any
    s_score: typing.Any
    s_probs: typing.Any
    s_context: typing.Any
    s_context_t: typing.Any
    s_query: typing.Any
    s_key_t: typing.Any
    s_value: typing.Any
    s_first: typing.Any
    s_low: typing.Any
    s_active: typing.Any
    s_slope: typing.Any
    s_active_t: typing.Any
    s_second: typing.Any
    s_vectors: typing.Any
    s_hidden: typing.Any
    s_tables: typing.Any
    local_sem: typing.Any
    send: typing.Any
    recv: typing.Any
    out_sem: typing.Any
    probs_sem: typing.Any
    slope_sem: typing.Any
    active_sem: typing.Any
    store_sem: typing.Any


def forward_kernel(waves, starts, *refs):
    r = ForwardRefs(*refs)
    place, core = coordinates()
    shards = [r.w_qkv, r.w_out, r.w_in, r.w_down, r.small]
    full = [r.h_qkv, r.h_out, r.h_in, r.h_down, r.h_small]
    outs = [r.full_qkv, r.full_out, r.full_in, r.full_down]
    length, width = r.s_row.shape
    padded = r.s_packed.shape[1]
    own = [
        pltpu.make_async_copy(
            shards[i], full[i].at[place[0], place[1], place[2], core], r.local_sem.at[i]
        )
        for i in range(len(shards))
    ]
    own.append(pltpu.make_async_copy(r.row, r.s_row, r.local_sem.at[5]))
    own.append(pltpu.make_async_copy(r.buckets, r.s_buckets, r.local_sem.at[6]))
    for copy in own:
        copy.start()
    greet(place, core)
    steps = [
        gather_steps(wave, number, full, outs, r.send, r.recv, r.out_sem, place, core)
        for number, wave in enumerate(waves)
    ]
    for copy in own[:5]:
        copy.wait()
    events = []
    for number, (start, lag) in enumerate(starts):
        for step in range(STEPS):
            events.append((start + lag * step, number, step))
    events.sort()
    ready = max(e[0] for e in events if waves[e[1]][0] in (0, 4))
    first_in = max(e[0] for e in events if waves[e[1]][0] in (0, 4, 1))

    def communicate(low, high):
        for slot, number, step in events:
            if low <= slot < high:
                steps[number][step]()

    def prepare():
        own[6].wait()
        for table in range(3):
            part = r.s_buckets[table] << (7 * table)
            packed = part if table == 0 else packed | part
        flipped = packed.T
        r.s_packed[...] = jnp.concatenate(
            [flipped, jnp.zeros((length, padded - length), jnp.int32)], axis=1
        )
        down = lax.broadcasted_iota(jnp.int32, (length, padded), 0)
        across = lax.broadcasted_iota(jnp.int32, (length, padded), 1)
        same = r.segments_down[...] == r.segments_across[...]
        usable = (r.valid_down[...] > 0) | (down == across)
        allowed = (same & usable) | (across >= length)
        r.s_mask[...] = jnp.where(allowed, 0.0, MASK_FILL)

    def spread():
        devices = DIMS[0] * DIMS[1] * DIMS[2] * 2
        piece = width // devices
        group = LANES // piece
        buckets_each = 3 * NB // devices
        tables = [jnp.zeros((H, LANES), jnp.float32) for t in range(3)]
        lane = lax.broadcasted_iota(jnp.int32, (H, LANES), 1)
        for device in range(devices):
            spot = (device // 8, (device // 4) % 2, (device // 2) % 2, device % 2)
            block = r.h_small[spot].astype(jnp.float32)
            mine = slice(device // group * LANES, (device // group + 1) * LANES)
            if device % group == 0:
                r.s_vectors[:, mine] = block[0:8]
            else:
                r.s_vectors[:, mine] = r.s_vectors[:, mine] + block[0:8]
            r.s_hidden[:, device * LANES : (device + 1) * LANES] = block[8:9]
            low, high = device * buckets_each, (device + 1) * buckets_each
            for table in range(low // NB, (high - 1) // NB + 1):
                inside = (lane >= low - table * NB) & (lane < high - table * NB)
                tables[table] = tables[table] + jnp.where(inside, block[16:32], 0.0)
        for table in range(3):
            fixed = jnp.round(tables[table] * TABLE_STEP).astype(jnp.int32)
            words = (fixed[0:8] << 16) | (fixed[8:16] & 0xFFFF)
            for pair in range(H // 2):
                r.s_tables[table, pair] = jnp.broadcast_to(words[pair : pair + 1], (8, LANES))

    communicate(0, 1)
    prepare()
    communicate(1, ready + 1)
    spread()
    own[5].wait()
    vectors = pltpu.make_async_copy(r.s_vectors, r.vectors, r.store_sem.at[0])
    vectors.start()
    qkv_view = r.h_qkv.reshape(width, 3 * width)

    def probs_copy(pair_number, slot):
        return pltpu.make_async_copy(
            r.s_probs.at[slot], r.probs.at[pl.ds(2 * pair_number, 2)],
            r.probs_sem.at[slot],
        )

    def one_pair(pair_number, carry):
        for number in range(H // 2):
            slot = ready + 1 + number
            if any(e[0] == slot for e in events):
                @pl.when(pair_number == number)
                def talk(slot=slot):
                    communicate(slot, slot + 1)

        slot = lax.rem(pair_number, 2)

        @pl.when(pair_number >= 2)
        def free():
            probs_copy(pair_number - 2, slot).wait()

        attention_pair(
            pair_number,
            (
                r.s_row, qkv_view, r.s_vectors, r.s_tables, r.s_packed,
                r.s_mask, r.s_score, r.s_probs.at[slot], r.s_query, r.s_key_t,
                r.s_value, r.s_context, r.s_context_t,
            ),
        )
        probs_copy(pair_number, slot).start()
        return carry

    pairs = H // 2
    lax.fori_loop(0, pairs, one_pair, 0)
    now = ready + 1 + pairs
    stores = [vectors]

    def store(scratch, out, number):
        made = pltpu.make_async_copy(scratch, out, r.store_sem.at[number])
        made.start()
        stores.append(made)

    store(r.s_context_t, r.context_t, 1)
    store(r.s_query, r.queries, 2)
    for part in range(padded // LANES):
        store(r.s_packed.at[:, part * LANES : (part + 1) * LANES], r.packed_t.at[part], 9 + part)
    store(r.s_key_t, r.keys_t, 3)
    store(r.s_value, r.values, 4)
    if first_in >= now:
        communicate(now, first_in + 1)
        now = first_in + 1
    out_view = r.h_out.reshape(width, width)
    tile = length // 3

    def one_out(number, carry):
        rows = pl.ds(pl.multiple_of(number * tile, tile), tile)
        first = (
            r.s_row[rows, :].astype(jnp.float32)
            + dot_plain(r.s_context[rows, :], out_view[...])
            + r.s_vectors[2:3, :]
        )
        r.s_first[rows, :] = first
        normed = norm_rows(first, r.s_vectors[6:7, :], r.s_vectors[4:5, :])
        r.s_low[rows, :] = normed.astype(jnp.bfloat16)
        r.s_second[rows, :] = normed + r.s_vectors[3:4, :]
        return carry

    lax.fori_loop(0, 3, one_out, 0)
    store(r.s_first, r.first_sum, 5)
    store(r.s_low, r.first_low, 6)
    hidden_units = r.s_active.shape[1]
    in_view = r.h_in.reshape(width, hidden_units)
    chunk = r.s_slope.shape[2]

    def slope_copy(number, slot):
        return pltpu.make_async_copy(
            r.s_slope.at[slot],
            r.slope.at[:, pl.ds(pl.multiple_of(number * chunk, chunk), chunk)],
            r.slope_sem.at[slot],
        )

    def active_copy(number, slot):
        return pltpu.make_async_copy(
            r.s_active_t.at[slot],
            r.active_t.at[pl.ds(pl.multiple_of(number * chunk, chunk), chunk)],
            r.active_sem.at[slot],
        )

    def one_in(number, carry):
        columns = pl.ds(pl.multiple_of(number * chunk, chunk), chunk)
        slot = lax.rem(number, 2)

        @pl.when(number >= 2)
        def free():
            slope_copy(number - 2, slot).wait()
            active_copy(number - 2, slot).wait()

        hidden = dot_plain(r.s_low[...], in_view[:, columns]) + r.s_hidden[:, columns]
        active, slope = gelu_and_slope(hidden)
        active_low = active.astype(jnp.bfloat16)
        r.s_active[:, columns] = active_low
        r.s_active_t[slot] = active_low.T
        active_copy(number, slot).start()
        r.s_slope[slot] = slope.astype(jnp.bfloat16)
        slope_copy(number, slot).start()
        return carry

    in_waves = [(w[3][-1], number) for number, w in enumerate(waves) if w[0] == 2]
    done = 0
    for edge, number in in_waves:
        arrived = starts[number][0] + starts[number][1] * (STEPS - 1)
        if arrived >= now:
            communicate(now, arrived + 1)
            now = arrived + 1
        lax.fori_loop(done, edge // chunk, one_in, 0)
        done = edge // chunk
    last = events[-1][0]
    down_view = r.h_down.reshape(hidden_units, width)
    for number, wave in enumerate(waves):
        if wave[0] == 3:
            arrived = starts[number][0] + starts[number][1] * (STEPS - 1)
            if arrived >= now:
                communicate(now, arrived + 1)
                now = arrived + 1
            columns = slice(wave[3][0], wave[3][-1])
            r.s_second[:, columns] = r.s_second[:, columns] + dot_plain(
                r.s_active[...], down_view[:, columns]
            )
    store(r.s_second, r.second_sum, 8)
    for pair_number in (pairs - 2, pairs - 1):
        probs_copy(pair_number, pair_number % 2).wait()
    chunks = hidden_units // chunk
    for number in (chunks - 2, chunks - 1):
        slope_copy(number, number % 2).wait()
        active_copy(number, number % 2).wait()
    for wave_steps in steps:
        wave_steps[STEPS]()
    for made in stores:
        made.wait()


def forward_all(shards, small, row_in, buckets, segments, validity, waves, starts, collective):
    length, width = row_in.shape
    padded = -(-length // LANES) * LANES
    hidden_units = shards[2].shape[1]
    chunk = 256
    routes = len(GATHER_ORDERS)
    hops = 2 * hops_before(GATHER_ORDERS[0], 3) + 1
    low = jnp.bfloat16
    shape = jax.ShapeDtypeStruct
    anywhere = pl.BlockSpec(memory_space=pl.ANY)
    in_vmem = pl.BlockSpec(memory_space=pltpu.VMEM)
    whole = [shape(DIMS + (2,) + shard.shape, shard.dtype) for shard in shards + [small]]
    outs = whole[:4] + [
        shape((H, length, padded), low),
        shape((width, padded), low),
        shape((padded, width), low),
        shape((width, length), low),
        shape((length, width), low),
        shape((length, width), jnp.float32),
        shape((length, width), low),
        shape((hidden_units, length), low),
        shape((length, hidden_units), low),
        shape((length, width), jnp.float32),
        shape((8, width), jnp.float32),
        shape((padded // LANES, length, LANES), jnp.int32),
    ]
    scratch = [pltpu.VMEM(one.shape, one.dtype) for one in whole] + [
        pltpu.VMEM((length, width), low),
        pltpu.VMEM((3, length, length), jnp.int32),
        pltpu.VMEM((length, padded), jnp.int32),
        pltpu.VMEM((length, padded), jnp.float32),
        pltpu.VMEM((2, length, padded), jnp.float32),
        pltpu.VMEM((2, 2, length, padded), low),
        pltpu.VMEM((length, width), low),
        pltpu.VMEM((width, padded), low),
        pltpu.VMEM((padded, width), low),
        pltpu.VMEM((width, length), low),
        pltpu.VMEM((length, width), low),
        pltpu.VMEM((length, width), jnp.float32),
        pltpu.VMEM((length, width), low),
        pltpu.VMEM((length, hidden_units), low),
        pltpu.VMEM((2, length, chunk), low),
        pltpu.VMEM((2, chunk, length), low),
        pltpu.VMEM((length, width), jnp.float32),
        pltpu.VMEM((8, width), jnp.float32),
        pltpu.VMEM((1, hidden_units), jnp.float32),
        pltpu.VMEM((3, H // 2, 8, LANES), jnp.int32),
        pltpu.SemaphoreType.DMA((7,)),
        pltpu.SemaphoreType.DMA((len(waves), routes, hops)),
        pltpu.SemaphoreType.DMA((len(waves), routes, hops)),
        pltpu.SemaphoreType.DMA((len(waves),)),
        pltpu.SemaphoreType.DMA((2,)),
        pltpu.SemaphoreType.DMA((2,)),
        pltpu.SemaphoreType.DMA((2,)),
        pltpu.SemaphoreType.DMA((9 + padded // LANES,)),
    ]
    across = jnp.pad(segments, (0, padded - length))[None, :]
    return pl.pallas_call(
        functools.partial(forward_kernel, waves, starts),
        in_specs=[anywhere] * 7 + [in_vmem] * 3,
        out_specs=[anywhere] * len(outs),
        out_shape=outs,
        scratch_shapes=scratch,
        compiler_params=pltpu.CompilerParams(
            collective_id=collective, has_side_effects=True, vmem_limit_bytes=VMEM_BYTES
        ),
    )(*shards, small, row_in, buckets, segments[:, None], validity[:, None], across)


def small_block(device, vec_bias, norm_gain, bias_hidden, rel_tables):
    piece = vec_bias.shape[1]
    group = LANES // piece
    lane = jnp.arange(LANES)
    tiled = jnp.tile(jnp.concatenate([vec_bias, norm_gain], axis=0), (1, group))
    placed = jnp.where(lane // piece == device % group, tiled, jnp.zeros_like(tiled))
    hidden = jnp.pad(bias_hidden[None, :], ((0, 7), (0, 0)))
    heads_first = rel_tables.reshape(-1, H).T
    buckets_each = heads_first.shape[1]
    wanted = (lane - device * buckets_each) % NB
    choose = (wanted[None, :] == jnp.arange(buckets_each)[:, None]).astype(jnp.bfloat16)
    tables = dot_plain(jnp.concatenate([heads_first[0::2], heads_first[1::2]], axis=0), choose)
    return jnp.concatenate([placed, hidden, tables.astype(jnp.bfloat16)], axis=0)


def reduce_orders():
    return [tuple(reversed(order)) for order in GATHER_ORDERS]


def axes_left(order, phase):
    return [axis for axis in range(3) if axis not in order[: phase + 1]]


def scatter_scratch(waves, dtypes):
    shapes = []
    for array, row, rows, bounds in waves:
        dtype = dtypes[array]
        block = DIMS + (rows, bounds[-1] - bounds[0])
        shapes += [pltpu.VMEM(block, dtype), pltpu.VMEM(block, dtype)]
        for route, order in enumerate(reduce_orders()):
            width = bounds[route + 1] - bounds[route]
            for phase in range(3 if width else 0):
                left = tuple(DIMS[axis] for axis in axes_left(order, phase))
                shapes.append(
                    pltpu.VMEM((DIMS[order[phase]] - 1,) + left + (rows, width), dtype)
                )
    return shapes


def scatter_steps(wave, number, source, out, scratch, own_sem, send, recv, place, core):
    array, row, rows, bounds = wave
    base = bounds[0]
    total = next(scratch)
    other = next(scratch)
    orders = reduce_orders()
    routes = [r for r in range(len(orders)) if bounds[r + 1] > bounds[r]]
    landing = {}
    for route in routes:
        for phase in range(3):
            landing[route, phase] = next(scratch)
    core_slot = hops_before(orders[0], 3)
    every = slice(None)

    def own_copy():
        return pltpu.make_async_copy(source.at[:, :, :, core], total, own_sem.at[number])

    def core_copy():
        return pltpu.make_async_remote_copy(
            source.at[:, :, :, 1 - core], other,
            send.at[number, 0, core_slot], recv.at[number, 0, core_slot],
            device_id=device_at(place, 1 - core), device_id_type=MESH,
        )

    def hop(route, phase, distance):
        order = orders[route]
        axis = order[phase]
        index = [every] * 3
        for done in order[:phase]:
            index[done] = place[done]
        index[axis] = lax.rem(place[axis] + distance, DIMS[axis])
        slot = hops_before(order, phase) + distance - 1
        return pltpu.make_async_remote_copy(
            total.at[
                index[0], index[1], index[2], :,
                pl.ds(bounds[route] - base, bounds[route + 1] - bounds[route]),
            ],
            landing[route, phase].at[distance - 1],
            send.at[number, route, slot], recv.at[number, route, slot],
            device_id=device_at(shifted(place, axis, distance), core), device_id_type=MESH,
        )

    def launch(phase):
        for route in routes:
            for distance in range(1, DIMS[orders[route][phase]]):
                hop(route, phase, distance).start()

    def land(phase):
        for route in routes:
            order = orders[route]
            axis = order[phase]
            for distance in range(1, DIMS[axis]):
                hop(route, phase, distance).wait_recv()
            left = axes_left(order, phase)
            columns = slice(bounds[route] - base, bounds[route + 1] - base)
            for spot in itertools.product(*[range(DIMS[a]) for a in left]):
                index = list(place)
                for a, value in zip(left, spot):
                    index[a] = value
                at = (index[0], index[1], index[2], every, columns)
                added = total[at].astype(jnp.float32)
                for distance in range(1, DIMS[axis]):
                    added += landing[route, phase][(distance - 1,) + spot].astype(jnp.float32)
                if phase == 2:
                    out[pl.ds(row, rows), bounds[route] : bounds[route + 1]] = added
                else:
                    total[at] = added.astype(total.dtype)

    def first():
        own_copy().start()
        core_copy().start()

    def second():
        own_copy().wait()
        core_copy().wait()

        def one_plane(plane, carry):
            for y, x in itertools.product(range(DIMS[1]), range(DIMS[2])):
                total[plane, y, x] = total[plane, y, x] + other[plane, y, x]
            return carry

        lax.fori_loop(0, DIMS[0], one_plane, 0)
        launch(0)

    def third():
        land(0)
        launch(1)

    def fourth():
        land(1)
        launch(2)

    def fifth():
        land(2)
        for route in routes:
            for phase in range(3):
                for distance in range(1, DIMS[orders[route][phase]]):
                    hop(route, phase, distance).wait_send()

    return [first, second, third, fourth, fifth]


SCATTER_AFTER = (0, 1, 3, 5, 7)


def step_runner(steps, starts):
    events = sorted(
        (start + SCATTER_AFTER[step], number, step)
        for number, start in enumerate(starts)
        for step in range(STEPS)
    )

    def communicate(slot):
        for when, number, step in events:
            if when == slot:
                steps[number][step]()

    return communicate, events[-1][0]


def store_blocks(target, product, rows):
    planes = product.shape[0] // rows
    for block in range(planes):
        spot = (block // 8, (block // 4) % 2, (block // 2) % 2, block % 2)
        target[spot] = product[block * rows : (block + 1) * rows].astype(target.dtype)


def fold_rows(values):
    total = values[0:8]
    for start in range(8, values.shape[0], 8):
        total = total + values[start : start + 8]
    return total


def norm_rows_backward(inputs, gain_row, upstream):
    average = jnp.mean(inputs, axis=-1, keepdims=True)
    centered = inputs - average
    spread = lax.rsqrt(jnp.mean(centered * centered, axis=-1, keepdims=True) + EPSILON)
    normed = centered * spread
    scaled = upstream * gain_row
    grad = spread * (
        scaled
        - jnp.mean(scaled, axis=-1, keepdims=True)
        - normed * jnp.mean(scaled * normed, axis=-1, keepdims=True)
    )
    return grad, normed


def attention_pair_backward(refs):
    (
        value_ref, context_grad_t_ref, context_grad_ref, query_ref, key_t_ref, probs_ref,
        grads_ref, score_grad_ref, prob_grad_ref, low_ref,
    ) = refs
    length, pair = value_ref.shape
    padded = context_grad_t_ref.shape[1]
    half = pair // 2
    scale = half ** (-0.5)
    feature = lax.broadcasted_iota(jnp.int32, (pair, padded), 0)
    upstream = context_grad_t_ref[...]
    zero = jnp.zeros_like(upstream)
    prob_grad_ref[0] = dot_plain(value_ref[...], jnp.where(feature < half, upstream, zero))
    prob_grad_ref[1] = dot_plain(value_ref[...], jnp.where(feature < half, zero, upstream))
    for part in range(padded // LANES):
        lanes = slice(part * LANES, (part + 1) * LANES)
        for side in range(2):
            probs = probs_ref[side, :, lanes].astype(jnp.float32)
            prob_grad = prob_grad_ref[side, :, lanes]
            inner = jnp.sum(probs * prob_grad, axis=0, keepdims=True)
            score_grad = probs * (prob_grad - inner)
            score_grad_ref[part, side] = score_grad
            low_ref[side, :, lanes] = score_grad.astype(jnp.bfloat16)
    grad_query_t = jnp.concatenate(
        [
            dot_plain(key_t_ref[side * half : (side + 1) * half, :], low_ref[side])
            for side in range(2)
        ],
        axis=0,
    )
    grads_ref[0] = (grad_query_t * scale).astype(jnp.bfloat16).T[0:length]
    first_half = lax.broadcasted_iota(jnp.int32, (length, pair), 1) < half
    grad_key = [dot_plain(low_ref[side], query_ref[...]) for side in range(2)]
    grads_ref[1] = jnp.where(first_half, grad_key[0], grad_key[1]).astype(jnp.bfloat16)
    grad_value = [dot_plain(probs_ref[side], context_grad_ref[...]) for side in range(2)]
    grads_ref[2] = jnp.where(first_half, grad_value[0], grad_value[1]).astype(jnp.bfloat16)


class FeedInputs(typing.NamedTuple):
    full_in: typing.Any
    full_down: typing.Any
    full_out: typing.Any
    second_sum: typing.Any
    cotangent: typing.Any
    first_sum: typing.Any
    first_low: typing.Any
    active_t: typing.Any
    slope: typing.Any
    probs: typing.Any
    queries: typing.Any
    keys_t: typing.Any
    values: typing.Any
    vectors: typing.Any


class FeedOutputs(typing.NamedTuple):
    shard_in: typing.Any
    shard_down: typing.Any
    output: typing.Any
    grad_first_sum: typing.Any
    branch_grad: typing.Any
    grad_mixed: typing.Any
    score_grad: typing.Any
    sums: typing.Any
    hidden_sums: typing.Any


class FeedRefs(typing.NamedTuple):
    full_in: typing.Any
    full_down: typing.Any
    full_out: typing.Any
    second_sum: typing.Any
    cotangent: typing.Any
    first_sum: typing.Any
    first_low: typing.Any
    active_t: typing.Any
    slope: typing.Any
    probs: typing.Any
    queries: typing.Any
    keys_t: typing.Any
    values: typing.Any
    vectors: typing.Any
    shard_in: typing.Any
    shard_down: typing.Any
    output: typing.Any
    grad_first_sum: typing.Any
    branch_grad: typing.Any
    grad_mixed: typing.Any
    score_grad: typing.Any
    sums: typing.Any
    hidden_sums: typing.Any
    own_sem: typing.Any
    send: typing.Any
    recv: typing.Any
    load_sem: typing.Any
    store_sem: typing.Any
    chunk_sem: typing.Any
    probs_sem: typing.Any
    grads_sem: typing.Any
    score_sem: typing.Any
    s_stage: typing.Any
    s_in: typing.Any
    s_down: typing.Any
    s_grad: typing.Any
    s_low: typing.Any
    s_vectors: typing.Any
    s_sums: typing.Any
    s_hidden: typing.Any
    s_branch: typing.Any


def feed_backward_kernel(waves, *refs):
    r = FeedRefs(*refs[: len(FeedRefs._fields)])
    buffers = refs[len(FeedRefs._fields) :]
    place, core = coordinates()
    length, width = r.s_low.shape
    hidden_units = r.s_hidden.shape[1]
    padded = r.probs.shape[2]
    chunk = 512
    down_waves = sum(wave[0] == 1 for wave in waves)
    loads = {}

    def load(source, target, number):
        made = pltpu.make_async_copy(source, target, r.load_sem.at[number])
        made.start()
        loads[number] = made

    load(r.vectors, r.s_vectors, 0)
    greet(place, core)
    counts = [len(scatter_scratch([wave], [jnp.bfloat16] * 2)) for wave in waves]
    offsets = [sum(counts[:number]) for number in range(len(waves))]

    def steps_of(number, stage):
        mine = iter(buffers[offsets[number] : offsets[number] + counts[number]])
        return scatter_steps(
            waves[number], number, stage,
            r.s_down if waves[number][0] == 1 else r.s_in, mine,
            r.own_sem, r.send, r.recv, place, core,
        )

    steps = [None] * len(waves)
    for number in range(down_waves, len(waves)):
        steps[number] = steps_of(number, r.s_stage.at[number % 2])
    communicate, last = step_runner(steps, list(range(len(waves))))
    stores = []

    def store(scratch, out, number):
        made = pltpu.make_async_copy(scratch, out, r.store_sem.at[number])
        made.start()
        stores.append(made)
        return made

    loads[0].wait()
    gains = [r.s_vectors[6:7, :], r.s_vectors[7:8, :]]
    tile = 32
    nothing = jnp.zeros((8, width), jnp.float32)

    def feed_phase(
        s_second, s_cot, s_out, s_active, s_low_rows, s_low_t, s_wd, s_wi, s_slope, s_stage_down
    ):
        for number in range(down_waves):
            steps[number] = steps_of(number, s_stage_down.at[number % 2])
        load(r.second_sum, s_second, 2)
        load(r.cotangent, s_cot, 3)
        load(r.active_t, s_active, 4)
        load(r.first_low, s_low_rows, 5)

        def chunk_copies(number, slot):
            columns = pl.ds(pl.multiple_of(number * chunk, chunk), chunk)
            return [
                pltpu.make_async_copy(
                    r.full_down.at[columns], s_wd.at[slot], r.chunk_sem.at[slot, 0]
                ),
                pltpu.make_async_copy(
                    r.full_in.at[:, columns], s_wi.at[slot], r.chunk_sem.at[slot, 1]
                ),
                pltpu.make_async_copy(
                    r.slope.at[:, columns], s_slope.at[slot], r.chunk_sem.at[slot, 2]
                ),
            ]

        for copy in chunk_copies(0, 0):
            copy.start()
        loads[2].wait()
        loads[3].wait()

        def one_norm(number, carry):
            rows = pl.ds(pl.multiple_of(number * tile, tile), tile)
            upstream = s_cot[rows, :].astype(jnp.float32)
            grad, normed = norm_rows_backward(s_second[rows, :], gains[1], upstream)
            s_out[rows, :] = (normed * gains[1] + r.s_vectors[5:6, :]).astype(jnp.bfloat16)
            r.s_grad[rows, :] = grad
            low = grad.astype(jnp.bfloat16)
            r.s_low[rows, :] = low
            return (
                carry[0] + fold_rows(low.astype(jnp.float32)),
                carry[1] + fold_rows(upstream),
                carry[2] + fold_rows(upstream * normed),
            )

        sums = lax.fori_loop(0, length // tile, one_norm, (nothing, nothing, nothing))
        for row, total in zip((3, 5, 7), sums):
            r.s_sums[row : row + 1, :] = jnp.sum(total, axis=0, keepdims=True)
        store(s_out, r.output, 0)
        loads[4].wait()
        rows_each = waves[0][2]
        spots = list(itertools.product(range(DIMS[1]), range(DIMS[2]), range(2)))

        def to_stage(stage, plane, product, rows, columns):
            for block, spot in enumerate(spots):
                stage[(plane,) + spot + (slice(None), columns)] = product[
                    block * rows : (block + 1) * rows
                ].astype(jnp.bfloat16)

        for number in range(down_waves):
            columns = slice(waves[number][3][0], waves[number][3][-1])

            def one_down(plane, carry, number=number, columns=columns):
                size = len(spots) * rows_each
                units = pl.ds(pl.multiple_of(plane * size, size), size)
                product = dot_plain(s_active[units, :], r.s_low[:, columns])
                to_stage(
                    s_stage_down.at[number % 2], plane, product, rows_each, slice(None)
                )
                return carry

            lax.fori_loop(0, DIMS[0], one_down, 0)
            communicate(number)
        loads[5].wait()
        s_low_t[...] = s_low_rows[...].T
        in_rows = waves[down_waves][2]
        per_wave = (waves[down_waves][3][-1] - waves[down_waves][3][0]) // chunk
        for number in range(down_waves, len(waves)):

            def one_piece(piece, carry, number=number):
                index = (number - down_waves) * per_wave + piece
                slot = lax.rem(index, 2)

                @pl.when(index + 1 < hidden_units // chunk)
                def fetch():
                    for copy in chunk_copies(index + 1, 1 - slot):
                        copy.start()

                for copy in chunk_copies(index, slot):
                    copy.wait()
                hidden_grad = dot_last(r.s_low[...], s_wd[slot]) * s_slope[slot].astype(
                    jnp.float32
                )
                low = hidden_grad.astype(jnp.bfloat16)
                here = pl.ds(pl.multiple_of(index * chunk, chunk), chunk)
                r.s_hidden[:, here] = jnp.sum(
                    low.astype(jnp.float32), axis=0, keepdims=True
                )
                there = pl.ds(pl.multiple_of(piece * chunk, chunk), chunk)
                size = len(spots) * in_rows
                for plane in range(DIMS[0]):
                    product = dot_plain(s_low_t[plane * size : (plane + 1) * size, :], low)
                    to_stage(r.s_stage.at[number % 2], plane, product, in_rows, there)
                r.s_grad[...] = r.s_grad[...] + dot_last(low, s_wi[slot])
                return carry

            lax.fori_loop(0, per_wave, one_piece, 0)
            communicate(number)
        stores[0].wait()

    bf, full32 = jnp.bfloat16, jnp.float32
    pl.run_scoped(
        feed_phase,
        pltpu.VMEM((length, width), full32),
        pltpu.VMEM((length, width), bf),
        pltpu.VMEM((length, width), bf),
        pltpu.VMEM((hidden_units, length), bf),
        pltpu.VMEM((length, width), bf),
        pltpu.VMEM((width, length), bf),
        pltpu.VMEM((2, chunk, width), bf),
        pltpu.VMEM((2, width, chunk), bf),
        pltpu.VMEM((2, length, chunk), bf),
        pltpu.VMEM((2,) + DIMS + (2, waves[0][2], waves[0][3][-1] - waves[0][3][0]), bf),
    )
    now = len(waves)
    pairs = H // 2
    pair = width // pairs

    def norm_phase(s_first):
        load(r.first_sum, s_first, 1)
        loads[1].wait()

        def one_norm(number, carry):
            rows = pl.ds(pl.multiple_of(number * tile, tile), tile)
            upstream = r.s_grad[rows, :]
            grad, normed = norm_rows_backward(s_first[rows, :], gains[0], upstream)
            r.s_grad[rows, :] = grad
            low = grad.astype(jnp.bfloat16)
            r.s_branch[rows, :] = low
            return (
                carry[0] + fold_rows(low.astype(jnp.float32)),
                carry[1] + fold_rows(upstream),
                carry[2] + fold_rows(upstream * normed),
            )

        sums = lax.fori_loop(0, length // tile, one_norm, (nothing, nothing, nothing))
        for row, total in zip((2, 4, 6), sums):
            r.s_sums[row : row + 1, :] = jnp.sum(total, axis=0, keepdims=True)

    pl.run_scoped(norm_phase, pltpu.VMEM((length, width), full32))
    store(r.s_grad, r.grad_first_sum, 1)
    store(r.s_branch, r.branch_grad, 2)
    communicate(now)

    def attention_phase(
        s_wout, s_context_grad, s_context_grad_t, s_query, s_key_t, s_value, s_probs, s_prob_grad,
        s_low, s_score, s_grads,
    ):
        load(r.full_out, s_wout, 6)
        load(r.queries, s_query, 7)
        load(r.keys_t, s_key_t, 8)
        load(r.values, s_value, 9)

        def probs_copy(number, slot):
            return pltpu.make_async_copy(
                r.probs.at[pl.ds(2 * number, 2)], s_probs.at[slot], r.probs_sem.at[slot]
            )

        def score_copy(number, slot):
            return pltpu.make_async_copy(
                s_score.at[slot], r.score_grad.at[:, pl.ds(2 * number, 2)],
                r.score_sem.at[slot],
            )

        def grads_copy(number, slot, part):
            columns = pl.ds(pl.multiple_of(part * width + number * pair, pair), pair)
            return pltpu.make_async_copy(
                s_grads.at[slot, part], r.grad_mixed.at[:, columns],
                r.grads_sem.at[slot, part],
            )

        probs_copy(0, 0).start()
        loads[6].wait()
        s_context_grad[length:, :] = jnp.zeros((padded - length, width), bf)
        s_context_grad[0:length, :] = dot_last(r.s_branch[...], s_wout[...]).astype(bf)
        s_context_grad_t[...] = s_context_grad[...].T
        communicate(now + 1)
        for number in (7, 8, 9):
            loads[number].wait()

        def one_pair(number, carry):
            slot = lax.rem(number, 2)
            probs_copy(number, slot).wait()

            @pl.when(number + 1 < pairs)
            def fetch():
                probs_copy(number + 1, 1 - slot).start()

            @pl.when(number >= 2)
            def free():
                score_copy(number - 2, slot).wait()
                for part in range(3):
                    grads_copy(number - 2, slot, part).wait()

            mine = pl.ds(pl.multiple_of(number * pair, pair), pair)
            attention_pair_backward(
                (
                    s_value.at[:, mine], s_context_grad_t.at[mine], s_context_grad.at[:, mine],
                    s_query.at[:, mine], s_key_t.at[mine], s_probs.at[slot], s_grads.at[slot],
                    s_score.at[slot], s_prob_grad, s_low,
                )
            )
            for row, part in ((0, 0), (1, 2)):
                r.s_sums[row : row + 1, mine] = jnp.sum(
                    s_grads[slot, part].astype(full32), axis=0, keepdims=True
                )
            score_copy(number, slot).start()
            for part in range(3):
                grads_copy(number, slot, part).start()
            for turn in range(pairs):
                if now + 2 + turn <= last:
                    @pl.when(number == turn)
                    def talk(turn=turn):
                        communicate(now + 2 + turn)

            return carry

        lax.fori_loop(0, pairs, one_pair, 0)
        for number in (pairs - 2, pairs - 1):
            score_copy(number, number % 2).wait()
            for part in range(3):
                grads_copy(number, number % 2, part).wait()

    pl.run_scoped(
        attention_phase,
        pltpu.VMEM((width, width), bf),
        pltpu.VMEM((padded, width), bf),
        pltpu.VMEM((width, padded), bf),
        pltpu.VMEM((padded, width), bf),
        pltpu.VMEM((width, length), bf),
        pltpu.VMEM((length, width), bf),
        pltpu.VMEM((2, 2, length, padded), bf),
        pltpu.VMEM((2, length, padded), full32),
        pltpu.VMEM((2, length, padded), bf),
        pltpu.VMEM((2, padded // LANES, 2, length, LANES), full32),
        pltpu.VMEM((2, 3, length, pair), bf),
    )
    for slot in range(now + 2 + pairs, last + 1):
        communicate(slot)
    store(r.s_sums, r.sums, 3)
    store(r.s_hidden, r.hidden_sums, 4)
    store(r.s_in, r.shard_in, 5)
    store(r.s_down, r.shard_down, 6)
    for made in stores[1:]:
        made.wait()


def feed_backward(inputs, in_shape, down_shape, collective):
    length, width = inputs.first_sum.shape
    hidden_units = inputs.slope.shape[1]
    padded = inputs.probs.shape[2]
    bf, full32 = jnp.bfloat16, jnp.float32
    shape = jax.ShapeDtypeStruct
    anywhere = pl.BlockSpec(memory_space=pl.ANY)
    waves = even_waves(1, down_shape, 2, (1, 1, 0)) + weight_waves(0, in_shape[0], in_shape[1], in_shape[0], 8)
    outs = [
        shape(in_shape, full32),
        shape(down_shape, full32),
        shape((length, width), bf),
        shape((length, width), full32),
        shape((length, width), bf),
        shape((length, 3 * width), bf),
        shape((padded // LANES, H, length, LANES), full32),
        shape((8, width), full32),
        shape((1, hidden_units), full32),
    ]
    sems = (len(waves), len(GATHER_ORDERS), hops_before(GATHER_ORDERS[0], 3) + 1)
    dma = pltpu.SemaphoreType.DMA
    scratch = [
        dma((len(waves),)), dma(sems), dma(sems), dma((10,)), dma((7,)), dma((2, 3)), dma((2,)),
        dma((2, 3)), dma((2,)),
        pltpu.VMEM((2,) + DIMS + (2, in_shape[0], waves[-1][3][-1] - waves[-1][3][0]), bf),
        pltpu.VMEM(in_shape, full32),
        pltpu.VMEM(down_shape, full32),
        pltpu.VMEM((length, width), full32),
        pltpu.VMEM((length, width), bf),
        pltpu.VMEM((8, width), full32),
        pltpu.VMEM((8, width), full32),
        pltpu.VMEM((1, hidden_units), full32),
        pltpu.VMEM((length, width), bf),
    ] + scatter_scratch(waves, [bf, bf])
    results = pl.pallas_call(
        functools.partial(feed_backward_kernel, waves),
        in_specs=[anywhere] * len(inputs),
        out_specs=[anywhere] * len(outs),
        out_shape=outs,
        scratch_shapes=scratch,
        compiler_params=pltpu.CompilerParams(
            collective_id=collective, has_side_effects=True, vmem_limit_bytes=VMEM_BYTES
        ),
    )(*inputs)
    return FeedOutputs(*results)


class LastInputs(typing.NamedTuple):
    row_in: typing.Any
    grad_mixed: typing.Any
    full_qkv: typing.Any
    context_t: typing.Any
    branch_grad: typing.Any
    score_grad: typing.Any
    packed_t: typing.Any
    grad_first_sum: typing.Any
    sums: typing.Any
    hidden_sums: typing.Any
    starts: typing.Any


class LastOutputs(typing.NamedTuple):
    shard_qkv: typing.Any
    shard_out: typing.Any
    shard_small: typing.Any
    grad_input: typing.Any


class LastRefs(typing.NamedTuple):
    row_in: typing.Any
    grad_mixed: typing.Any
    full_qkv: typing.Any
    context_t: typing.Any
    branch_grad: typing.Any
    score_grad: typing.Any
    packed_t: typing.Any
    grad_first_sum: typing.Any
    sums: typing.Any
    hidden_sums: typing.Any
    starts: typing.Any
    shard_qkv: typing.Any
    shard_out: typing.Any
    shard_small: typing.Any
    grad_input: typing.Any
    own_sem: typing.Any
    send: typing.Any
    recv: typing.Any
    load_sem: typing.Any
    store_sem: typing.Any
    score_sem: typing.Any
    s_stage: typing.Any
    s_small: typing.Any
    s_out_qkv: typing.Any
    s_out_out: typing.Any
    s_out_small: typing.Any
    s_row: typing.Any
    s_row_t: typing.Any
    s_mixed: typing.Any
    s_qkv: typing.Any
    s_context_t: typing.Any
    s_branch: typing.Any
    s_packed: typing.Any
    s_input: typing.Any
    s_sums: typing.Any
    s_hidden: typing.Any
    s_score: typing.Any
    s_work: typing.Any
    s_product: typing.Any


def last_backward_kernel(waves, *refs):
    r = LastRefs(*refs[: len(LastRefs._fields)])
    buffers = iter(refs[len(LastRefs._fields) :])
    place, core = coordinates()
    length, width = r.s_row.shape
    padded = r.s_packed.shape[0] * LANES
    rows_each = waves[0][2]
    loads = {}
    for number, (source, target) in enumerate(
        (
            (r.row_in, r.s_row), (r.grad_mixed, r.s_mixed), (r.context_t, r.s_context_t),
            (r.branch_grad, r.s_branch), (r.packed_t, r.s_packed), (r.full_qkv, r.s_qkv),
            (r.grad_first_sum, r.s_input), (r.sums, r.s_sums), (r.hidden_sums, r.s_hidden),
        )
    ):
        loads[number] = pltpu.make_async_copy(source, target, r.load_sem.at[number])
        loads[number].start()

    def score_copy(block, slot):
        rows = pl.ds(pl.multiple_of(block * GRAD_TILE, GRAD_TILE), GRAD_TILE)
        return pltpu.make_async_copy(
            r.score_grad.at[:, :, rows], r.s_score.at[slot], r.score_sem.at[slot]
        )

    score_copy(0, 0).start()
    greet(place, core)
    results = [r.s_out_qkv, r.s_out_out, r.s_out_small]
    main = len(waves) - 1
    steps = [
        scatter_steps(
            wave, number, r.s_small if number == main else r.s_stage.at[number % 2],
            results[wave[0]], buffers, r.own_sem, r.send, r.recv, place, core,
        )
        for number, wave in enumerate(waves)
    ]
    communicate, last = step_runner(steps, list(range(main)))
    spots = list(itertools.product(range(DIMS[1]), range(DIMS[2]), range(2)))
    size = len(spots) * rows_each
    loads[0].wait()
    r.s_row_t[...] = r.s_row[...].T
    loads[1].wait()
    for number in range(main):
        array, row, rows, bounds = waves[number]
        columns = slice(bounds[0], bounds[-1])
        if array == 1:
            loads[2].wait()
            loads[3].wait()

        def one_plane(plane, carry, array=array, number=number, columns=columns):
            units = pl.ds(pl.multiple_of(plane * size, size), size)
            if array == 0:
                product = dot_plain(r.s_row_t[units, :], r.s_mixed[:, columns])
            else:
                product = dot_plain(
                    r.s_context_t[units, 0:length], r.s_branch[:, columns]
                )
            for block, spot in enumerate(spots):
                r.s_stage[(number % 2, plane) + spot] = product[
                    block * rows_each : (block + 1) * rows_each
                ].astype(jnp.bfloat16)
            return carry

        lax.fori_loop(0, DIMS[0], one_plane, 0)
        communicate(number)
    loads[5].wait()
    loads[6].wait()
    strip = 256
    for start in range(0, width, strip):
        r.s_input[:, start : start + strip] = r.s_input[:, start : start + strip] + dot_last(
            r.s_mixed[...], r.s_qkv[start : start + strip, :]
        )
    stored = pltpu.make_async_copy(r.s_input, r.grad_input, r.store_sem.at[0])
    stored.start()
    communicate(main)
    loads[4].wait()
    parts = padded // LANES
    span = WINDOW_TILES * LANES
    levels = lax.broadcasted_iota(jnp.int32, (LOW_PARTS, span), 0).astype(jnp.bfloat16)
    one = jnp.ones((LOW_PARTS, span), jnp.bfloat16)
    no_one = jnp.zeros((LOW_PARTS, span), jnp.bfloat16)
    nothing = jnp.zeros((H, span), jnp.bfloat16)

    def window(tiles, turn):
        rolled = [pltpu.roll(one_tile, (LANES - turn) & (LANES - 1), 1) for one_tile in tiles]
        kept = lax.broadcasted_iota(jnp.int32, tiles[0].shape, 1) < LANES - turn
        return jnp.concatenate(
            [jnp.where(kept, here, after) for here, after in zip(rolled[:-1], rolled[1:])],
            axis=1,
        )

    def spread_digit(digit, rows):
        as_float = digit.astype(jnp.float32)
        low = jnp.concatenate([as_float, as_float], axis=0).astype(jnp.bfloat16)
        return jnp.concatenate([low] * (rows // 16), axis=0)

    r.s_product[...] = jnp.zeros(r.s_product.shape, jnp.float32)
    blocks = length // GRAD_TILE

    def one_block(block, carry):
        slot = lax.rem(block, 2)

        @pl.when(block + 1 < blocks)
        def fetch():
            score_copy(block + 1, 1 - slot).start()

        score_copy(block, slot).wait()
        r.s_work[...] = r.s_score[slot]
        flat = r.s_work.reshape(parts * H * GRAD_TILE, LANES)

        def one_group(group, total):
            lefts = []
            rights = []
            for offset in range(ROWS_AT_ONCE):
                row = group * ROWS_AT_ONCE + offset
                begin = r.starts[block * GRAD_TILE + row]
                tile = begin // LANES
                turn = lax.rem(begin, LANES)
                grads_parts = []
                packed_parts = []
                for part in range(WINDOW_TILES + 1):
                    which = lax.rem(tile + part, parts)
                    grads_parts.append(
                        flat[pl.ds(which * H * GRAD_TILE + row, H, stride=GRAD_TILE), :]
                    )
                    packed_parts.append(
                        jnp.broadcast_to(
                            r.s_packed[which, pl.ds(block * GRAD_TILE + row, 1), :], (8, LANES)
                        )
                    )
                grads = window(grads_parts, turn).astype(jnp.bfloat16)
                packed = window(packed_parts, turn)
                masked = []
                onehot = []
                for table in range(3):
                    high = spread_digit((packed >> (7 * table + 5)) & (HIGH_PARTS - 1), H)
                    for part in range(HIGH_PARTS):
                        masked.append(jnp.where(high == jnp.bfloat16(part), grads, nothing))
                    low = spread_digit((packed >> (7 * table)) & (LOW_PARTS - 1), LOW_PARTS)
                    onehot.append(jnp.where(low == levels, one, no_one))
                lefts.append(jnp.concatenate(masked, axis=0))
                rights.append(jnp.concatenate(onehot, axis=0))
            return total + dot_last(
                jnp.concatenate(lefts, axis=1), jnp.concatenate(rights, axis=1)
            )

        total = lax.fori_loop(
            0, GRAD_TILE // ROWS_AT_ONCE, one_group, jnp.zeros(r.s_product.shape, jnp.float32)
        )
        r.s_product[...] = r.s_product[...] + total
        for turn in range(blocks):
            if main + 1 + turn <= last:
                @pl.when(block == turn)
                def talk(turn=turn):
                    communicate(main + 1 + turn)

        return carry

    lax.fori_loop(0, blocks, one_block, 0)
    for slot in range(main + 1 + blocks, last + 1):
        communicate(slot)
    loads[7].wait()
    loads[8].wait()
    lane = lax.broadcasted_iota(jnp.int32, (H, LANES), 1)
    product = jnp.concatenate(
        [
            r.s_product[...],
            jnp.zeros((3 * HIGH_PARTS * H, LANES - 3 * LOW_PARTS), jnp.float32),
        ],
        axis=1,
    )
    tables = []
    for table in range(3):
        whole = jnp.zeros((H, LANES), jnp.float32)
        for part in range(HIGH_PARTS):
            start = (table * HIGH_PARTS + part) * H
            turned = pltpu.roll(
                product[start : start + H], ((part - table) * LOW_PARTS) % LANES, 1
            )
            inside = (lane >= part * LOW_PARTS) & (lane < (part + 1) * LOW_PARTS)
            whole = jnp.where(inside, turned, whole)
        tables.append(whole)
    devices = DIMS[0] * DIMS[1] * DIMS[2] * 2
    group = LANES // (width // devices)
    buckets_each = 3 * NB // devices
    empty = jnp.zeros((7, LANES), jnp.float32)
    for device in range(devices):
        spot = (device // 8, (device // 4) % 2, (device // 2) % 2, device % 2)
        columns = slice(device // group * LANES, (device // group + 1) * LANES)
        low = device * buckets_each
        table = low // NB
        mine = tables[table]
        if (low + buckets_each - 1) // NB > table:
            mine = jnp.where(lane >= low - table * NB, mine, tables[table + 1])
        hidden = r.s_hidden[:, device * LANES : (device + 1) * LANES]
        r.s_small[spot] = jnp.concatenate(
            [r.s_sums[:, columns], hidden, empty, mine], axis=0
        )
    for step in steps[main]:
        step()
    stores = [stored]
    for number, (source, target) in enumerate(
        ((r.s_out_qkv, r.shard_qkv), (r.s_out_out, r.shard_out), (r.s_out_small, r.shard_small))
    ):
        stores.append(
            pltpu.make_async_copy(source, target, r.store_sem.at[number + 1])
        )
        stores[-1].start()
    for made in stores:
        made.wait()


def last_backward(inputs, qkv_shape, out_shape, collective):
    length, width = inputs.row_in.shape
    hidden_units = inputs.hidden_sums.shape[1]
    padded = inputs.packed_t.shape[0] * LANES
    bf, full32 = jnp.bfloat16, jnp.float32
    shape = jax.ShapeDtypeStruct
    anywhere = pl.BlockSpec(memory_space=pl.ANY)
    small_rows = 16 + H
    waves = weight_waves(0, qkv_shape[0], qkv_shape[1], qkv_shape[0], 8)
    waves += weight_waves(1, out_shape[0], out_shape[1], out_shape[0], 8)
    waves.append(wave_of(2, 0, small_rows, 0, 1, 0, 0))
    outs = [
        shape(qkv_shape, full32),
        shape(out_shape, full32),
        shape((small_rows, LANES), full32),
        shape((length, width), full32),
    ]
    sems = (len(waves), len(GATHER_ORDERS), hops_before(GATHER_ORDERS[0], 3) + 1)
    dma = pltpu.SemaphoreType.DMA
    scratch = [
        dma((len(waves),)), dma(sems), dma(sems), dma((9,)), dma((4,)), dma((2,)),
        pltpu.VMEM((2,) + DIMS + (2, qkv_shape[0], waves[0][3][-1] - waves[0][3][0]), bf),
        pltpu.VMEM(DIMS + (2, small_rows, LANES), full32),
        pltpu.VMEM(qkv_shape, full32),
        pltpu.VMEM(out_shape, full32),
        pltpu.VMEM((small_rows, LANES), full32),
        pltpu.VMEM((length, width), bf),
        pltpu.VMEM((width, length), bf),
        pltpu.VMEM((length, 3 * width), bf),
        pltpu.VMEM((width, 3 * width), bf),
        pltpu.VMEM((width, padded), bf),
        pltpu.VMEM((length, width), bf),
        pltpu.VMEM((padded // LANES, length, LANES), jnp.int32),
        pltpu.VMEM((length, width), full32),
        pltpu.VMEM((8, width), full32),
        pltpu.VMEM((1, hidden_units), full32),
        pltpu.VMEM((2, padded // LANES, H, GRAD_TILE, LANES), full32),
        pltpu.VMEM((padded // LANES, H, GRAD_TILE, LANES), full32),
        pltpu.VMEM((3 * HIGH_PARTS * H, 3 * LOW_PARTS), full32),
    ] + scatter_scratch(waves, [bf, bf, full32])
    results = pl.pallas_call(
        functools.partial(last_backward_kernel, waves),
        in_specs=[anywhere] * (len(inputs) - 1) + [pl.BlockSpec(memory_space=pltpu.SMEM)],
        out_specs=[anywhere] * len(outs),
        out_shape=outs,
        scratch_shapes=scratch,
        compiler_params=pltpu.CompilerParams(
            collective_id=collective, has_side_effects=True, vmem_limit_bytes=VMEM_BYTES
        ),
    )(*inputs)
    return LastOutputs(*results)


def even_waves(array, shape, tiles, parts):
    return [
        wave_of(array, 0, shape[0], tile * LANES, *parts)
        for tile in range(0, shape[1] // LANES, tiles)
    ]


def split_wave(array, row, rows, column, tiles, turn):
    edge = tiles // 8
    one = (tiles - edge + turn) // 2
    return wave_of(array, row, rows, column, one, tiles - edge - one, edge)


def forward_plan(weights, small):
    w_qkv, w_out, w_in, w_down = weights
    waves = [wave_of(4, 0, small.shape[0], 0, 1, 0, 0)]
    waves += weight_waves(0, w_qkv.shape[0], w_qkv.shape[1], w_qkv.shape[0], 8)
    early = len(waves)
    waves += weight_waves(1, w_out.shape[0], w_out.shape[1], w_out.shape[0], 8)
    waves += weight_waves(2, w_in.shape[0], w_in.shape[1], w_in.shape[0], 8)
    waves += even_waves(3, w_down.shape, 2, (1, 1, 0))
    starts = [(number, 1) if number < early else (number, LAG) for number in range(len(waves))]
    return waves, starts


def weight_waves(array, rows, columns, row_step, tile_step):
    waves = []
    tiles = columns // LANES
    for row in range(0, rows, row_step):
        for tile in range(0, tiles, tile_step):
            size = min(tile_step, tiles - tile)
            waves.append(
                split_wave(array, row, row_step, tile * LANES, size, (len(waves) + array) % 2)
            )
    return waves


def attention_forward_kernel(
    key_ref, query_ref, value_ref, packed_ref, table_ref, mask_ref, probs_ref, context_ref,
    score_ref,
):
    length = key_ref.shape[0]
    padded = packed_ref.shape[1]
    pair = query_ref.shape[0]
    half = pair // 2
    feature = lax.broadcasted_iota(jnp.int32, (pair, padded), 0)
    queries = query_ref[...]
    zero = jnp.zeros_like(queries)
    score_ref[0] = dot_plain(key_ref[...], jnp.where(feature < half, queries, zero))
    score_ref[1] = dot_plain(key_ref[...], jnp.where(feature < half, zero, queries))
    for column in range(0, padded, LANES):
        lanes = slice(column, column + LANES)
        rows = [jnp.broadcast_to(table_ref[t, 0], (8, LANES)) for t in range(3)]
        tops = [jnp.full((8, LANES), 3.0 * MASK_FILL, jnp.float32) for side in range(2)]
        for start in range(0, length, 8):
            here = slice(start, start + 8)
            packed = packed_ref[here, lanes]
            sums = [None, None]
            for table in range(3):
                index = (packed >> (7 * table)) & (NB - 1)
                word = jnp.take_along_axis(rows[table], index, axis=1)
                for side, term in ((0, word >> 16), (1, (word << 16) >> 16)):
                    sums[side] = term if table == 0 else sums[side] + term
            mask = mask_ref[here, lanes]
            for side in range(2):
                scores = score_ref[side, here, lanes] + (
                    sums[side].astype(jnp.float32) * (1.0 / TABLE_STEP) + mask
                )
                score_ref[side, here, lanes] = scores
                tops[side] = jnp.maximum(tops[side], scores)
        for side in range(2):
            top = jnp.max(tops[side], axis=0, keepdims=True)
            exponent = jnp.exp(score_ref[side, :, lanes] - top)
            total = jnp.sum(exponent, axis=0, keepdims=True)
            probs_ref[side, :, lanes] = (exponent * (1.0 / total)).astype(jnp.bfloat16)
    for side in range(2):
        mine = slice(side * half, (side + 1) * half)
        context_ref[mine, :] = dot_plain(value_ref[mine, :], probs_ref[side]).astype(jnp.bfloat16)


def attention_forward(keys, queries_t, values_t, packed, tables, mask):
    length, width = keys.shape
    padded = packed.shape[1]
    pairs = H // 2
    pair = width // pairs
    whole = pl.BlockSpec((length, padded), lambda p: (0, 0))
    return pl.pallas_call(
        attention_forward_kernel,
        grid=(pairs,),
        in_specs=[
            pl.BlockSpec((length, pair), lambda p: (0, p)),
            pl.BlockSpec((pair, padded), lambda p: (p, 0)),
            pl.BlockSpec((pair, length), lambda p: (p, 0)),
            whole,
            pl.BlockSpec((3, 1, 1, NB), lambda p: (0, p, 0, 0)),
            whole,
        ],
        out_specs=[
            pl.BlockSpec((2, length, padded), lambda p: (p, 0, 0)),
            pl.BlockSpec((pair, padded), lambda p: (p, 0)),
        ],
        out_shape=[
            jax.ShapeDtypeStruct((H, length, padded), jnp.bfloat16),
            jax.ShapeDtypeStruct((width, padded), jnp.bfloat16),
        ],
        scratch_shapes=[pltpu.VMEM((2, length, padded), jnp.float32)],
        compiler_params=pltpu.CompilerParams(vmem_limit_bytes=VMEM_BYTES),
    )(keys, queries_t, values_t, packed, tables, mask)


def attention_backward_kernel(
    value_ref, context_grad_t_ref, context_grad_ref, query_ref, key_t_ref, probs_ref,
    grad_query_ref, grad_key_ref, grad_value_ref, score_grad_ref, prob_grad_ref, low_ref,
):
    length = value_ref.shape[0]
    pair, padded = context_grad_t_ref.shape
    half = pair // 2
    scale = half ** (-0.5)
    feature = lax.broadcasted_iota(jnp.int32, (pair, padded), 0)
    upstream = context_grad_t_ref[...]
    zero = jnp.zeros_like(upstream)
    prob_grad_ref[0] = dot_plain(value_ref[...], jnp.where(feature < half, upstream, zero))
    prob_grad_ref[1] = dot_plain(value_ref[...], jnp.where(feature < half, zero, upstream))
    for part in range(padded // LANES):
        lanes = slice(part * LANES, (part + 1) * LANES)
        for side in range(2):
            probs = probs_ref[side, :, lanes].astype(jnp.float32)
            prob_grad = prob_grad_ref[side, :, lanes]
            inner = jnp.sum(probs * prob_grad, axis=0, keepdims=True)
            score_grad = probs * (prob_grad - inner)
            score_grad_ref[part, side] = score_grad
            low_ref[side, :, lanes] = score_grad.astype(jnp.bfloat16)
    for side in range(2):
        mine = slice(side * half, (side + 1) * half)
        grad_query_ref[mine, :] = (dot_plain(key_t_ref[mine, :], low_ref[side]) * scale).astype(
            jnp.bfloat16
        )
    first_half = lax.broadcasted_iota(jnp.int32, (length, pair), 1) < half
    grad_key = [dot_plain(low_ref[side], query_ref[...]) for side in range(2)]
    grad_key_ref[...] = jnp.where(first_half, grad_key[0], grad_key[1]).astype(jnp.bfloat16)
    grad_value = [dot_plain(probs_ref[side], context_grad_ref[...]) for side in range(2)]
    grad_value_ref[...] = jnp.where(first_half, grad_value[0], grad_value[1]).astype(jnp.bfloat16)


def attention_backward(values, context_grad_t, context_grad, queries, keys_t, probs):
    length, width = values.shape
    padded = probs.shape[2]
    pairs = H // 2
    pair = width // pairs
    natural = pl.BlockSpec((length, pair), lambda p: (0, p))
    longer = pl.BlockSpec((padded, pair), lambda p: (0, p))
    flipped = pl.BlockSpec((pair, padded), lambda p: (p, 0))
    return pl.pallas_call(
        attention_backward_kernel,
        grid=(pairs,),
        in_specs=[
            natural,
            flipped,
            longer,
            longer,
            pl.BlockSpec((pair, length), lambda p: (p, 0)),
            pl.BlockSpec((2, length, padded), lambda p: (p, 0, 0)),
        ],
        out_specs=[
            flipped,
            natural,
            natural,
            pl.BlockSpec((padded // LANES, 2, length, LANES), lambda p: (0, p, 0, 0)),
        ],
        out_shape=[
            jax.ShapeDtypeStruct((width, padded), jnp.bfloat16),
            jax.ShapeDtypeStruct((length, width), jnp.bfloat16),
            jax.ShapeDtypeStruct((length, width), jnp.bfloat16),
            jax.ShapeDtypeStruct((padded // LANES, H, length, LANES), jnp.float32),
        ],
        scratch_shapes=[
            pltpu.VMEM((2, length, padded), jnp.float32),
            pltpu.VMEM((2, length, padded), jnp.bfloat16),
        ],
        compiler_params=pltpu.CompilerParams(vmem_limit_bytes=VMEM_BYTES),
    )(values, context_grad_t, context_grad, queries, keys_t, probs)


def table_grad_kernel(digit_ref, score_grad_ref, out_ref):
    padded = score_grad_ref.shape[0] * LANES

    @pl.when(pl.program_id(0) == 0)
    def start():
        out_ref[...] = jnp.zeros_like(out_ref)

    levels = lax.broadcasted_iota(jnp.int32, (LOW_PARTS, padded), 0).astype(jnp.bfloat16)
    one = jnp.ones((LOW_PARTS, padded), jnp.bfloat16)
    no_one = jnp.zeros((LOW_PARTS, padded), jnp.bfloat16)
    nothing = jnp.zeros((H, padded), jnp.bfloat16)
    flat_ref = score_grad_ref.reshape(padded // LANES * H * GRAD_TILE, LANES)

    def one_group(group, total):
        for offset in range(4):
            row = group * 4 + offset
            grads = jnp.concatenate(
                [
                    flat_ref[pl.ds(part * H * GRAD_TILE + row, H, stride=GRAD_TILE), :]
                    for part in range(padded // LANES)
                ],
                axis=1,
            ).astype(jnp.bfloat16)
            masked = []
            onehot = []
            for table in range(3):
                high = jnp.broadcast_to(digit_ref[row, table : table + 1, :], (H, padded))
                for part in range(HIGH_PARTS):
                    masked.append(jnp.where(high == jnp.bfloat16(part), grads, nothing))
                low = jnp.broadcast_to(digit_ref[row, 3 + table : 4 + table, :], (LOW_PARTS, padded))
                onehot.append(jnp.where(low == levels, one, no_one))
            total = total + dot_last(jnp.concatenate(masked, axis=0), jnp.concatenate(onehot, axis=0))
        return total

    out_ref[...] += lax.fori_loop(
        0, GRAD_TILE // 4, one_group, jnp.zeros(out_ref.shape, jnp.float32)
    )


def table_grads(digits, score_grad):
    length = score_grad.shape[2]
    padded = score_grad.shape[0] * LANES
    shape = (3 * HIGH_PARTS * H, 3 * LOW_PARTS)
    products = pl.pallas_call(
        table_grad_kernel,
        grid=(length // GRAD_TILE,),
        in_specs=[
            pl.BlockSpec((GRAD_TILE, 6, padded), lambda i: (i, 0, 0)),
            pl.BlockSpec((padded // LANES, H, GRAD_TILE, LANES), lambda i: (0, 0, i, 0)),
        ],
        out_specs=pl.BlockSpec(shape, lambda i: (0, 0)),
        out_shape=jax.ShapeDtypeStruct(shape, jnp.float32),
        compiler_params=pltpu.CompilerParams(vmem_limit_bytes=VMEM_BYTES),
    )(digits, score_grad)
    split = products.reshape(3, HIGH_PARTS, H, 3, LOW_PARTS)
    return jnp.stack(
        [jnp.transpose(split[t, :, :, t, :], (0, 2, 1)).reshape(NB, H) for t in range(3)]
    )


def norm_backward(inputs, gain_row, upstream):
    average = jnp.mean(inputs, axis=-1, keepdims=True)
    centered = inputs - average
    spread = lax.rsqrt(jnp.mean(centered * centered, axis=-1, keepdims=True) + EPSILON)
    normed = centered * spread
    scaled = upstream * gain_row
    grad = spread * (
        scaled
        - jnp.mean(scaled, axis=-1, keepdims=True)
        - normed * jnp.mean(scaled * normed, axis=-1, keepdims=True)
    )
    return grad, jnp.sum(upstream * normed, axis=0), jnp.sum(upstream, axis=0)


def spread_small(everything, vec_bias, norm_gain, bias_hidden):
    devices = everything.shape[0]
    vec_size, gain_size = vec_bias.size, norm_gain.size
    vectors, gains, hidden, tables = jnp.split(
        everything, [vec_size, vec_size + gain_size, vec_size + gain_size + bias_hidden.size], axis=1
    )
    vectors = jnp.transpose(vectors.reshape(devices, vec_bias.shape[0], -1), (1, 0, 2))
    gains = jnp.transpose(gains.reshape(devices, norm_gain.shape[0], -1), (1, 0, 2))
    rows = jnp.concatenate(
        [vectors.reshape(vec_bias.shape[0], -1), gains.reshape(norm_gain.shape[0], -1)], axis=0
    )
    return rows.astype(jnp.float32), hidden.reshape(-1).astype(jnp.float32), tables.reshape(3, NB, H)


def forward_by_ops(
    weights, row_in, buckets, segments, validity, vec_bias, norm_gain, bias_hidden, rel_tables
):
    length, width = row_in.shape
    padded = -(-length // LANES) * LANES
    scale = (width // H) ** (-0.5)
    full = [lax.all_gather(weight, BOTH, axis=0, tiled=True) for weight in weights]
    small = jnp.concatenate(
        [vec_bias.reshape(-1), norm_gain.reshape(-1), bias_hidden, rel_tables]
    )
    everything = lax.all_gather(small, BOTH, axis=0, tiled=False)
    vectors, hidden_bias, tables = spread_small(everything, vec_bias, norm_gain, bias_hidden)
    wide = ((0, 0), (0, padded - length))
    flipped = jnp.swapaxes(buckets, 1, 2)
    packed = jnp.pad(flipped[0] | (flipped[1] << 7) | (flipped[2] << 14), wide)
    position = jnp.arange(length)
    allowed = (segments[:, None] == segments[None, :]) & (
        (validity[:, None] > 0) | (position[:, None] == position[None, :])
    )
    mask = jnp.pad(jnp.where(allowed, 0.0, MASK_FILL), wide)
    fixed = jnp.round(tables.astype(jnp.float32) * TABLE_STEP).astype(jnp.int32)
    pair_tables = (fixed[:, :, 0::2] << 16) | (fixed[:, :, 1::2] & 0xFFFF)
    pair_tables = jnp.transpose(pair_tables, (0, 2, 1))[:, :, None, :]
    mixed = dot_plain(row_in, full[0])
    queries = (mixed[:, :width] + vectors[0]).astype(jnp.bfloat16) * jnp.bfloat16(scale)
    keys = mixed[:, width : 2 * width].astype(jnp.bfloat16)
    values = (mixed[:, 2 * width :] + vectors[1]).astype(jnp.bfloat16)
    queries = jnp.pad(queries, ((0, padded - length), (0, 0)))
    probs, context_t = attention_forward(keys, queries.T, values.T, packed, pair_tables, mask)
    branch = dot_first(context_t[:, :length], full[1])
    first_sum = row_in.astype(jnp.float32) + branch + vectors[2]
    normed_first = layer_norm(first_sum, vectors[6], vectors[4])
    first_low = normed_first.astype(jnp.bfloat16)
    hidden = dot_plain(first_low, full[2]) + hidden_bias
    active, slope = gelu_and_slope(hidden)
    active = active.astype(jnp.bfloat16)
    second_sum = normed_first + dot_plain(active, full[3]) + vectors[3]
    return full + [
        probs, context_t, queries, keys.T, values, first_sum, first_low, active, slope,
        second_sum, vectors, packed,
    ]


class Kept(typing.NamedTuple):
    full_qkv: typing.Any
    full_out: typing.Any
    full_in: typing.Any
    full_down: typing.Any
    probs: typing.Any
    context_t: typing.Any
    queries: typing.Any
    keys_t: typing.Any
    values: typing.Any
    first_sum: typing.Any
    first_low: typing.Any
    active_t: typing.Any
    slope: typing.Any
    second_sum: typing.Any
    vectors: typing.Any
    packed_t: typing.Any


def body(
    own_kernels, block_input, cotangent, seg_ids, slot_valid, rel_buckets, w_qkv, w_out, w_in,
    w_down, vec_bias, norm_gain, bias_hidden, rel_tables,
):
    row_in = block_input[0]
    row_cot = cotangent[0].astype(jnp.float32)
    length, width = row_in.shape
    devices = lax.axis_size(BOTH)
    weights = [w_qkv, w_out, w_in, w_down]
    if own_kernels:
        device = lax.axis_index("dp") * 2 + lax.axis_index("fsdp")
        small = small_block(device, vec_bias, norm_gain, bias_hidden, rel_tables)
        waves, starts = forward_plan(weights, small)
        forward = forward_all(
            weights, small, row_in, rel_buckets[0], seg_ids[0], slot_valid[0], waves, starts, 1
        )
        forward = [whole.reshape(-1, whole.shape[-1]) for whole in forward[:4]] + list(forward[4:])
    else:
        forward = forward_by_ops(
            weights, row_in, rel_buckets[0], seg_ids[0], slot_valid[0], vec_bias, norm_gain,
            bias_hidden, rel_tables,
        )
    if own_kernels:
        kept = Kept(*forward)
        fed = feed_backward(
            FeedInputs(
                kept.full_in, kept.full_down, kept.full_out, kept.second_sum, cotangent[0],
                kept.first_sum, kept.first_low, kept.active_t, kept.slope, kept.probs,
                kept.queries, kept.keys_t, kept.values, kept.vectors,
            ),
            w_in.shape, w_down.shape, 2,
        )
        segments = seg_ids[0]
        starts = jnp.sum(segments[None, :] < segments[:, None], axis=1, dtype=jnp.int32)
        done = last_backward(
            LastInputs(
                row_in, fed.grad_mixed, kept.full_qkv, kept.context_t, fed.branch_grad,
                fed.score_grad, kept.packed_t, fed.grad_first_sum, fed.sums, fed.hidden_sums,
                starts,
            ),
            w_qkv.shape, w_out.shape, 3,
        )
        small = done.shard_small
        piece = vec_bias.shape[1]
        vec_rows = vec_bias.shape[0]
        sums = lax.dynamic_slice(
            small, (0, device % (LANES // piece) * piece), (8, piece)
        )
        buckets_each = rel_tables.shape[0] // H
        twice = jnp.concatenate([small[16:], small[16:]], axis=1)
        tables = lax.dynamic_slice(twice, (0, device * buckets_each % NB), (H, buckets_each))
        return (
            fed.output[None],
            done.grad_input[None],
            done.shard_qkv,
            done.shard_out,
            fed.shard_in,
            fed.shard_down,
            sums[:vec_rows],
            sums[vec_rows:],
            small[8],
            tables.T.reshape(-1),
        )
    (
        full_qkv, full_out, full_in, full_down, probs, context_t, queries, keys_t, values,
        first_sum, first_low, active, slope, second_sum, vectors, packed,
    ) = forward
    padded = packed.shape[1]
    gains = vectors[6:8]
    taller = ((0, padded - length), (0, 0))
    context_t = context_t[:, :length]
    digits = jnp.stack(
        [
            (packed >> (7 * t + shift)) & mask
            for shift, mask in ((5, HIGH_PARTS - 1), (0, LOW_PARTS - 1))
            for t in range(3)
        ],
        axis=1,
    ).astype(jnp.bfloat16)
    output = layer_norm(second_sum, gains[1], vectors[5]).astype(jnp.bfloat16)

    grad_second, grad_gain_two, grad_shift_two = norm_backward(second_sum, gains[1], row_cot)
    down_grad = grad_second.astype(jnp.bfloat16)
    grad_w_down = dot_first(active, down_grad).astype(jnp.bfloat16)
    hidden_grad = (dot_last(down_grad, full_down) * slope.astype(jnp.float32)).astype(jnp.bfloat16)
    grad_w_in = dot_first(first_low, hidden_grad).astype(jnp.bfloat16)
    grad_first = dot_last(hidden_grad, full_in) + grad_second
    grad_first_sum, grad_gain_one, grad_shift_one = norm_backward(first_sum, gains[0], grad_first)
    branch_grad = grad_first_sum.astype(jnp.bfloat16)
    grad_w_out = dot_plain(context_t, branch_grad).astype(jnp.bfloat16)
    context_grad = jnp.pad(dot_last(branch_grad, full_out).astype(jnp.bfloat16), taller)
    grad_queries_t, grad_keys, grad_values, score_grad = attention_backward(
        values, context_grad.T, context_grad, queries, keys_t, probs
    )
    grad_queries = grad_queries_t[:, :length].T
    grad_mixed = jnp.concatenate([grad_queries, grad_keys, grad_values], axis=1)
    grad_w_qkv = dot_first(row_in, grad_mixed).astype(jnp.bfloat16)
    grad_input = grad_first_sum + dot_last(grad_mixed, full_qkv)
    grad_tables = table_grads(digits, score_grad)

    grad_vectors = jnp.stack(
        [
            jnp.sum(grad_queries.astype(jnp.float32), axis=0),
            jnp.sum(grad_values.astype(jnp.float32), axis=0),
            jnp.sum(branch_grad.astype(jnp.float32), axis=0),
            jnp.sum(down_grad.astype(jnp.float32), axis=0),
            grad_shift_one,
            grad_shift_two,
        ]
    )
    grad_gains = jnp.stack([grad_gain_one, grad_gain_two])
    grad_hidden_bias = jnp.sum(hidden_grad.astype(jnp.float32), axis=0)

    def by_device(matrix):
        return jnp.transpose(matrix.reshape(matrix.shape[0], devices, -1), (1, 0, 2)).reshape(
            devices, -1
        )

    small_grads = jnp.concatenate(
        [
            by_device(grad_vectors),
            by_device(grad_gains),
            grad_hidden_bias.reshape(devices, -1),
            grad_tables.reshape(devices, -1),
        ],
        axis=1,
    )
    weight_grads = [grad_w_qkv, grad_w_out, grad_w_in, grad_w_down]
    shards = [
        lax.psum_scatter(
            grad.astype(jnp.float32), BOTH, scatter_dimension=0, tiled=True
        )
        for grad in weight_grads
    ]
    small_shard = lax.psum_scatter(small_grads, BOTH, scatter_dimension=0, tiled=True)[0]
    shard_vectors, shard_gains, shard_hidden, shard_tables = jnp.split(
        small_shard,
        [
            vec_bias.size,
            vec_bias.size + norm_gain.size,
            vec_bias.size + norm_gain.size + bias_hidden.size,
        ],
    )
    return (
        output[None],
        grad_input[None],
        shards[0],
        shards[1],
        shards[2],
        shards[3],
        shard_vectors.reshape(vec_bias.shape),
        shard_gains.reshape(norm_gain.shape),
        shard_hidden,
        shard_tables,
    )


def solution(mesh):
    rows = P(BOTH)
    columns = P(None, BOTH)
    in_specs = (rows,) * 9 + (columns, columns, rows, rows)
    out_specs = (rows,) * 6 + (columns, columns, rows, rows)
    chips = DIMS[0] * DIMS[1] * DIMS[2]
    own_kernels = mesh.shape["dp"] == chips and mesh.shape["fsdp"] == 2
    return jax.shard_map(
        functools.partial(body, own_kernels),
        mesh=mesh,
        in_specs=in_specs,
        out_specs=out_specs,
        check_vma=False,
    )
```

```python
import functools
import itertools
import typing

import jax
import jax.numpy as jnp
from jax import lax
from jax.experimental import pallas as pl
from jax.experimental.pallas import tpu as pltpu
from jax.sharding import PartitionSpec as P

H = 16
NB = 128
LANES = 128
EPSILON = 1e-05
MASK_FILL = -1e30
TABLE_STEP = 8192.0
VMEM_BYTES = 60 << 20
BOTH = ("dp", "fsdp")
MESH = pl.DeviceIdType.MESH
DIMS = (4, 2, 2)
GATHER_ORDERS = ((0, 2, 1), (0, 1, 2), (2, 1, 0))
STEPS = 5
LAG = 3
GRAD_TILE = 64
ROWS_AT_ONCE = 16
WINDOW_TILES = 3
HIGH_PARTS = 4
LOW_PARTS = NB // HIGH_PARTS


def dot_plain(left, right):
    return jnp.dot(left, right, preferred_element_type=jnp.float32)


def dot_first(left, right):
    return lax.dot_general(
        left, right, (((0,), (0,)), ((), ())), preferred_element_type=jnp.float32
    )


def dot_last(left, right):
    return lax.dot_general(
        left, right, (((1,), (1,)), ((), ())), preferred_element_type=jnp.float32
    )


def layer_norm(inputs, gain_row, shift_row):
    average = jnp.mean(inputs, axis=-1, keepdims=True)
    centered = inputs - average
    variance = jnp.mean(centered * centered, axis=-1, keepdims=True)
    return centered * lax.rsqrt(variance + EPSILON) * gain_row + shift_row


def gelu_exact(inputs):
    return jax.nn.gelu(inputs, approximate=False)


def coordinates():
    chip = lax.axis_index("dp")
    core = lax.axis_index("fsdp")
    planes, rows, columns = DIMS
    place = (
        chip // (rows * columns),
        lax.rem(chip // columns, rows),
        lax.rem(chip, columns),
    )
    return place, core


def device_at(place, core):
    return ((place[0] * DIMS[1] + place[1]) * DIMS[2] + place[2], core)


def shifted(place, axis, distance):
    moved = list(place)
    moved[axis] = lax.rem(moved[axis] + distance, DIMS[axis])
    return tuple(moved)


def greet(place, core):
    barrier = pltpu.get_barrier_semaphore()
    peers = [
        device_at(shifted(place, axis, distance), core)
        for axis in range(3)
        for distance in range(1, DIMS[axis])
    ]
    peers.append(device_at(place, 1 - core))
    for peer in peers:
        pl.semaphore_signal(barrier, inc=1, device_id=peer, device_id_type=MESH)
    pl.semaphore_wait(barrier, len(peers))


def schedule(waves, lag):
    events = []
    for wave in range(waves):
        for step in range(STEPS):
            events.append((wave + lag * step, wave, step))
    return [(wave, step) for slot, wave, step in sorted(events)]


def wave_of(array, row, rows, column, *tiles):
    bounds = [column]
    for count in tiles:
        bounds.append(bounds[-1] + count * LANES)
    return (array, row, rows, tuple(bounds))


def hops_before(order, phase):
    return sum(DIMS[axis] - 1 for axis in order[:phase])


def gather_steps(wave, number, full, outs, send, recv, out_sem, place, core):
    array, row, rows, bounds = wave
    whole = full[array]
    routes = [r for r in range(len(GATHER_ORDERS)) if bounds[r + 1] > bounds[r]]
    total_hops = hops_before(GATHER_ORDERS[0], 3)

    def copy(route, slot, index, target):
        part = whole.at[
            index[0], index[1], index[2], core,
            pl.ds(row, rows), pl.ds(bounds[route], bounds[route + 1] - bounds[route]),
        ]
        return pltpu.make_async_remote_copy(
            part, part, send.at[number, route, slot], recv.at[number, route, slot],
            device_id=target, device_id_type=MESH,
        )

    def to_core(route, phase, distance):
        if phase is None:
            return copy(route, total_hops, list(place), device_at(place, 1 - core))
        order = GATHER_ORDERS[route]
        axis = order[phase]
        index = list(place)
        for done in order[:phase]:
            index[done] = slice(None)
        index[axis] = lax.rem(place[axis] + DIMS[axis] - distance, DIMS[axis])
        slot = total_hops + hops_before(order, phase) + distance
        return copy(route, slot, index, device_at(place, 1 - core))

    def hop(route, phase, distance):
        order = GATHER_ORDERS[route]
        index = list(place)
        for axis in order[:phase]:
            index[axis] = slice(None)
        return copy(
            route, hops_before(order, phase) + distance - 1, index,
            device_at(shifted(place, order[phase], distance), core),
        )

    def hops(phase):
        return [
            (route, phase, distance)
            for route in routes
            for distance in range(1, DIMS[GATHER_ORDERS[route][phase]])
        ]

    def launch(phase):
        for which in hops(phase):
            hop(*which).start()

    def land(phase):
        for which in hops(phase):
            hop(*which).wait_recv()
            to_core(*which).start()

    def out_copy():
        part = (slice(None),) * 4 + (
            pl.ds(row, rows), pl.ds(bounds[0], bounds[-1] - bounds[0]),
        )
        return pltpu.make_async_copy(
            full[array].at[part], outs[array].at[part], out_sem.at[number]
        )

    def first():
        for route in routes:
            to_core(route, None, 0).start()
        launch(0)

    def second():
        land(0)
        launch(1)

    def third():
        land(1)
        launch(2)

    def fourth():
        land(2)

    def fifth():
        for route in routes:
            to_core(route, None, 0).wait_recv()
        for phase in range(3):
            for which in hops(phase):
                to_core(*which).wait_recv()
        if array < len(outs):
            out_copy().start()

    def finish():
        for route in routes:
            to_core(route, None, 0).wait_send()
        for phase in range(3):
            for which in hops(phase):
                hop(*which).wait_send()
                to_core(*which).wait_send()
        if array < len(outs):
            out_copy().wait()

    return [first, second, third, fourth, fifth, finish]


def erf(values):
    clipped = jnp.clip(values, -3.832506856900711, 3.832506856900711)
    square = clipped * clipped
    top = jnp.full_like(square, 0.00022905065861350646)
    for term in (
        0.0034082910107109506, 0.050955695062380861, 0.18520832239976145, 1.128379143519084,
    ):
        top = top * square + term
    bottom = jnp.full_like(square, -1.1791602954361697e-7)
    for term in (
        0.000023547966471313185, 0.0010179625278914885, 0.014070470171167667,
        0.11098505178285362, 0.49746925110067538, 1.0,
    ):
        bottom = bottom * square + term
    return clipped * top / bottom


def gelu_and_slope(hidden):
    chance = 0.5 + 0.5 * erf(hidden * (0.5**0.5))
    density = jnp.exp(-0.5 * hidden * hidden) * 0.3989422804014327
    return hidden * chance, chance + hidden * density


def norm_rows(inputs, gain_row, shift_row):
    average = jnp.mean(inputs, axis=-1, keepdims=True)
    centered = inputs - average
    variance = jnp.mean(centered * centered, axis=-1, keepdims=True)
    return centered * lax.rsqrt(variance + EPSILON) * gain_row + shift_row


def attention_pair(pair_number, refs):
    (
        row_ref, qkv_ref, vector_ref, table_ref, packed_ref, mask_ref, score_ref, probs_ref,
        query_ref, key_t_ref, value_ref, context_ref, context_t_ref,
    ) = refs
    length, width = row_ref.shape
    padded = packed_ref.shape[1]
    pair = 2 * width // H
    half = pair // 2
    scale = half ** (-0.5)
    at = pl.multiple_of(pair_number * pair, pair)
    mine = pl.ds(at, pair)
    row_in = row_ref[...]

    def project(part):
        columns = pl.ds(pl.multiple_of(part * width + at, pair), pair)
        return dot_plain(row_in, qkv_ref[:, columns])

    queries = ((project(0) + vector_ref[0:1, mine]).astype(jnp.bfloat16)) * jnp.bfloat16(scale)
    keys = project(1).astype(jnp.bfloat16)
    values = (project(2) + vector_ref[1:2, mine]).astype(jnp.bfloat16)
    query_ref[0:length, mine] = queries
    query_ref[length:, mine] = jnp.zeros((padded - length, pair), jnp.bfloat16)
    value_ref[:, mine] = values
    queries_t = jnp.concatenate(
        [queries.T, jnp.zeros((pair, padded - length), jnp.bfloat16)], axis=1
    )
    key_t_ref[mine, :] = keys.T
    values_t = values.T
    feature = lax.broadcasted_iota(jnp.int32, (pair, padded), 0)
    zero = jnp.zeros_like(queries_t)
    score_ref[0] = dot_plain(keys, jnp.where(feature < half, queries_t, zero))
    score_ref[1] = dot_plain(keys, jnp.where(feature < half, zero, queries_t))
    for column in range(0, padded, LANES):
        lanes = slice(column, column + LANES)
        rows = [table_ref[t, pair_number] for t in range(3)]
        tops = [jnp.full((8, LANES), 3.0 * MASK_FILL, jnp.float32) for side in range(2)]
        for start in range(0, length, 8):
            here = slice(start, start + 8)
            packed = packed_ref[here, lanes]
            sums = [None, None]
            for table in range(3):
                index = (packed >> (7 * table)) & (NB - 1)
                word = jnp.take_along_axis(rows[table], index, axis=1)
                for side, term in ((0, word >> 16), (1, (word << 16) >> 16)):
                    sums[side] = term if table == 0 else sums[side] + term
            mask = mask_ref[here, lanes]
            for side in range(2):
                scores = score_ref[side, here, lanes] + (
                    sums[side].astype(jnp.float32) * (1.0 / TABLE_STEP) + mask
                )
                score_ref[side, here, lanes] = scores
                tops[side] = jnp.maximum(tops[side], scores)
        for side in range(2):
            top = jnp.max(tops[side], axis=0, keepdims=True)
            exponent = jnp.exp(score_ref[side, :, lanes] - top)
            total = jnp.sum(exponent, axis=0, keepdims=True)
            probs_ref[side, :, lanes] = (exponent * (1.0 / total)).astype(jnp.bfloat16)
    context_t = jnp.concatenate(
        [
            dot_plain(values_t[side * half : (side + 1) * half], probs_ref[side])
            for side in range(2)
        ],
        axis=0,
    ).astype(jnp.bfloat16)
    context_t_ref[mine, :] = context_t
    context_ref[:, mine] = context_t.T[0:length]


class ForwardRefs(typing.NamedTuple):
    w_qkv: typing.Any
    w_out: typing.Any
    w_in: typing.Any
    w_down: typing.Any
    small: typing.Any
    row: typing.Any
    buckets: typing.Any
    segments_down: typing.Any
    segments_across: typing.Any
    full_qkv: typing.Any
    full_out: typing.Any
    full_in: typing.Any
    full_down: typing.Any
    probs: typing.Any
    context_t: typing.Any
    queries: typing.Any
    keys_t: typing.Any
    values: typing.Any
    first_sum: typing.Any
    first_low: typing.Any
    active_t: typing.Any
    slope: typing.Any
    second_sum: typing.Any
    vectors: typing.Any
    packed_t: typing.Any
    h_qkv: typing.Any
    h_out: typing.Any
    h_in: typing.Any
    h_down: typing.Any
    h_small: typing.Any
    s_row: typing.Any
    s_buckets: typing.Any
    s_packed: typing.Any
    s_mask: typing.Any
    s_score: typing.Any
    s_probs: typing.Any
    s_context: typing.Any
    s_context_t: typing.Any
    s_query: typing.Any
    s_key_t: typing.Any
    s_value: typing.Any
    s_first: typing.Any
    s_low: typing.Any
    s_active: typing.Any
    s_slope: typing.Any
    s_active_t: typing.Any
    s_second: typing.Any
    s_vectors: typing.Any
    s_hidden: typing.Any
    s_tables: typing.Any
    local_sem: typing.Any
    send: typing.Any
    recv: typing.Any
    out_sem: typing.Any
    probs_sem: typing.Any
    slope_sem: typing.Any
    active_sem: typing.Any
    store_sem: typing.Any


def forward_kernel(waves, starts, *refs):
    r = ForwardRefs(*refs)
    place, core = coordinates()
    shards = [r.w_qkv, r.w_out, r.w_in, r.w_down, r.small]
    full = [r.h_qkv, r.h_out, r.h_in, r.h_down, r.h_small]
    outs = [r.full_qkv, r.full_out, r.full_in, r.full_down]
    length, width = r.s_row.shape
    padded = r.s_packed.shape[1]
    own = [
        pltpu.make_async_copy(
            shards[i], full[i].at[place[0], place[1], place[2], core], r.local_sem.at[i]
        )
        for i in range(len(shards))
    ]
    own.append(pltpu.make_async_copy(r.row, r.s_row, r.local_sem.at[5]))
    own.append(pltpu.make_async_copy(r.buckets, r.s_buckets, r.local_sem.at[6]))
    for copy in own:
        copy.start()
    greet(place, core)
    steps = [
        gather_steps(wave, number, full, outs, r.send, r.recv, r.out_sem, place, core)
        for number, wave in enumerate(waves)
    ]
    for copy in own[:5]:
        copy.wait()
    events = []
    for number, (start, lag) in enumerate(starts):
        for step in range(STEPS):
            events.append((start + lag * step, number, step))
    events.sort()
    ready = max(e[0] for e in events if waves[e[1]][0] in (0, 4))
    first_in = max(e[0] for e in events if waves[e[1]][0] in (0, 4, 1))

    def communicate(low, high):
        for slot, number, step in events:
            if low <= slot < high:
                steps[number][step]()

    def prepare():
        own[6].wait()
        for table in range(3):
            part = r.s_buckets[table] << (7 * table)
            packed = part if table == 0 else packed | part
        flipped = packed.T
        r.s_packed[...] = jnp.concatenate(
            [flipped, jnp.zeros((length, padded - length), jnp.int32)], axis=1
        )
        down = lax.broadcasted_iota(jnp.int32, (length, padded), 0)
        across = lax.broadcasted_iota(jnp.int32, (length, padded), 1)
        same = (r.segments_down[...] >> 1) == r.segments_across[...]
        usable = ((r.segments_down[...] & 1) > 0) | (down == across)
        allowed = (same & usable) | (across >= length)
        r.s_mask[...] = jnp.where(allowed, 0.0, MASK_FILL)

    def spread():
        devices = DIMS[0] * DIMS[1] * DIMS[2] * 2
        piece = width // devices
        group = LANES // piece
        buckets_each = 3 * NB // devices
        tables = [jnp.zeros((H, LANES), jnp.float32) for t in range(3)]
        lane = lax.broadcasted_iota(jnp.int32, (H, LANES), 1)
        for device in range(devices):
            spot = (device // 8, (device // 4) % 2, (device // 2) % 2, device % 2)
            block = r.h_small[spot].astype(jnp.float32)
            mine = slice(device // group * LANES, (device // group + 1) * LANES)
            if device % group == 0:
                r.s_vectors[:, mine] = block[0:8]
            else:
                r.s_vectors[:, mine] = r.s_vectors[:, mine] + block[0:8]
            r.s_hidden[:, device * LANES : (device + 1) * LANES] = block[8:9]
            low, high = device * buckets_each, (device + 1) * buckets_each
            for table in range(low // NB, (high - 1) // NB + 1):
                inside = (lane >= low - table * NB) & (lane < high - table * NB)
                tables[table] = tables[table] + jnp.where(inside, block[16:32], 0.0)
        for table in range(3):
            fixed = jnp.round(tables[table] * TABLE_STEP).astype(jnp.int32)
            words = (fixed[0:8] << 16) | (fixed[8:16] & 0xFFFF)
            for pair in range(H // 2):
                r.s_tables[table, pair] = jnp.broadcast_to(words[pair : pair + 1], (8, LANES))

    communicate(0, 1)
    prepare()
    communicate(1, ready + 1)
    spread()
    own[5].wait()
    vectors = pltpu.make_async_copy(r.s_vectors, r.vectors, r.store_sem.at[0])
    vectors.start()
    qkv_view = r.h_qkv.reshape(width, 3 * width)

    def probs_copy(pair_number, slot):
        return pltpu.make_async_copy(
            r.s_probs.at[slot], r.probs.at[pl.ds(2 * pair_number, 2)],
            r.probs_sem.at[slot],
        )

    def one_pair(pair_number, carry):
        for number in range(H // 2):
            slot = ready + 1 + number
            if any(e[0] == slot for e in events):
                @pl.when(pair_number == number)
                def talk(slot=slot):
                    communicate(slot, slot + 1)

        slot = lax.rem(pair_number, 2)

        @pl.when(pair_number >= 2)
        def free():
            probs_copy(pair_number - 2, slot).wait()

        attention_pair(
            pair_number,
            (
                r.s_row, qkv_view, r.s_vectors, r.s_tables, r.s_packed,
                r.s_mask, r.s_score, r.s_probs.at[slot], r.s_query, r.s_key_t,
                r.s_value, r.s_context, r.s_context_t,
            ),
        )
        probs_copy(pair_number, slot).start()
        return carry

    pairs = H // 2
    lax.fori_loop(0, pairs, one_pair, 0)
    now = ready + 1 + pairs
    stores = [vectors]

    def store(scratch, out, number):
        made = pltpu.make_async_copy(scratch, out, r.store_sem.at[number])
        made.start()
        stores.append(made)

    store(r.s_context_t, r.context_t, 1)
    store(r.s_query, r.queries, 2)
    for part in range(padded // LANES):
        store(r.s_packed.at[:, part * LANES : (part + 1) * LANES], r.packed_t.at[part], 9 + part)
    store(r.s_key_t, r.keys_t, 3)
    store(r.s_value, r.values, 4)
    if first_in >= now:
        communicate(now, first_in + 1)
        now = first_in + 1
    out_view = r.h_out.reshape(width, width)
    tile = length // 3

    def one_out(number, carry):
        rows = pl.ds(pl.multiple_of(number * tile, tile), tile)
        first = (
            r.s_row[rows, :].astype(jnp.float32)
            + dot_plain(r.s_context[rows, :], out_view[...])
            + r.s_vectors[2:3, :]
        )
        r.s_first[rows, :] = first
        normed = norm_rows(first, r.s_vectors[6:7, :], r.s_vectors[4:5, :])
        r.s_low[rows, :] = normed.astype(jnp.bfloat16)
        r.s_second[rows, :] = normed + r.s_vectors[3:4, :]
        return carry

    lax.fori_loop(0, 3, one_out, 0)
    store(r.s_first, r.first_sum, 5)
    store(r.s_low, r.first_low, 6)
    hidden_units = r.s_active.shape[1]
    in_view = r.h_in.reshape(width, hidden_units)
    chunk = r.s_slope.shape[2]
    unit = r.active_t.shape[1]

    def slope_copy(number, slot):
        return pltpu.make_async_copy(
            r.s_slope.at[slot],
            r.slope.at[:, pl.ds(pl.multiple_of(number * chunk, chunk), chunk)],
            r.slope_sem.at[slot],
        )

    def active_copy(number, slot):
        return pltpu.make_async_copy(
            r.s_active_t.at[slot],
            r.active_t.at[pl.ds(number * (chunk // unit), chunk // unit)],
            r.active_sem.at[slot],
        )

    def one_in(number, carry):
        columns = pl.ds(pl.multiple_of(number * chunk, chunk), chunk)
        slot = lax.rem(number, 2)

        @pl.when(number >= 2)
        def free():
            slope_copy(number - 2, slot).wait()
            active_copy(number - 2, slot).wait()

        hidden = dot_plain(r.s_low[...], in_view[:, columns]) + r.s_hidden[:, columns]
        active, slope = gelu_and_slope(hidden)
        active_low = active.astype(jnp.bfloat16)
        r.s_active[:, columns] = active_low
        r.s_active_t[slot] = active_low.T.reshape(chunk // unit, unit, length)
        active_copy(number, slot).start()
        r.s_slope[slot] = slope.astype(jnp.bfloat16)
        slope_copy(number, slot).start()
        return carry

    in_waves = [(w[3][-1], number) for number, w in enumerate(waves) if w[0] == 2]
    done = 0
    for edge, number in in_waves:
        arrived = starts[number][0] + starts[number][1] * (STEPS - 1)
        if arrived >= now:
            communicate(now, arrived + 1)
            now = arrived + 1
        lax.fori_loop(done, edge // chunk, one_in, 0)
        done = edge // chunk
    last = events[-1][0]
    down_view = r.h_down.reshape(hidden_units, width)
    for number, wave in enumerate(waves):
        if wave[0] == 3:
            arrived = starts[number][0] + starts[number][1] * (STEPS - 1)
            if arrived >= now:
                communicate(now, arrived + 1)
                now = arrived + 1
            columns = slice(wave[3][0], wave[3][-1])
            r.s_second[:, columns] = r.s_second[:, columns] + dot_plain(
                r.s_active[...], down_view[:, columns]
            )
    store(r.s_second, r.second_sum, 8)
    for pair_number in (pairs - 2, pairs - 1):
        probs_copy(pair_number, pair_number % 2).wait()
    chunks = hidden_units // chunk
    for number in (chunks - 2, chunks - 1):
        slope_copy(number, number % 2).wait()
        active_copy(number, number % 2).wait()
    for wave_steps in steps:
        wave_steps[STEPS]()
    for made in stores:
        made.wait()


def forward_all(shards, small, row_in, buckets, segments, validity, waves, starts, collective):
    length, width = row_in.shape
    padded = -(-length // LANES) * LANES
    hidden_units = shards[2].shape[1]
    unit = shards[3].shape[0]
    chunk = 256
    routes = len(GATHER_ORDERS)
    hops = 2 * hops_before(GATHER_ORDERS[0], 3) + 1
    low = jnp.bfloat16
    shape = jax.ShapeDtypeStruct
    anywhere = pl.BlockSpec(memory_space=pl.ANY)
    in_vmem = pl.BlockSpec(memory_space=pltpu.VMEM)
    whole = [shape(DIMS + (2,) + shard.shape, shard.dtype) for shard in shards + [small]]
    outs = whole[:4] + [
        shape((H, length, padded), low),
        shape((width, padded), low),
        shape((padded, width), low),
        shape((width, length), low),
        shape((length, width), low),
        shape((length, width), jnp.float32),
        shape((length, width), low),
        shape((hidden_units // unit, unit, length), low),
        shape((length, hidden_units), low),
        shape((length, width), jnp.float32),
        shape((8, width), jnp.float32),
        shape((padded // LANES, length, LANES), jnp.int32),
    ]
    scratch = [pltpu.VMEM(one.shape, one.dtype) for one in whole] + [
        pltpu.VMEM((length, width), low),
        pltpu.VMEM((3, length, length), jnp.int32),
        pltpu.VMEM((length, padded), jnp.int32),
        pltpu.VMEM((length, padded), jnp.float32),
        pltpu.VMEM((2, length, padded), jnp.float32),
        pltpu.VMEM((2, 2, length, padded), low),
        pltpu.VMEM((length, width), low),
        pltpu.VMEM((width, padded), low),
        pltpu.VMEM((padded, width), low),
        pltpu.VMEM((width, length), low),
        pltpu.VMEM((length, width), low),
        pltpu.VMEM((length, width), jnp.float32),
        pltpu.VMEM((length, width), low),
        pltpu.VMEM((length, hidden_units), low),
        pltpu.VMEM((2, length, chunk), low),
        pltpu.VMEM((2, chunk // unit, unit, length), low),
        pltpu.VMEM((length, width), jnp.float32),
        pltpu.VMEM((8, width), jnp.float32),
        pltpu.VMEM((1, hidden_units), jnp.float32),
        pltpu.VMEM((3, H // 2, 8, LANES), jnp.int32),
        pltpu.SemaphoreType.DMA((7,)),
        pltpu.SemaphoreType.DMA((len(waves), routes, hops)),
        pltpu.SemaphoreType.DMA((len(waves), routes, hops)),
        pltpu.SemaphoreType.DMA((len(waves),)),
        pltpu.SemaphoreType.DMA((2,)),
        pltpu.SemaphoreType.DMA((2,)),
        pltpu.SemaphoreType.DMA((2,)),
        pltpu.SemaphoreType.DMA((9 + padded // LANES,)),
    ]
    across = jnp.pad(segments, (0, padded - length))[None, :]
    marks = segments * 2 + (validity > 0).astype(jnp.int32)
    return pl.pallas_call(
        functools.partial(forward_kernel, waves, starts),
        in_specs=[anywhere] * 7 + [in_vmem] * 2,
        out_specs=[anywhere] * len(outs),
        out_shape=outs,
        scratch_shapes=scratch,
        compiler_params=pltpu.CompilerParams(
            collective_id=collective, has_side_effects=True, vmem_limit_bytes=VMEM_BYTES
        ),
    )(*shards, small, row_in, buckets, marks[:, None], across)


def small_block(device, vec_bias, norm_gain, bias_hidden, rel_tables):
    piece = vec_bias.shape[1]
    group = LANES // piece
    lane = jnp.arange(LANES)
    tiled = jnp.tile(jnp.concatenate([vec_bias, norm_gain], axis=0), (1, group))
    placed = jnp.where(lane // piece == device % group, tiled, jnp.zeros_like(tiled))
    hidden = jnp.pad(bias_hidden[None, :], ((0, 7), (0, 0)))
    heads_first = rel_tables.reshape(-1, H).T
    buckets_each = heads_first.shape[1]
    wanted = (lane - device * buckets_each) % NB
    choose = (wanted[None, :] == jnp.arange(buckets_each)[:, None]).astype(jnp.bfloat16)
    tables = dot_plain(jnp.concatenate([heads_first[0::2], heads_first[1::2]], axis=0), choose)
    return jnp.concatenate([placed, hidden, tables.astype(jnp.bfloat16)], axis=0)


def reduce_orders():
    return [tuple(reversed(order)) for order in GATHER_ORDERS]


def axes_left(order, phase):
    return [axis for axis in range(3) if axis not in order[: phase + 1]]


def scatter_scratch(waves, dtypes):
    shapes = []
    for array, row, rows, bounds in waves:
        dtype = dtypes[array]
        block = DIMS + (rows, bounds[-1] - bounds[0])
        shapes += [pltpu.VMEM(block, dtype), pltpu.VMEM(block, dtype)]
        for route, order in enumerate(reduce_orders()):
            width = bounds[route + 1] - bounds[route]
            for phase in range(3 if width else 0):
                left = tuple(DIMS[axis] for axis in axes_left(order, phase))
                shapes.append(
                    pltpu.VMEM((DIMS[order[phase]] - 1,) + left + (rows, width), dtype)
                )
    return shapes


def scatter_steps(wave, number, source, out, scratch, own_sem, send, recv, place, core):
    array, row, rows, bounds = wave
    base = bounds[0]
    total = next(scratch)
    other = next(scratch)
    orders = reduce_orders()
    routes = [r for r in range(len(orders)) if bounds[r + 1] > bounds[r]]
    landing = {}
    for route in routes:
        for phase in range(3):
            landing[route, phase] = next(scratch)
    core_slot = hops_before(orders[0], 3)
    every = slice(None)

    def own_copy():
        return pltpu.make_async_copy(source.at[:, :, :, core], total, own_sem.at[number])

    def core_copy():
        return pltpu.make_async_remote_copy(
            source.at[:, :, :, 1 - core], other,
            send.at[number, 0, core_slot], recv.at[number, 0, core_slot],
            device_id=device_at(place, 1 - core), device_id_type=MESH,
        )

    def hop(route, phase, distance):
        order = orders[route]
        axis = order[phase]
        index = [every] * 3
        for done in order[:phase]:
            index[done] = place[done]
        index[axis] = lax.rem(place[axis] + distance, DIMS[axis])
        slot = hops_before(order, phase) + distance - 1
        return pltpu.make_async_remote_copy(
            total.at[
                index[0], index[1], index[2], :,
                pl.ds(bounds[route] - base, bounds[route + 1] - bounds[route]),
            ],
            landing[route, phase].at[distance - 1],
            send.at[number, route, slot], recv.at[number, route, slot],
            device_id=device_at(shifted(place, axis, distance), core), device_id_type=MESH,
        )

    def launch(phase):
        for route in routes:
            for distance in range(1, DIMS[orders[route][phase]]):
                hop(route, phase, distance).start()

    def land(phase):
        for route in routes:
            order = orders[route]
            axis = order[phase]
            for distance in range(1, DIMS[axis]):
                hop(route, phase, distance).wait_recv()
            left = axes_left(order, phase)
            columns = slice(bounds[route] - base, bounds[route + 1] - base)
            for spot in itertools.product(*[range(DIMS[a]) for a in left]):
                index = list(place)
                for a, value in zip(left, spot):
                    index[a] = value
                at = (index[0], index[1], index[2], every, columns)
                added = total[at].astype(jnp.float32)
                for distance in range(1, DIMS[axis]):
                    added += landing[route, phase][(distance - 1,) + spot].astype(jnp.float32)
                if phase == 2:
                    out[pl.ds(row, rows), bounds[route] : bounds[route + 1]] = added
                else:
                    total[at] = added.astype(total.dtype)

    def first():
        own_copy().start()
        core_copy().start()

    def second():
        own_copy().wait()
        core_copy().wait()

        def one_plane(plane, carry):
            for y, x in itertools.product(range(DIMS[1]), range(DIMS[2])):
                total[plane, y, x] = total[plane, y, x] + other[plane, y, x]
            return carry

        lax.fori_loop(0, DIMS[0], one_plane, 0)
        launch(0)

    def third():
        land(0)
        launch(1)

    def fourth():
        land(1)
        launch(2)

    def fifth():
        land(2)
        for route in routes:
            for phase in range(3):
                for distance in range(1, DIMS[orders[route][phase]]):
                    hop(route, phase, distance).wait_send()

    return [first, second, third, fourth, fifth]


SCATTER_AFTER = (0, 1, 4, 7, 10)


def step_runner(steps, starts):
    events = sorted(
        (start + SCATTER_AFTER[step], number, step)
        for number, start in enumerate(starts)
        for step in range(STEPS)
    )

    def communicate(slot):
        for when, number, step in events:
            if when == slot:
                steps[number][step]()

    return communicate, events[-1][0]


def store_blocks(target, product, rows):
    planes = product.shape[0] // rows
    for block in range(planes):
        spot = (block // 8, (block // 4) % 2, (block // 2) % 2, block % 2)
        target[spot] = product[block * rows : (block + 1) * rows].astype(target.dtype)


def fold_rows(values):
    total = values[0:8]
    for start in range(8, values.shape[0], 8):
        total = total + values[start : start + 8]
    return total


def norm_rows_backward(inputs, gain_row, upstream):
    average = jnp.mean(inputs, axis=-1, keepdims=True)
    centered = inputs - average
    spread = lax.rsqrt(jnp.mean(centered * centered, axis=-1, keepdims=True) + EPSILON)
    normed = centered * spread
    scaled = upstream * gain_row
    grad = spread * (
        scaled
        - jnp.mean(scaled, axis=-1, keepdims=True)
        - normed * jnp.mean(scaled * normed, axis=-1, keepdims=True)
    )
    return grad, normed


def attention_pair_backward(refs):
    (
        value_ref, context_grad_t_ref, context_grad_ref, query_ref, key_t_ref, probs_ref,
        grads_ref, score_grad_ref, prob_grad_ref, low_ref,
    ) = refs
    length, pair = value_ref.shape
    padded = context_grad_t_ref.shape[1]
    half = pair // 2
    scale = half ** (-0.5)
    feature = lax.broadcasted_iota(jnp.int32, (pair, padded), 0)
    upstream = context_grad_t_ref[...]
    zero = jnp.zeros_like(upstream)
    prob_grad_ref[0] = dot_plain(value_ref[...], jnp.where(feature < half, upstream, zero))
    prob_grad_ref[1] = dot_plain(value_ref[...], jnp.where(feature < half, zero, upstream))
    for part in range(padded // LANES):
        lanes = slice(part * LANES, (part + 1) * LANES)
        for side in range(2):
            probs = probs_ref[side, :, lanes].astype(jnp.float32)
            prob_grad = prob_grad_ref[side, :, lanes]
            inner = jnp.sum(probs * prob_grad, axis=0, keepdims=True)
            score_grad = probs * (prob_grad - inner)
            score_grad_ref[part, side] = score_grad
            low_ref[side, :, lanes] = score_grad.astype(jnp.bfloat16)
    grad_query_t = jnp.concatenate(
        [
            dot_plain(key_t_ref[side * half : (side + 1) * half, :], low_ref[side])
            for side in range(2)
        ],
        axis=0,
    )
    grads_ref[0] = (grad_query_t * scale).astype(jnp.bfloat16).T[0:length]
    first_half = lax.broadcasted_iota(jnp.int32, (length, pair), 1) < half
    grad_key = [dot_plain(low_ref[side], query_ref[...]) for side in range(2)]
    grads_ref[1] = jnp.where(first_half, grad_key[0], grad_key[1]).astype(jnp.bfloat16)
    grad_value = [dot_plain(probs_ref[side], context_grad_ref[...]) for side in range(2)]
    grads_ref[2] = jnp.where(first_half, grad_value[0], grad_value[1]).astype(jnp.bfloat16)


class FeedInputs(typing.NamedTuple):
    full_in: typing.Any
    full_down: typing.Any
    full_out: typing.Any
    second_sum: typing.Any
    cotangent: typing.Any
    first_sum: typing.Any
    first_low: typing.Any
    active_t: typing.Any
    slope: typing.Any
    probs: typing.Any
    queries: typing.Any
    keys_t: typing.Any
    values: typing.Any
    vectors: typing.Any


class FeedOutputs(typing.NamedTuple):
    shard_in: typing.Any
    shard_down: typing.Any
    output: typing.Any
    grad_first_sum: typing.Any
    branch_grad: typing.Any
    grad_mixed: typing.Any
    score_grad: typing.Any
    sums: typing.Any
    hidden_sums: typing.Any


class FeedRefs(typing.NamedTuple):
    full_in: typing.Any
    full_down: typing.Any
    full_out: typing.Any
    second_sum: typing.Any
    cotangent: typing.Any
    first_sum: typing.Any
    first_low: typing.Any
    active_t: typing.Any
    slope: typing.Any
    probs: typing.Any
    queries: typing.Any
    keys_t: typing.Any
    values: typing.Any
    vectors: typing.Any
    shard_in: typing.Any
    shard_down: typing.Any
    output: typing.Any
    grad_first_sum: typing.Any
    branch_grad: typing.Any
    grad_mixed: typing.Any
    score_grad: typing.Any
    sums: typing.Any
    hidden_sums: typing.Any
    own_sem: typing.Any
    send: typing.Any
    recv: typing.Any
    load_sem: typing.Any
    store_sem: typing.Any
    chunk_sem: typing.Any
    probs_sem: typing.Any
    grads_sem: typing.Any
    score_sem: typing.Any
    s_stage: typing.Any
    s_in: typing.Any
    s_down: typing.Any
    s_grad: typing.Any
    s_low: typing.Any
    s_vectors: typing.Any
    s_sums: typing.Any
    s_hidden: typing.Any
    s_branch: typing.Any


def feed_backward_kernel(waves, *refs):
    r = FeedRefs(*refs[: len(FeedRefs._fields)])
    buffers = refs[len(FeedRefs._fields) :]
    place, core = coordinates()
    length, width = r.s_low.shape
    hidden_units = r.s_hidden.shape[1]
    padded = r.probs.shape[2]
    chunk = 512
    down_waves = sum(wave[0] == 1 for wave in waves)
    loads = {}

    def load(source, target, number):
        made = pltpu.make_async_copy(source, target, r.load_sem.at[number])
        made.start()
        loads[number] = made

    load(r.vectors, r.s_vectors, 0)
    greet(place, core)
    counts = [len(scatter_scratch([wave], [jnp.bfloat16] * 2)) for wave in waves]
    offsets = [sum(counts[:number]) for number in range(len(waves))]

    def steps_of(number, stage):
        mine = iter(buffers[offsets[number] : offsets[number] + counts[number]])
        return scatter_steps(
            waves[number], number, stage,
            r.s_down if waves[number][0] == 1 else r.s_in, mine,
            r.own_sem, r.send, r.recv, place, core,
        )

    steps = [None] * len(waves)
    for number in range(len(waves)):
        steps[number] = steps_of(number, r.s_stage.at[number % 2])
    communicate, last = step_runner(steps, list(range(len(waves))))
    stores = []

    def store(scratch, out, number):
        made = pltpu.make_async_copy(scratch, out, r.store_sem.at[number])
        made.start()
        stores.append(made)
        return made

    loads[0].wait()
    gains = [r.s_vectors[6:7, :], r.s_vectors[7:8, :]]
    tile = 32
    nothing = jnp.zeros((8, width), jnp.float32)

    def feed_phase(
        s_second, s_cot, s_out, s_active, s_low_rows, s_low_t, s_wd, s_wi, s_slope
    ):
        load(r.second_sum, s_second, 2)
        load(r.cotangent, s_cot, 3)
        load(r.active_t, s_active, 4)
        load(r.first_low, s_low_rows, 5)

        def chunk_copies(number, slot):
            columns = pl.ds(pl.multiple_of(number * chunk, chunk), chunk)
            return [
                pltpu.make_async_copy(
                    r.full_down.at[columns], s_wd.at[slot], r.chunk_sem.at[slot, 0]
                ),
                pltpu.make_async_copy(
                    r.full_in.at[:, columns], s_wi.at[slot], r.chunk_sem.at[slot, 1]
                ),
                pltpu.make_async_copy(
                    r.slope.at[:, columns], s_slope.at[slot], r.chunk_sem.at[slot, 2]
                ),
            ]

        for copy in chunk_copies(0, 0):
            copy.start()
        loads[2].wait()
        loads[3].wait()

        def one_norm(number, carry):
            rows = pl.ds(pl.multiple_of(number * tile, tile), tile)
            upstream = s_cot[rows, :].astype(jnp.float32)
            grad, normed = norm_rows_backward(s_second[rows, :], gains[1], upstream)
            s_out[rows, :] = (normed * gains[1] + r.s_vectors[5:6, :]).astype(jnp.bfloat16)
            r.s_grad[rows, :] = grad
            low = grad.astype(jnp.bfloat16)
            r.s_low[rows, :] = low
            return (
                carry[0] + fold_rows(low.astype(jnp.float32)),
                carry[1] + fold_rows(upstream),
                carry[2] + fold_rows(upstream * normed),
            )

        sums = lax.fori_loop(0, length // tile, one_norm, (nothing, nothing, nothing))
        for row, total in zip((3, 5, 7), sums):
            r.s_sums[row : row + 1, :] = jnp.sum(total, axis=0, keepdims=True)
        store(s_out, r.output, 0)
        loads[4].wait()
        rows_each = waves[0][2]
        spots = list(itertools.product(range(DIMS[1]), range(DIMS[2]), range(2)))

        def to_stage(stage, plane, product, rows, columns):
            for block, spot in enumerate(spots):
                stage[(plane,) + spot + (slice(None), columns)] = product[
                    block * rows : (block + 1) * rows
                ].astype(jnp.bfloat16)

        for number in range(down_waves):
            first_row = waves[number][1]

            def one_down(plane, carry, number=number, first_row=first_row):
                group = pl.ds(plane * len(spots), len(spots))
                units = s_active[group, first_row : first_row + rows_each, :]
                product = dot_plain(
                    units.reshape(len(spots) * rows_each, length), r.s_low[...]
                )
                to_stage(r.s_stage.at[number % 2], plane, product, rows_each, slice(None))
                return carry

            lax.fori_loop(0, DIMS[0], one_down, 0)
            communicate(number)
        loads[5].wait()
        s_low_t[...] = s_low_rows[...].T
        in_rows = waves[down_waves][2]
        per_wave = (waves[down_waves][3][-1] - waves[down_waves][3][0]) // chunk
        for number in range(down_waves, len(waves)):

            def one_piece(piece, carry, number=number):
                index = (number - down_waves) * per_wave + piece
                slot = lax.rem(index, 2)

                @pl.when(index + 1 < hidden_units // chunk)
                def fetch():
                    for copy in chunk_copies(index + 1, 1 - slot):
                        copy.start()

                for copy in chunk_copies(index, slot):
                    copy.wait()
                hidden_grad = dot_last(r.s_low[...], s_wd[slot]) * s_slope[slot].astype(
                    jnp.float32
                )
                low = hidden_grad.astype(jnp.bfloat16)
                here = pl.ds(pl.multiple_of(index * chunk, chunk), chunk)
                r.s_hidden[:, here] = jnp.sum(
                    low.astype(jnp.float32), axis=0, keepdims=True
                )
                there = pl.ds(pl.multiple_of(piece * chunk, chunk), chunk)
                size = len(spots) * in_rows
                for plane in range(DIMS[0]):
                    product = dot_plain(s_low_t[plane * size : (plane + 1) * size, :], low)
                    to_stage(r.s_stage.at[number % 2], plane, product, in_rows, there)
                r.s_grad[...] = r.s_grad[...] + dot_last(low, s_wi[slot])
                return carry

            lax.fori_loop(0, per_wave, one_piece, 0)
            communicate(number)
        stores[0].wait()

    bf, full32 = jnp.bfloat16, jnp.float32
    pl.run_scoped(
        feed_phase,
        pltpu.VMEM((length, width), full32),
        pltpu.VMEM((length, width), bf),
        pltpu.VMEM((length, width), bf),
        pltpu.VMEM(r.active_t.shape, bf),
        pltpu.VMEM((length, width), bf),
        pltpu.VMEM((width, length), bf),
        pltpu.VMEM((2, chunk, width), bf),
        pltpu.VMEM((2, width, chunk), bf),
        pltpu.VMEM((2, length, chunk), bf),
    )
    now = len(waves)
    pairs = H // 2
    pair = width // pairs

    def norm_phase(s_first):
        load(r.first_sum, s_first, 1)
        loads[1].wait()

        def one_norm(number, carry):
            rows = pl.ds(pl.multiple_of(number * tile, tile), tile)
            upstream = r.s_grad[rows, :]
            grad, normed = norm_rows_backward(s_first[rows, :], gains[0], upstream)
            r.s_grad[rows, :] = grad
            low = grad.astype(jnp.bfloat16)
            r.s_branch[rows, :] = low
            return (
                carry[0] + fold_rows(low.astype(jnp.float32)),
                carry[1] + fold_rows(upstream),
                carry[2] + fold_rows(upstream * normed),
            )

        sums = lax.fori_loop(0, length // tile, one_norm, (nothing, nothing, nothing))
        for row, total in zip((2, 4, 6), sums):
            r.s_sums[row : row + 1, :] = jnp.sum(total, axis=0, keepdims=True)

    pl.run_scoped(norm_phase, pltpu.VMEM((length, width), full32))
    store(r.s_grad, r.grad_first_sum, 1)
    store(r.s_branch, r.branch_grad, 2)
    communicate(now)

    def attention_phase(
        s_wout, s_context_grad, s_context_grad_t, s_query, s_key_t, s_value, s_probs, s_prob_grad,
        s_low, s_score, s_grads,
    ):
        load(r.full_out, s_wout, 6)
        load(r.queries, s_query, 7)
        load(r.keys_t, s_key_t, 8)
        load(r.values, s_value, 9)

        def probs_copy(number, slot):
            return pltpu.make_async_copy(
                r.probs.at[pl.ds(2 * number, 2)], s_probs.at[slot], r.probs_sem.at[slot]
            )

        def score_copy(number, slot):
            return pltpu.make_async_copy(
                s_score.at[slot], r.score_grad.at[:, pl.ds(2 * number, 2)],
                r.score_sem.at[slot],
            )

        def grads_copy(number, slot, part):
            columns = pl.ds(pl.multiple_of(part * width + number * pair, pair), pair)
            return pltpu.make_async_copy(
                s_grads.at[slot, part], r.grad_mixed.at[:, columns],
                r.grads_sem.at[slot, part],
            )

        probs_copy(0, 0).start()
        loads[6].wait()
        s_context_grad[length:, :] = jnp.zeros((padded - length, width), bf)
        s_context_grad[0:length, :] = dot_last(r.s_branch[...], s_wout[...]).astype(bf)
        s_context_grad_t[...] = s_context_grad[...].T
        communicate(now + 1)
        for number in (7, 8, 9):
            loads[number].wait()

        def one_pair(number, carry):
            slot = lax.rem(number, 2)
            probs_copy(number, slot).wait()

            @pl.when(number + 1 < pairs)
            def fetch():
                probs_copy(number + 1, 1 - slot).start()

            @pl.when(number >= 2)
            def free():
                score_copy(number - 2, slot).wait()
                for part in range(3):
                    grads_copy(number - 2, slot, part).wait()

            mine = pl.ds(pl.multiple_of(number * pair, pair), pair)
            attention_pair_backward(
                (
                    s_value.at[:, mine], s_context_grad_t.at[mine], s_context_grad.at[:, mine],
                    s_query.at[:, mine], s_key_t.at[mine], s_probs.at[slot], s_grads.at[slot],
                    s_score.at[slot], s_prob_grad, s_low,
                )
            )
            for row, part in ((0, 0), (1, 2)):
                r.s_sums[row : row + 1, mine] = jnp.sum(
                    s_grads[slot, part].astype(full32), axis=0, keepdims=True
                )
            score_copy(number, slot).start()
            for part in range(3):
                grads_copy(number, slot, part).start()
            for turn in range(pairs):
                if now + 2 + turn <= last:
                    @pl.when(number == turn)
                    def talk(turn=turn):
                        communicate(now + 2 + turn)

            return carry

        lax.fori_loop(0, pairs, one_pair, 0)
        for number in (pairs - 2, pairs - 1):
            score_copy(number, number % 2).wait()
            for part in range(3):
                grads_copy(number, number % 2, part).wait()

    pl.run_scoped(
        attention_phase,
        pltpu.VMEM((width, width), bf),
        pltpu.VMEM((padded, width), bf),
        pltpu.VMEM((width, padded), bf),
        pltpu.VMEM((padded, width), bf),
        pltpu.VMEM((width, length), bf),
        pltpu.VMEM((length, width), bf),
        pltpu.VMEM((2, 2, length, padded), bf),
        pltpu.VMEM((2, length, padded), full32),
        pltpu.VMEM((2, length, padded), bf),
        pltpu.VMEM((2, padded // LANES, 2, length, LANES), full32),
        pltpu.VMEM((2, 3, length, pair), bf),
    )
    for slot in range(now + 2 + pairs, last + 1):
        communicate(slot)
    store(r.s_sums, r.sums, 3)
    store(r.s_hidden, r.hidden_sums, 4)
    store(r.s_in, r.shard_in, 5)
    store(r.s_down, r.shard_down, 6)
    for made in stores[1:]:
        made.wait()


def feed_backward(inputs, in_shape, down_shape, collective):
    length, width = inputs.first_sum.shape
    hidden_units = inputs.slope.shape[1]
    padded = inputs.probs.shape[2]
    bf, full32 = jnp.bfloat16, jnp.float32
    shape = jax.ShapeDtypeStruct
    anywhere = pl.BlockSpec(memory_space=pl.ANY)
    waves = weight_waves(1, down_shape[0], down_shape[1], in_shape[0], 8)
    waves += weight_waves(0, in_shape[0], in_shape[1], in_shape[0], 8)
    outs = [
        shape(in_shape, full32),
        shape(down_shape, full32),
        shape((length, width), bf),
        shape((length, width), full32),
        shape((length, width), bf),
        shape((length, 3 * width), bf),
        shape((padded // LANES, H, length, LANES), full32),
        shape((8, width), full32),
        shape((1, hidden_units), full32),
    ]
    sems = (len(waves), len(GATHER_ORDERS), hops_before(GATHER_ORDERS[0], 3) + 1)
    dma = pltpu.SemaphoreType.DMA
    scratch = [
        dma((len(waves),)), dma(sems), dma(sems), dma((10,)), dma((7,)), dma((2, 3)), dma((2,)),
        dma((2, 3)), dma((2,)),
        pltpu.VMEM((2,) + DIMS + (2, in_shape[0], waves[-1][3][-1] - waves[-1][3][0]), bf),
        pltpu.VMEM(in_shape, full32),
        pltpu.VMEM(down_shape, full32),
        pltpu.VMEM((length, width), full32),
        pltpu.VMEM((length, width), bf),
        pltpu.VMEM((8, width), full32),
        pltpu.VMEM((8, width), full32),
        pltpu.VMEM((1, hidden_units), full32),
        pltpu.VMEM((length, width), bf),
    ] + scatter_scratch(waves, [bf, bf])
    results = pl.pallas_call(
        functools.partial(feed_backward_kernel, waves),
        in_specs=[anywhere] * len(inputs),
        out_specs=[anywhere] * len(outs),
        out_shape=outs,
        scratch_shapes=scratch,
        compiler_params=pltpu.CompilerParams(
            collective_id=collective, has_side_effects=True, vmem_limit_bytes=VMEM_BYTES
        ),
    )(*inputs)
    return FeedOutputs(*results)


class LastInputs(typing.NamedTuple):
    row_in: typing.Any
    grad_mixed: typing.Any
    full_qkv: typing.Any
    context_t: typing.Any
    branch_grad: typing.Any
    score_grad: typing.Any
    packed_t: typing.Any
    grad_first_sum: typing.Any
    sums: typing.Any
    hidden_sums: typing.Any
    starts: typing.Any


class LastOutputs(typing.NamedTuple):
    shard_qkv: typing.Any
    shard_out: typing.Any
    shard_small: typing.Any
    grad_input: typing.Any


class LastRefs(typing.NamedTuple):
    row_in: typing.Any
    grad_mixed: typing.Any
    full_qkv: typing.Any
    context_t: typing.Any
    branch_grad: typing.Any
    score_grad: typing.Any
    packed_t: typing.Any
    grad_first_sum: typing.Any
    sums: typing.Any
    hidden_sums: typing.Any
    starts: typing.Any
    shard_qkv: typing.Any
    shard_out: typing.Any
    shard_small: typing.Any
    grad_input: typing.Any
    own_sem: typing.Any
    send: typing.Any
    recv: typing.Any
    load_sem: typing.Any
    store_sem: typing.Any
    score_sem: typing.Any
    s_stage: typing.Any
    s_small: typing.Any
    s_out_qkv: typing.Any
    s_out_out: typing.Any
    s_out_small: typing.Any
    s_row: typing.Any
    s_row_t: typing.Any
    s_mixed: typing.Any
    s_qkv: typing.Any
    s_context_t: typing.Any
    s_branch: typing.Any
    s_packed: typing.Any
    s_input: typing.Any
    s_sums: typing.Any
    s_hidden: typing.Any
    s_score: typing.Any
    s_work: typing.Any
    s_product: typing.Any


def last_backward_kernel(waves, *refs):
    r = LastRefs(*refs[: len(LastRefs._fields)])
    buffers = iter(refs[len(LastRefs._fields) :])
    place, core = coordinates()
    length, width = r.s_row.shape
    padded = r.s_packed.shape[0] * LANES
    rows_each = waves[0][2]
    loads = {}
    for number, (source, target) in enumerate(
        (
            (r.row_in, r.s_row), (r.grad_mixed, r.s_mixed), (r.context_t, r.s_context_t),
            (r.branch_grad, r.s_branch), (r.packed_t, r.s_packed), (r.full_qkv, r.s_qkv),
            (r.grad_first_sum, r.s_input), (r.sums, r.s_sums), (r.hidden_sums, r.s_hidden),
        )
    ):
        loads[number] = pltpu.make_async_copy(source, target, r.load_sem.at[number])
        loads[number].start()

    def score_copy(block, slot):
        rows = pl.ds(pl.multiple_of(block * GRAD_TILE, GRAD_TILE), GRAD_TILE)
        return pltpu.make_async_copy(
            r.score_grad.at[:, :, rows], r.s_score.at[slot], r.score_sem.at[slot]
        )

    score_copy(0, 0).start()
    greet(place, core)
    results = [r.s_out_qkv, r.s_out_out, r.s_out_small]
    main = len(waves) - 1
    steps = [
        scatter_steps(
            wave, number, r.s_small if number == main else r.s_stage.at[number % 2],
            results[wave[0]], buffers, r.own_sem, r.send, r.recv, place, core,
        )
        for number, wave in enumerate(waves)
    ]
    communicate, last = step_runner(steps, list(range(main)))
    spots = list(itertools.product(range(DIMS[1]), range(DIMS[2]), range(2)))
    size = len(spots) * rows_each
    loads[0].wait()
    r.s_row_t[...] = r.s_row[...].T
    loads[1].wait()
    for number in range(main):
        array, row, rows, bounds = waves[number]
        columns = slice(bounds[0], bounds[-1])
        if array == 1:
            loads[2].wait()
            loads[3].wait()

        def one_plane(plane, carry, array=array, number=number, columns=columns):
            units = pl.ds(pl.multiple_of(plane * size, size), size)
            if array == 0:
                product = dot_plain(r.s_row_t[units, :], r.s_mixed[:, columns])
            else:
                product = dot_plain(
                    r.s_context_t[units, 0:length], r.s_branch[:, columns]
                )
            for block, spot in enumerate(spots):
                r.s_stage[(number % 2, plane) + spot] = product[
                    block * rows_each : (block + 1) * rows_each
                ].astype(jnp.bfloat16)
            return carry

        lax.fori_loop(0, DIMS[0], one_plane, 0)
        communicate(number)
    loads[5].wait()
    loads[6].wait()
    strip = 256
    for start in range(0, width, strip):
        r.s_input[:, start : start + strip] = r.s_input[:, start : start + strip] + dot_last(
            r.s_mixed[...], r.s_qkv[start : start + strip, :]
        )
    stored = pltpu.make_async_copy(r.s_input, r.grad_input, r.store_sem.at[0])
    stored.start()
    communicate(main)
    loads[4].wait()
    parts = padded // LANES
    span = WINDOW_TILES * LANES
    levels = lax.broadcasted_iota(jnp.int32, (LOW_PARTS, span), 0).astype(jnp.bfloat16)
    one = jnp.ones((LOW_PARTS, span), jnp.bfloat16)
    no_one = jnp.zeros((LOW_PARTS, span), jnp.bfloat16)
    nothing = jnp.zeros((H, span), jnp.bfloat16)

    def window(tiles, turn):
        rolled = [pltpu.roll(one_tile, (LANES - turn) & (LANES - 1), 1) for one_tile in tiles]
        kept = lax.broadcasted_iota(jnp.int32, tiles[0].shape, 1) < LANES - turn
        return jnp.concatenate(
            [jnp.where(kept, here, after) for here, after in zip(rolled[:-1], rolled[1:])],
            axis=1,
        )

    def spread_digit(digit, rows):
        as_float = digit.astype(jnp.float32)
        low = jnp.concatenate([as_float, as_float], axis=0).astype(jnp.bfloat16)
        return jnp.concatenate([low] * (rows // 16), axis=0)

    r.s_product[...] = jnp.zeros(r.s_product.shape, jnp.float32)
    blocks = length // GRAD_TILE

    def one_block(block, carry):
        slot = lax.rem(block, 2)

        @pl.when(block + 1 < blocks)
        def fetch():
            score_copy(block + 1, 1 - slot).start()

        score_copy(block, slot).wait()
        r.s_work[...] = r.s_score[slot]
        flat = r.s_work.reshape(parts * H * GRAD_TILE, LANES)

        def one_group(group, total):
            lefts = []
            rights = []
            for offset in range(ROWS_AT_ONCE):
                row = group * ROWS_AT_ONCE + offset
                begin = r.starts[block * GRAD_TILE + row]
                tile = begin // LANES
                turn = lax.rem(begin, LANES)
                grads_parts = []
                packed_parts = []
                for part in range(WINDOW_TILES + 1):
                    which = lax.rem(tile + part, parts)
                    grads_parts.append(
                        flat[pl.ds(which * H * GRAD_TILE + row, H, stride=GRAD_TILE), :]
                    )
                    packed_parts.append(
                        jnp.broadcast_to(
                            r.s_packed[which, pl.ds(block * GRAD_TILE + row, 1), :], (8, LANES)
                        )
                    )
                grads = window(grads_parts, turn).astype(jnp.bfloat16)
                packed = window(packed_parts, turn)
                masked = []
                onehot = []
                for table in range(3):
                    high = spread_digit((packed >> (7 * table + 5)) & (HIGH_PARTS - 1), H)
                    for part in range(HIGH_PARTS):
                        masked.append(jnp.where(high == jnp.bfloat16(part), grads, nothing))
                    low = spread_digit((packed >> (7 * table)) & (LOW_PARTS - 1), LOW_PARTS)
                    onehot.append(jnp.where(low == levels, one, no_one))
                lefts.append(jnp.concatenate(masked, axis=0))
                rights.append(jnp.concatenate(onehot, axis=0))
            return total + dot_last(
                jnp.concatenate(lefts, axis=1), jnp.concatenate(rights, axis=1)
            )

        total = lax.fori_loop(
            0, GRAD_TILE // ROWS_AT_ONCE, one_group, jnp.zeros(r.s_product.shape, jnp.float32)
        )
        r.s_product[...] = r.s_product[...] + total
        for turn in range(blocks):
            if main + 1 + turn <= last:
                @pl.when(block == turn)
                def talk(turn=turn):
                    communicate(main + 1 + turn)

        return carry

    lax.fori_loop(0, blocks, one_block, 0)
    for slot in range(main + 1 + blocks, last + 1):
        communicate(slot)
    loads[7].wait()
    loads[8].wait()
    lane = lax.broadcasted_iota(jnp.int32, (H, LANES), 1)
    product = jnp.concatenate(
        [
            r.s_product[...],
            jnp.zeros((3 * HIGH_PARTS * H, LANES - 3 * LOW_PARTS), jnp.float32),
        ],
        axis=1,
    )
    tables = []
    for table in range(3):
        whole = jnp.zeros((H, LANES), jnp.float32)
        for part in range(HIGH_PARTS):
            start = (table * HIGH_PARTS + part) * H
            turned = pltpu.roll(
                product[start : start + H], ((part - table) * LOW_PARTS) % LANES, 1
            )
            inside = (lane >= part * LOW_PARTS) & (lane < (part + 1) * LOW_PARTS)
            whole = jnp.where(inside, turned, whole)
        tables.append(whole)
    devices = DIMS[0] * DIMS[1] * DIMS[2] * 2
    group = LANES // (width // devices)
    buckets_each = 3 * NB // devices
    empty = jnp.zeros((7, LANES), jnp.float32)
    for device in range(devices):
        spot = (device // 8, (device // 4) % 2, (device // 2) % 2, device % 2)
        columns = slice(device // group * LANES, (device // group + 1) * LANES)
        low = device * buckets_each
        table = low // NB
        mine = tables[table]
        if (low + buckets_each - 1) // NB > table:
            mine = jnp.where(lane >= low - table * NB, mine, tables[table + 1])
        hidden = r.s_hidden[:, device * LANES : (device + 1) * LANES]
        r.s_small[spot] = jnp.concatenate(
            [r.s_sums[:, columns], hidden, empty, mine], axis=0
        )
    for step in steps[main]:
        step()
    stores = [stored]
    for number, (source, target) in enumerate(
        ((r.s_out_qkv, r.shard_qkv), (r.s_out_out, r.shard_out), (r.s_out_small, r.shard_small))
    ):
        stores.append(
            pltpu.make_async_copy(source, target, r.store_sem.at[number + 1])
        )
        stores[-1].start()
    for made in stores:
        made.wait()


def last_backward(inputs, qkv_shape, out_shape, collective):
    length, width = inputs.row_in.shape
    hidden_units = inputs.hidden_sums.shape[1]
    padded = inputs.packed_t.shape[0] * LANES
    bf, full32 = jnp.bfloat16, jnp.float32
    shape = jax.ShapeDtypeStruct
    anywhere = pl.BlockSpec(memory_space=pl.ANY)
    small_rows = 16 + H
    waves = weight_waves(0, qkv_shape[0], qkv_shape[1], qkv_shape[0], 8)
    waves += weight_waves(1, out_shape[0], out_shape[1], out_shape[0], 8)
    waves.append(wave_of(2, 0, small_rows, 0, 1, 0, 0))
    outs = [
        shape(qkv_shape, full32),
        shape(out_shape, full32),
        shape((small_rows, LANES), full32),
        shape((length, width), full32),
    ]
    sems = (len(waves), len(GATHER_ORDERS), hops_before(GATHER_ORDERS[0], 3) + 1)
    dma = pltpu.SemaphoreType.DMA
    scratch = [
        dma((len(waves),)), dma(sems), dma(sems), dma((9,)), dma((4,)), dma((2,)),
        pltpu.VMEM((2,) + DIMS + (2, qkv_shape[0], waves[0][3][-1] - waves[0][3][0]), bf),
        pltpu.VMEM(DIMS + (2, small_rows, LANES), full32),
        pltpu.VMEM(qkv_shape, full32),
        pltpu.VMEM(out_shape, full32),
        pltpu.VMEM((small_rows, LANES), full32),
        pltpu.VMEM((length, width), bf),
        pltpu.VMEM((width, length), bf),
        pltpu.VMEM((length, 3 * width), bf),
        pltpu.VMEM((width, 3 * width), bf),
        pltpu.VMEM((width, padded), bf),
        pltpu.VMEM((length, width), bf),
        pltpu.VMEM((padded // LANES, length, LANES), jnp.int32),
        pltpu.VMEM((length, width), full32),
        pltpu.VMEM((8, width), full32),
        pltpu.VMEM((1, hidden_units), full32),
        pltpu.VMEM((2, padded // LANES, H, GRAD_TILE, LANES), full32),
        pltpu.VMEM((padded // LANES, H, GRAD_TILE, LANES), full32),
        pltpu.VMEM((3 * HIGH_PARTS * H, 3 * LOW_PARTS), full32),
    ] + scatter_scratch(waves, [bf, bf, full32])
    results = pl.pallas_call(
        functools.partial(last_backward_kernel, waves),
        in_specs=[anywhere] * (len(inputs) - 1) + [pl.BlockSpec(memory_space=pltpu.SMEM)],
        out_specs=[anywhere] * len(outs),
        out_shape=outs,
        scratch_shapes=scratch,
        compiler_params=pltpu.CompilerParams(
            collective_id=collective, has_side_effects=True, vmem_limit_bytes=VMEM_BYTES
        ),
    )(*inputs)
    return LastOutputs(*results)


def even_waves(array, shape, tiles, parts):
    return [
        wave_of(array, 0, shape[0], tile * LANES, *parts)
        for tile in range(0, shape[1] // LANES, tiles)
    ]


def split_wave(array, row, rows, column, tiles, turn):
    edge = tiles // 8
    one = (tiles - edge + turn) // 2
    return wave_of(array, row, rows, column, one, tiles - edge - one, edge)


def forward_plan(weights, small):
    w_qkv, w_out, w_in, w_down = weights
    waves = [wave_of(4, 0, small.shape[0], 0, 1, 0, 0)]
    waves += weight_waves(0, w_qkv.shape[0], w_qkv.shape[1], w_qkv.shape[0], 8)
    early = len(waves)
    waves += weight_waves(1, w_out.shape[0], w_out.shape[1], w_out.shape[0], 8)
    waves += weight_waves(2, w_in.shape[0], w_in.shape[1], w_in.shape[0], 8)
    waves += even_waves(3, w_down.shape, 2, (1, 1, 0))
    starts = [(number, 1) if number < early else (number - 1, LAG) for number in range(len(waves))]
    return waves, starts


def weight_waves(array, rows, columns, row_step, tile_step):
    waves = []
    tiles = columns // LANES
    for row in range(0, rows, row_step):
        for tile in range(0, tiles, tile_step):
            size = min(tile_step, tiles - tile)
            waves.append(
                split_wave(array, row, row_step, tile * LANES, size, (len(waves) + array) % 2)
            )
    return waves


def attention_forward_kernel(
    key_ref, query_ref, value_ref, packed_ref, table_ref, mask_ref, probs_ref, context_ref,
    score_ref,
):
    length = key_ref.shape[0]
    padded = packed_ref.shape[1]
    pair = query_ref.shape[0]
    half = pair // 2
    feature = lax.broadcasted_iota(jnp.int32, (pair, padded), 0)
    queries = query_ref[...]
    zero = jnp.zeros_like(queries)
    score_ref[0] = dot_plain(key_ref[...], jnp.where(feature < half, queries, zero))
    score_ref[1] = dot_plain(key_ref[...], jnp.where(feature < half, zero, queries))
    for column in range(0, padded, LANES):
        lanes = slice(column, column + LANES)
        rows = [jnp.broadcast_to(table_ref[t, 0], (8, LANES)) for t in range(3)]
        tops = [jnp.full((8, LANES), 3.0 * MASK_FILL, jnp.float32) for side in range(2)]
        for start in range(0, length, 8):
            here = slice(start, start + 8)
            packed = packed_ref[here, lanes]
            sums = [None, None]
            for table in range(3):
                index = (packed >> (7 * table)) & (NB - 1)
                word = jnp.take_along_axis(rows[table], index, axis=1)
                for side, term in ((0, word >> 16), (1, (word << 16) >> 16)):
                    sums[side] = term if table == 0 else sums[side] + term
            mask = mask_ref[here, lanes]
            for side in range(2):
                scores = score_ref[side, here, lanes] + (
                    sums[side].astype(jnp.float32) * (1.0 / TABLE_STEP) + mask
                )
                score_ref[side, here, lanes] = scores
                tops[side] = jnp.maximum(tops[side], scores)
        for side in range(2):
            top = jnp.max(tops[side], axis=0, keepdims=True)
            exponent = jnp.exp(score_ref[side, :, lanes] - top)
            total = jnp.sum(exponent, axis=0, keepdims=True)
            probs_ref[side, :, lanes] = (exponent * (1.0 / total)).astype(jnp.bfloat16)
    for side in range(2):
        mine = slice(side * half, (side + 1) * half)
        context_ref[mine, :] = dot_plain(value_ref[mine, :], probs_ref[side]).astype(jnp.bfloat16)


def attention_forward(keys, queries_t, values_t, packed, tables, mask):
    length, width = keys.shape
    padded = packed.shape[1]
    pairs = H // 2
    pair = width // pairs
    whole = pl.BlockSpec((length, padded), lambda p: (0, 0))
    return pl.pallas_call(
        attention_forward_kernel,
        grid=(pairs,),
        in_specs=[
            pl.BlockSpec((length, pair), lambda p: (0, p)),
            pl.BlockSpec((pair, padded), lambda p: (p, 0)),
            pl.BlockSpec((pair, length), lambda p: (p, 0)),
            whole,
            pl.BlockSpec((3, 1, 1, NB), lambda p: (0, p, 0, 0)),
            whole,
        ],
        out_specs=[
            pl.BlockSpec((2, length, padded), lambda p: (p, 0, 0)),
            pl.BlockSpec((pair, padded), lambda p: (p, 0)),
        ],
        out_shape=[
            jax.ShapeDtypeStruct((H, length, padded), jnp.bfloat16),
            jax.ShapeDtypeStruct((width, padded), jnp.bfloat16),
        ],
        scratch_shapes=[pltpu.VMEM((2, length, padded), jnp.float32)],
        compiler_params=pltpu.CompilerParams(vmem_limit_bytes=VMEM_BYTES),
    )(keys, queries_t, values_t, packed, tables, mask)


def attention_backward_kernel(
    value_ref, context_grad_t_ref, context_grad_ref, query_ref, key_t_ref, probs_ref,
    grad_query_ref, grad_key_ref, grad_value_ref, score_grad_ref, prob_grad_ref, low_ref,
):
    length = value_ref.shape[0]
    pair, padded = context_grad_t_ref.shape
    half = pair // 2
    scale = half ** (-0.5)
    feature = lax.broadcasted_iota(jnp.int32, (pair, padded), 0)
    upstream = context_grad_t_ref[...]
    zero = jnp.zeros_like(upstream)
    prob_grad_ref[0] = dot_plain(value_ref[...], jnp.where(feature < half, upstream, zero))
    prob_grad_ref[1] = dot_plain(value_ref[...], jnp.where(feature < half, zero, upstream))
    for part in range(padded // LANES):
        lanes = slice(part * LANES, (part + 1) * LANES)
        for side in range(2):
            probs = probs_ref[side, :, lanes].astype(jnp.float32)
            prob_grad = prob_grad_ref[side, :, lanes]
            inner = jnp.sum(probs * prob_grad, axis=0, keepdims=True)
            score_grad = probs * (prob_grad - inner)
            score_grad_ref[part, side] = score_grad
            low_ref[side, :, lanes] = score_grad.astype(jnp.bfloat16)
    for side in range(2):
        mine = slice(side * half, (side + 1) * half)
        grad_query_ref[mine, :] = (dot_plain(key_t_ref[mine, :], low_ref[side]) * scale).astype(
            jnp.bfloat16
        )
    first_half = lax.broadcasted_iota(jnp.int32, (length, pair), 1) < half
    grad_key = [dot_plain(low_ref[side], query_ref[...]) for side in range(2)]
    grad_key_ref[...] = jnp.where(first_half, grad_key[0], grad_key[1]).astype(jnp.bfloat16)
    grad_value = [dot_plain(probs_ref[side], context_grad_ref[...]) for side in range(2)]
    grad_value_ref[...] = jnp.where(first_half, grad_value[0], grad_value[1]).astype(jnp.bfloat16)


def attention_backward(values, context_grad_t, context_grad, queries, keys_t, probs):
    length, width = values.shape
    padded = probs.shape[2]
    pairs = H // 2
    pair = width // pairs
    natural = pl.BlockSpec((length, pair), lambda p: (0, p))
    longer = pl.BlockSpec((padded, pair), lambda p: (0, p))
    flipped = pl.BlockSpec((pair, padded), lambda p: (p, 0))
    return pl.pallas_call(
        attention_backward_kernel,
        grid=(pairs,),
        in_specs=[
            natural,
            flipped,
            longer,
            longer,
            pl.BlockSpec((pair, length), lambda p: (p, 0)),
            pl.BlockSpec((2, length, padded), lambda p: (p, 0, 0)),
        ],
        out_specs=[
            flipped,
            natural,
            natural,
            pl.BlockSpec((padded // LANES, 2, length, LANES), lambda p: (0, p, 0, 0)),
        ],
        out_shape=[
            jax.ShapeDtypeStruct((width, padded), jnp.bfloat16),
            jax.ShapeDtypeStruct((length, width), jnp.bfloat16),
            jax.ShapeDtypeStruct((length, width), jnp.bfloat16),
            jax.ShapeDtypeStruct((padded // LANES, H, length, LANES), jnp.float32),
        ],
        scratch_shapes=[
            pltpu.VMEM((2, length, padded), jnp.float32),
            pltpu.VMEM((2, length, padded), jnp.bfloat16),
        ],
        compiler_params=pltpu.CompilerParams(vmem_limit_bytes=VMEM_BYTES),
    )(values, context_grad_t, context_grad, queries, keys_t, probs)


def table_grad_kernel(digit_ref, score_grad_ref, out_ref):
    padded = score_grad_ref.shape[0] * LANES

    @pl.when(pl.program_id(0) == 0)
    def start():
        out_ref[...] = jnp.zeros_like(out_ref)

    levels = lax.broadcasted_iota(jnp.int32, (LOW_PARTS, padded), 0).astype(jnp.bfloat16)
    one = jnp.ones((LOW_PARTS, padded), jnp.bfloat16)
    no_one = jnp.zeros((LOW_PARTS, padded), jnp.bfloat16)
    nothing = jnp.zeros((H, padded), jnp.bfloat16)
    flat_ref = score_grad_ref.reshape(padded // LANES * H * GRAD_TILE, LANES)

    def one_group(group, total):
        for offset in range(4):
            row = group * 4 + offset
            grads = jnp.concatenate(
                [
                    flat_ref[pl.ds(part * H * GRAD_TILE + row, H, stride=GRAD_TILE), :]
                    for part in range(padded // LANES)
                ],
                axis=1,
            ).astype(jnp.bfloat16)
            masked = []
            onehot = []
            for table in range(3):
                high = jnp.broadcast_to(digit_ref[row, table : table + 1, :], (H, padded))
                for part in range(HIGH_PARTS):
                    masked.append(jnp.where(high == jnp.bfloat16(part), grads, nothing))
                low = jnp.broadcast_to(digit_ref[row, 3 + table : 4 + table, :], (LOW_PARTS, padded))
                onehot.append(jnp.where(low == levels, one, no_one))
            total = total + dot_last(jnp.concatenate(masked, axis=0), jnp.concatenate(onehot, axis=0))
        return total

    out_ref[...] += lax.fori_loop(
        0, GRAD_TILE // 4, one_group, jnp.zeros(out_ref.shape, jnp.float32)
    )


def table_grads(digits, score_grad):
    length = score_grad.shape[2]
    padded = score_grad.shape[0] * LANES
    shape = (3 * HIGH_PARTS * H, 3 * LOW_PARTS)
    products = pl.pallas_call(
        table_grad_kernel,
        grid=(length // GRAD_TILE,),
        in_specs=[
            pl.BlockSpec((GRAD_TILE, 6, padded), lambda i: (i, 0, 0)),
            pl.BlockSpec((padded // LANES, H, GRAD_TILE, LANES), lambda i: (0, 0, i, 0)),
        ],
        out_specs=pl.BlockSpec(shape, lambda i: (0, 0)),
        out_shape=jax.ShapeDtypeStruct(shape, jnp.float32),
        compiler_params=pltpu.CompilerParams(vmem_limit_bytes=VMEM_BYTES),
    )(digits, score_grad)
    split = products.reshape(3, HIGH_PARTS, H, 3, LOW_PARTS)
    return jnp.stack(
        [jnp.transpose(split[t, :, :, t, :], (0, 2, 1)).reshape(NB, H) for t in range(3)]
    )


def norm_backward(inputs, gain_row, upstream):
    average = jnp.mean(inputs, axis=-1, keepdims=True)
    centered = inputs - average
    spread = lax.rsqrt(jnp.mean(centered * centered, axis=-1, keepdims=True) + EPSILON)
    normed = centered * spread
    scaled = upstream * gain_row
    grad = spread * (
        scaled
        - jnp.mean(scaled, axis=-1, keepdims=True)
        - normed * jnp.mean(scaled * normed, axis=-1, keepdims=True)
    )
    return grad, jnp.sum(upstream * normed, axis=0), jnp.sum(upstream, axis=0)


def spread_small(everything, vec_bias, norm_gain, bias_hidden):
    devices = everything.shape[0]
    vec_size, gain_size = vec_bias.size, norm_gain.size
    vectors, gains, hidden, tables = jnp.split(
        everything, [vec_size, vec_size + gain_size, vec_size + gain_size + bias_hidden.size], axis=1
    )
    vectors = jnp.transpose(vectors.reshape(devices, vec_bias.shape[0], -1), (1, 0, 2))
    gains = jnp.transpose(gains.reshape(devices, norm_gain.shape[0], -1), (1, 0, 2))
    rows = jnp.concatenate(
        [vectors.reshape(vec_bias.shape[0], -1), gains.reshape(norm_gain.shape[0], -1)], axis=0
    )
    return rows.astype(jnp.float32), hidden.reshape(-1).astype(jnp.float32), tables.reshape(3, NB, H)


def forward_by_ops(
    weights, row_in, buckets, segments, validity, vec_bias, norm_gain, bias_hidden, rel_tables
):
    length, width = row_in.shape
    padded = -(-length // LANES) * LANES
    scale = (width // H) ** (-0.5)
    full = [lax.all_gather(weight, BOTH, axis=0, tiled=True) for weight in weights]
    small = jnp.concatenate(
        [vec_bias.reshape(-1), norm_gain.reshape(-1), bias_hidden, rel_tables]
    )
    everything = lax.all_gather(small, BOTH, axis=0, tiled=False)
    vectors, hidden_bias, tables = spread_small(everything, vec_bias, norm_gain, bias_hidden)
    wide = ((0, 0), (0, padded - length))
    flipped = jnp.swapaxes(buckets, 1, 2)
    packed = jnp.pad(flipped[0] | (flipped[1] << 7) | (flipped[2] << 14), wide)
    position = jnp.arange(length)
    allowed = (segments[:, None] == segments[None, :]) & (
        (validity[:, None] > 0) | (position[:, None] == position[None, :])
    )
    mask = jnp.pad(jnp.where(allowed, 0.0, MASK_FILL), wide)
    fixed = jnp.round(tables.astype(jnp.float32) * TABLE_STEP).astype(jnp.int32)
    pair_tables = (fixed[:, :, 0::2] << 16) | (fixed[:, :, 1::2] & 0xFFFF)
    pair_tables = jnp.transpose(pair_tables, (0, 2, 1))[:, :, None, :]
    mixed = dot_plain(row_in, full[0])
    queries = (mixed[:, :width] + vectors[0]).astype(jnp.bfloat16) * jnp.bfloat16(scale)
    keys = mixed[:, width : 2 * width].astype(jnp.bfloat16)
    values = (mixed[:, 2 * width :] + vectors[1]).astype(jnp.bfloat16)
    queries = jnp.pad(queries, ((0, padded - length), (0, 0)))
    probs, context_t = attention_forward(keys, queries.T, values.T, packed, pair_tables, mask)
    branch = dot_first(context_t[:, :length], full[1])
    first_sum = row_in.astype(jnp.float32) + branch + vectors[2]
    normed_first = layer_norm(first_sum, vectors[6], vectors[4])
    first_low = normed_first.astype(jnp.bfloat16)
    hidden = dot_plain(first_low, full[2]) + hidden_bias
    active, slope = gelu_and_slope(hidden)
    active = active.astype(jnp.bfloat16)
    second_sum = normed_first + dot_plain(active, full[3]) + vectors[3]
    return full + [
        probs, context_t, queries, keys.T, values, first_sum, first_low, active, slope,
        second_sum, vectors, packed,
    ]


class Kept(typing.NamedTuple):
    full_qkv: typing.Any
    full_out: typing.Any
    full_in: typing.Any
    full_down: typing.Any
    probs: typing.Any
    context_t: typing.Any
    queries: typing.Any
    keys_t: typing.Any
    values: typing.Any
    first_sum: typing.Any
    first_low: typing.Any
    active_t: typing.Any
    slope: typing.Any
    second_sum: typing.Any
    vectors: typing.Any
    packed_t: typing.Any


def body(
    own_kernels, block_input, cotangent, seg_ids, slot_valid, rel_buckets, w_qkv, w_out, w_in,
    w_down, vec_bias, norm_gain, bias_hidden, rel_tables,
):
    row_in = block_input[0]
    row_cot = cotangent[0].astype(jnp.float32)
    length, width = row_in.shape
    devices = lax.axis_size(BOTH)
    weights = [w_qkv, w_out, w_in, w_down]
    if own_kernels:
        device = lax.axis_index("dp") * 2 + lax.axis_index("fsdp")
        small = small_block(device, vec_bias, norm_gain, bias_hidden, rel_tables)
        waves, starts = forward_plan(weights, small)
        forward = forward_all(
            weights, small, row_in, rel_buckets[0], seg_ids[0], slot_valid[0], waves, starts, 1
        )
        forward = [whole.reshape(-1, whole.shape[-1]) for whole in forward[:4]] + list(forward[4:])
    else:
        forward = forward_by_ops(
            weights, row_in, rel_buckets[0], seg_ids[0], slot_valid[0], vec_bias, norm_gain,
            bias_hidden, rel_tables,
        )
    if own_kernels:
        kept = Kept(*forward)
        fed = feed_backward(
            FeedInputs(
                kept.full_in, kept.full_down, kept.full_out, kept.second_sum, cotangent[0],
                kept.first_sum, kept.first_low, kept.active_t, kept.slope, kept.probs,
                kept.queries, kept.keys_t, kept.values, kept.vectors,
            ),
            w_in.shape, w_down.shape, 2,
        )
        segments = seg_ids[0]
        starts = jnp.sum(segments[None, :] < segments[:, None], axis=1, dtype=jnp.int32)
        done = last_backward(
            LastInputs(
                row_in, fed.grad_mixed, kept.full_qkv, kept.context_t, fed.branch_grad,
                fed.score_grad, kept.packed_t, fed.grad_first_sum, fed.sums, fed.hidden_sums,
                starts,
            ),
            w_qkv.shape, w_out.shape, 3,
        )
        small = done.shard_small
        piece = vec_bias.shape[1]
        vec_rows = vec_bias.shape[0]
        sums = lax.dynamic_slice(
            small, (0, device % (LANES // piece) * piece), (8, piece)
        )
        buckets_each = rel_tables.shape[0] // H
        twice = jnp.concatenate([small[16:], small[16:]], axis=1)
        tables = lax.dynamic_slice(twice, (0, device * buckets_each % NB), (H, buckets_each))
        return (
            fed.output[None],
            done.grad_input[None],
            done.shard_qkv,
            done.shard_out,
            fed.shard_in,
            fed.shard_down,
            sums[:vec_rows],
            sums[vec_rows:],
            small[8],
            tables.T.reshape(-1),
        )
    (
        full_qkv, full_out, full_in, full_down, probs, context_t, queries, keys_t, values,
        first_sum, first_low, active, slope, second_sum, vectors, packed,
    ) = forward
    padded = packed.shape[1]
    gains = vectors[6:8]
    taller = ((0, padded - length), (0, 0))
    context_t = context_t[:, :length]
    digits = jnp.stack(
        [
            (packed >> (7 * t + shift)) & mask
            for shift, mask in ((5, HIGH_PARTS - 1), (0, LOW_PARTS - 1))
            for t in range(3)
        ],
        axis=1,
    ).astype(jnp.bfloat16)
    output = layer_norm(second_sum, gains[1], vectors[5]).astype(jnp.bfloat16)

    grad_second, grad_gain_two, grad_shift_two = norm_backward(second_sum, gains[1], row_cot)
    down_grad = grad_second.astype(jnp.bfloat16)
    grad_w_down = dot_first(active, down_grad).astype(jnp.bfloat16)
    hidden_grad = (dot_last(down_grad, full_down) * slope.astype(jnp.float32)).astype(jnp.bfloat16)
    grad_w_in = dot_first(first_low, hidden_grad).astype(jnp.bfloat16)
    grad_first = dot_last(hidden_grad, full_in) + grad_second
    grad_first_sum, grad_gain_one, grad_shift_one = norm_backward(first_sum, gains[0], grad_first)
    branch_grad = grad_first_sum.astype(jnp.bfloat16)
    grad_w_out = dot_plain(context_t, branch_grad).astype(jnp.bfloat16)
    context_grad = jnp.pad(dot_last(branch_grad, full_out).astype(jnp.bfloat16), taller)
    grad_queries_t, grad_keys, grad_values, score_grad = attention_backward(
        values, context_grad.T, context_grad, queries, keys_t, probs
    )
    grad_queries = grad_queries_t[:, :length].T
    grad_mixed = jnp.concatenate([grad_queries, grad_keys, grad_values], axis=1)
    grad_w_qkv = dot_first(row_in, grad_mixed).astype(jnp.bfloat16)
    grad_input = grad_first_sum + dot_last(grad_mixed, full_qkv)
    grad_tables = table_grads(digits, score_grad)

    grad_vectors = jnp.stack(
        [
            jnp.sum(grad_queries.astype(jnp.float32), axis=0),
            jnp.sum(grad_values.astype(jnp.float32), axis=0),
            jnp.sum(branch_grad.astype(jnp.float32), axis=0),
            jnp.sum(down_grad.astype(jnp.float32), axis=0),
            grad_shift_one,
            grad_shift_two,
        ]
    )
    grad_gains = jnp.stack([grad_gain_one, grad_gain_two])
    grad_hidden_bias = jnp.sum(hidden_grad.astype(jnp.float32), axis=0)

    def by_device(matrix):
        return jnp.transpose(matrix.reshape(matrix.shape[0], devices, -1), (1, 0, 2)).reshape(
            devices, -1
        )

    small_grads = jnp.concatenate(
        [
            by_device(grad_vectors),
            by_device(grad_gains),
            grad_hidden_bias.reshape(devices, -1),
            grad_tables.reshape(devices, -1),
        ],
        axis=1,
    )
    weight_grads = [grad_w_qkv, grad_w_out, grad_w_in, grad_w_down]
    shards = [
        lax.psum_scatter(
            grad.astype(jnp.float32), BOTH, scatter_dimension=0, tiled=True
        )
        for grad in weight_grads
    ]
    small_shard = lax.psum_scatter(small_grads, BOTH, scatter_dimension=0, tiled=True)[0]
    shard_vectors, shard_gains, shard_hidden, shard_tables = jnp.split(
        small_shard,
        [
            vec_bias.size,
            vec_bias.size + norm_gain.size,
            vec_bias.size + norm_gain.size + bias_hidden.size,
        ],
    )
    return (
        output[None],
        grad_input[None],
        shards[0],
        shards[1],
        shards[2],
        shards[3],
        shard_vectors.reshape(vec_bias.shape),
        shard_gains.reshape(norm_gain.shape),
        shard_hidden,
        shard_tables,
    )


def solution(mesh):
    rows = P(BOTH)
    columns = P(None, BOTH)
    in_specs = (rows,) * 9 + (columns, columns, rows, rows)
    out_specs = (rows,) * 6 + (columns, columns, rows, rows)
    chips = DIMS[0] * DIMS[1] * DIMS[2]
    own_kernels = mesh.shape["dp"] == chips and mesh.shape["fsdp"] == 2
    return jax.shard_map(
        functools.partial(body, own_kernels),
        mesh=mesh,
        in_specs=in_specs,
        out_specs=out_specs,
        check_vma=False,
    )
```

```python
import functools
import itertools
import typing

import jax
import jax.numpy as jnp
from jax import lax
from jax.experimental import pallas as pl
from jax.experimental.pallas import tpu as pltpu
from jax.sharding import PartitionSpec as P

H = 16
NB = 128
LANES = 128
EPSILON = 1e-05
MASK_FILL = -1e30
TABLE_STEP = 8192.0
VMEM_BYTES = 60 << 20
BOTH = ("dp", "fsdp")
MESH = pl.DeviceIdType.MESH
DIMS = (4, 2, 2)
GATHER_ORDERS = ((0, 2, 1), (0, 1, 2), (2, 1, 0))
STEPS = 5
LAG = 3
GRAD_TILE = 64
ROWS_AT_ONCE = 16
WINDOW_TILES = 3
HIGH_PARTS = 4
LOW_PARTS = NB // HIGH_PARTS


def dot_plain(left, right):
    return jnp.dot(left, right, preferred_element_type=jnp.float32)


def dot_first(left, right):
    return lax.dot_general(
        left, right, (((0,), (0,)), ((), ())), preferred_element_type=jnp.float32
    )


def dot_last(left, right):
    return lax.dot_general(
        left, right, (((1,), (1,)), ((), ())), preferred_element_type=jnp.float32
    )


def layer_norm(inputs, gain_row, shift_row):
    average = jnp.mean(inputs, axis=-1, keepdims=True)
    centered = inputs - average
    variance = jnp.mean(centered * centered, axis=-1, keepdims=True)
    return centered * lax.rsqrt(variance + EPSILON) * gain_row + shift_row


def gelu_exact(inputs):
    return jax.nn.gelu(inputs, approximate=False)


def coordinates():
    chip = lax.axis_index("dp")
    core = lax.axis_index("fsdp")
    planes, rows, columns = DIMS
    place = (
        chip // (rows * columns),
        lax.rem(chip // columns, rows),
        lax.rem(chip, columns),
    )
    return place, core


def device_at(place, core):
    return ((place[0] * DIMS[1] + place[1]) * DIMS[2] + place[2], core)


def shifted(place, axis, distance):
    moved = list(place)
    moved[axis] = lax.rem(moved[axis] + distance, DIMS[axis])
    return tuple(moved)


def greet(place, core):
    barrier = pltpu.get_barrier_semaphore()
    peers = [
        device_at(shifted(place, axis, distance), core)
        for axis in range(3)
        for distance in range(1, DIMS[axis])
    ]
    peers.append(device_at(place, 1 - core))
    for peer in peers:
        pl.semaphore_signal(barrier, inc=1, device_id=peer, device_id_type=MESH)
    pl.semaphore_wait(barrier, len(peers))


def schedule(waves, lag):
    events = []
    for wave in range(waves):
        for step in range(STEPS):
            events.append((wave + lag * step, wave, step))
    return [(wave, step) for slot, wave, step in sorted(events)]


def wave_of(array, row, rows, column, *tiles):
    bounds = [column]
    for count in tiles:
        bounds.append(bounds[-1] + count * LANES)
    return (array, row, rows, tuple(bounds))


def hops_before(order, phase):
    return sum(DIMS[axis] - 1 for axis in order[:phase])


def gather_steps(wave, number, full, outs, send, recv, out_sem, place, core):
    array, row, rows, bounds = wave
    whole = full[array]
    routes = [r for r in range(len(GATHER_ORDERS)) if bounds[r + 1] > bounds[r]]
    total_hops = hops_before(GATHER_ORDERS[0], 3)

    def copy(route, slot, index, target):
        part = whole.at[
            index[0], index[1], index[2], core,
            pl.ds(row, rows), pl.ds(bounds[route], bounds[route + 1] - bounds[route]),
        ]
        return pltpu.make_async_remote_copy(
            part, part, send.at[number, route, slot], recv.at[number, route, slot],
            device_id=target, device_id_type=MESH,
        )

    def to_core(route, phase, distance):
        if phase is None:
            return copy(route, total_hops, list(place), device_at(place, 1 - core))
        order = GATHER_ORDERS[route]
        axis = order[phase]
        index = list(place)
        for done in order[:phase]:
            index[done] = slice(None)
        index[axis] = lax.rem(place[axis] + DIMS[axis] - distance, DIMS[axis])
        slot = total_hops + hops_before(order, phase) + distance
        return copy(route, slot, index, device_at(place, 1 - core))

    def hop(route, phase, distance):
        order = GATHER_ORDERS[route]
        index = list(place)
        for axis in order[:phase]:
            index[axis] = slice(None)
        return copy(
            route, hops_before(order, phase) + distance - 1, index,
            device_at(shifted(place, order[phase], distance), core),
        )

    def hops(phase):
        return [
            (route, phase, distance)
            for route in routes
            for distance in range(1, DIMS[GATHER_ORDERS[route][phase]])
        ]

    def launch(phase):
        for which in hops(phase):
            hop(*which).start()

    def land(phase):
        for which in hops(phase):
            hop(*which).wait_recv()
            to_core(*which).start()

    def out_copy():
        part = (slice(None),) * 4 + (
            pl.ds(row, rows), pl.ds(bounds[0], bounds[-1] - bounds[0]),
        )
        return pltpu.make_async_copy(
            full[array].at[part], outs[array].at[part], out_sem.at[number]
        )

    def first():
        for route in routes:
            to_core(route, None, 0).start()
        launch(0)

    def second():
        land(0)
        launch(1)

    def third():
        land(1)
        launch(2)

    def fourth():
        land(2)

    def fifth():
        for route in routes:
            to_core(route, None, 0).wait_recv()
        for phase in range(3):
            for which in hops(phase):
                to_core(*which).wait_recv()
        if array < len(outs):
            out_copy().start()

    def finish():
        for route in routes:
            to_core(route, None, 0).wait_send()
        for phase in range(3):
            for which in hops(phase):
                hop(*which).wait_send()
                to_core(*which).wait_send()
        if array < len(outs):
            out_copy().wait()

    return [first, second, third, fourth, fifth, finish]


def erf(values):
    clipped = jnp.clip(values, -3.832506856900711, 3.832506856900711)
    square = clipped * clipped
    top = jnp.full_like(square, 0.00022905065861350646)
    for term in (
        0.0034082910107109506, 0.050955695062380861, 0.18520832239976145, 1.128379143519084,
    ):
        top = top * square + term
    bottom = jnp.full_like(square, -1.1791602954361697e-7)
    for term in (
        0.000023547966471313185, 0.0010179625278914885, 0.014070470171167667,
        0.11098505178285362, 0.49746925110067538, 1.0,
    ):
        bottom = bottom * square + term
    return clipped * top / bottom


def gelu_and_slope(hidden):
    chance = 0.5 + 0.5 * erf(hidden * (0.5**0.5))
    density = jnp.exp(-0.5 * hidden * hidden) * 0.3989422804014327
    return hidden * chance, chance + hidden * density


def norm_rows(inputs, gain_row, shift_row):
    average = jnp.mean(inputs, axis=-1, keepdims=True)
    centered = inputs - average
    variance = jnp.mean(centered * centered, axis=-1, keepdims=True)
    return centered * lax.rsqrt(variance + EPSILON) * gain_row + shift_row


def attention_pair(pair_number, refs):
    (
        row_ref, qkv_ref, vector_ref, table_ref, packed_ref, mask_ref, score_ref, probs_ref,
        query_ref, key_t_ref, value_ref, context_ref, context_t_ref,
    ) = refs
    length, width = row_ref.shape
    padded = packed_ref.shape[1]
    pair = 2 * width // H
    half = pair // 2
    scale = half ** (-0.5)
    at = pl.multiple_of(pair_number * pair, pair)
    mine = pl.ds(at, pair)
    row_in = row_ref[...]

    def project(part):
        columns = pl.ds(pl.multiple_of(part * width + at, pair), pair)
        return dot_plain(row_in, qkv_ref[:, columns])

    queries = ((project(0) + vector_ref[0:1, mine]).astype(jnp.bfloat16)) * jnp.bfloat16(scale)
    keys = project(1).astype(jnp.bfloat16)
    values = (project(2) + vector_ref[1:2, mine]).astype(jnp.bfloat16)
    query_ref[0:length, mine] = queries
    query_ref[length:, mine] = jnp.zeros((padded - length, pair), jnp.bfloat16)
    value_ref[:, mine] = values
    queries_t = jnp.concatenate(
        [queries.T, jnp.zeros((pair, padded - length), jnp.bfloat16)], axis=1
    )
    key_t_ref[mine, :] = keys.T
    values_t = values.T
    feature = lax.broadcasted_iota(jnp.int32, (pair, padded), 0)
    zero = jnp.zeros_like(queries_t)
    score_ref[0] = dot_plain(keys, jnp.where(feature < half, queries_t, zero))
    score_ref[1] = dot_plain(keys, jnp.where(feature < half, zero, queries_t))
    for column in range(0, padded, LANES):
        lanes = slice(column, column + LANES)
        rows = [table_ref[t, pair_number] for t in range(3)]
        tops = [jnp.full((8, LANES), 3.0 * MASK_FILL, jnp.float32) for side in range(2)]
        for start in range(0, length, 8):
            here = slice(start, start + 8)
            packed = packed_ref[here, lanes]
            sums = [None, None]
            for table in range(3):
                index = (packed >> (7 * table)) & (NB - 1)
                word = jnp.take_along_axis(rows[table], index, axis=1)
                for side, term in ((0, word >> 16), (1, (word << 16) >> 16)):
                    sums[side] = term if table == 0 else sums[side] + term
            mask = mask_ref[here, lanes]
            for side in range(2):
                scores = score_ref[side, here, lanes] + (
                    sums[side].astype(jnp.float32) * (1.0 / TABLE_STEP) + mask
                )
                score_ref[side, here, lanes] = scores
                tops[side] = jnp.maximum(tops[side], scores)
        for side in range(2):
            top = jnp.max(tops[side], axis=0, keepdims=True)
            exponent = jnp.exp(score_ref[side, :, lanes] - top)
            total = jnp.sum(exponent, axis=0, keepdims=True)
            probs_ref[side, :, lanes] = (exponent * (1.0 / total)).astype(jnp.bfloat16)
    context_t = jnp.concatenate(
        [
            dot_plain(values_t[side * half : (side + 1) * half], probs_ref[side])
            for side in range(2)
        ],
        axis=0,
    ).astype(jnp.bfloat16)
    context_t_ref[mine, :] = context_t
    context_ref[:, mine] = context_t.T[0:length]


class ForwardRefs(typing.NamedTuple):
    w_qkv: typing.Any
    w_out: typing.Any
    w_in: typing.Any
    w_down: typing.Any
    small: typing.Any
    row: typing.Any
    buckets: typing.Any
    segments_down: typing.Any
    segments_across: typing.Any
    full_qkv: typing.Any
    full_out: typing.Any
    full_in: typing.Any
    full_down: typing.Any
    probs: typing.Any
    context_t: typing.Any
    queries: typing.Any
    keys_t: typing.Any
    values: typing.Any
    first_sum: typing.Any
    first_low: typing.Any
    active_t: typing.Any
    slope: typing.Any
    second_sum: typing.Any
    vectors: typing.Any
    packed_t: typing.Any
    h_qkv: typing.Any
    h_out: typing.Any
    h_in: typing.Any
    h_down: typing.Any
    h_small: typing.Any
    s_row: typing.Any
    s_buckets: typing.Any
    s_packed: typing.Any
    s_mask: typing.Any
    s_score: typing.Any
    s_probs: typing.Any
    s_context: typing.Any
    s_context_t: typing.Any
    s_query: typing.Any
    s_key_t: typing.Any
    s_value: typing.Any
    s_first: typing.Any
    s_low: typing.Any
    s_active: typing.Any
    s_slope: typing.Any
    s_active_t: typing.Any
    s_second: typing.Any
    s_vectors: typing.Any
    s_hidden: typing.Any
    s_tables: typing.Any
    local_sem: typing.Any
    send: typing.Any
    recv: typing.Any
    out_sem: typing.Any
    probs_sem: typing.Any
    slope_sem: typing.Any
    active_sem: typing.Any
    store_sem: typing.Any


def forward_kernel(waves, starts, *refs):
    r = ForwardRefs(*refs)
    place, core = coordinates()
    shards = [r.w_qkv, r.w_out, r.w_in, r.w_down, r.small]
    full = [r.h_qkv, r.h_out, r.h_in, r.h_down, r.h_small]
    outs = [r.full_qkv, r.full_out, r.full_in, r.full_down]
    length, width = r.s_row.shape
    padded = r.s_packed.shape[1]
    own = [
        pltpu.make_async_copy(
            shards[i], full[i].at[place[0], place[1], place[2], core], r.local_sem.at[i]
        )
        for i in range(len(shards))
    ]
    own.append(pltpu.make_async_copy(r.row, r.s_row, r.local_sem.at[5]))
    own.append(pltpu.make_async_copy(r.buckets, r.s_buckets, r.local_sem.at[6]))
    for copy in own:
        copy.start()
    greet(place, core)
    steps = [
        gather_steps(wave, number, full, outs, r.send, r.recv, r.out_sem, place, core)
        for number, wave in enumerate(waves)
    ]
    for copy in own[:5]:
        copy.wait()
    events = []
    for number, (start, lag) in enumerate(starts):
        for step in range(STEPS):
            events.append((start + lag * step, number, step))
    events.sort()
    ready = max(e[0] for e in events if waves[e[1]][0] in (0, 4))
    first_in = max(e[0] for e in events if waves[e[1]][0] in (0, 4, 1))

    def communicate(low, high):
        for slot, number, step in events:
            if low <= slot < high:
                steps[number][step]()

    def prepare():
        own[6].wait()
        for table in range(3):
            part = r.s_buckets[table] << (7 * table)
            packed = part if table == 0 else packed | part
        flipped = packed.T
        r.s_packed[...] = jnp.concatenate(
            [flipped, jnp.zeros((length, padded - length), jnp.int32)], axis=1
        )
        down = lax.broadcasted_iota(jnp.int32, (length, padded), 0)
        across = lax.broadcasted_iota(jnp.int32, (length, padded), 1)
        same = (r.segments_down[...] >> 1) == r.segments_across[...]
        usable = ((r.segments_down[...] & 1) > 0) | (down == across)
        allowed = (same & usable) | (across >= length)
        r.s_mask[...] = jnp.where(allowed, 0.0, MASK_FILL)

    def spread():
        devices = DIMS[0] * DIMS[1] * DIMS[2] * 2
        piece = width // devices
        group = LANES // piece
        buckets_each = 3 * NB // devices
        tables = [jnp.zeros((H, LANES), jnp.float32) for t in range(3)]
        lane = lax.broadcasted_iota(jnp.int32, (H, LANES), 1)
        for device in range(devices):
            spot = (device // 8, (device // 4) % 2, (device // 2) % 2, device % 2)
            block = r.h_small[spot].astype(jnp.float32)
            mine = slice(device // group * LANES, (device // group + 1) * LANES)
            if device % group == 0:
                r.s_vectors[:, mine] = block[0:8]
            else:
                r.s_vectors[:, mine] = r.s_vectors[:, mine] + block[0:8]
            r.s_hidden[:, device * LANES : (device + 1) * LANES] = block[8:9]
            low, high = device * buckets_each, (device + 1) * buckets_each
            for table in range(low // NB, (high - 1) // NB + 1):
                inside = (lane >= low - table * NB) & (lane < high - table * NB)
                tables[table] = tables[table] + jnp.where(inside, block[16:32], 0.0)
        for table in range(3):
            fixed = jnp.round(tables[table] * TABLE_STEP).astype(jnp.int32)
            words = (fixed[0:8] << 16) | (fixed[8:16] & 0xFFFF)
            for pair in range(H // 2):
                r.s_tables[table, pair] = jnp.broadcast_to(words[pair : pair + 1], (8, LANES))

    communicate(0, 1)
    prepare()
    communicate(1, ready + 1)
    spread()
    own[5].wait()
    vectors = pltpu.make_async_copy(r.s_vectors, r.vectors, r.store_sem.at[0])
    vectors.start()
    qkv_view = r.h_qkv.reshape(width, 3 * width)

    def probs_copy(pair_number, slot):
        return pltpu.make_async_copy(
            r.s_probs.at[slot], r.probs.at[pl.ds(2 * pair_number, 2)],
            r.probs_sem.at[slot],
        )

    def one_pair(pair_number, carry):
        for number in range(H // 2):
            slot = ready + 1 + number
            if any(e[0] == slot for e in events):
                @pl.when(pair_number == number)
                def talk(slot=slot):
                    communicate(slot, slot + 1)

        slot = lax.rem(pair_number, 2)

        @pl.when(pair_number >= 2)
        def free():
            probs_copy(pair_number - 2, slot).wait()

        attention_pair(
            pair_number,
            (
                r.s_row, qkv_view, r.s_vectors, r.s_tables, r.s_packed,
                r.s_mask, r.s_score, r.s_probs.at[slot], r.s_query, r.s_key_t,
                r.s_value, r.s_context, r.s_context_t,
            ),
        )
        probs_copy(pair_number, slot).start()
        return carry

    pairs = H // 2
    lax.fori_loop(0, pairs, one_pair, 0)
    now = ready + 1 + pairs
    stores = [vectors]

    def store(scratch, out, number):
        made = pltpu.make_async_copy(scratch, out, r.store_sem.at[number])
        made.start()
        stores.append(made)

    store(r.s_context_t, r.context_t, 1)
    store(r.s_query, r.queries, 2)
    for part in range(padded // LANES):
        store(r.s_packed.at[:, part * LANES : (part + 1) * LANES], r.packed_t.at[part], 9 + part)
    store(r.s_key_t, r.keys_t, 3)
    store(r.s_value, r.values, 4)
    if first_in >= now:
        communicate(now, first_in + 1)
        now = first_in + 1
    out_view = r.h_out.reshape(width, width)
    tile = length // 3

    def one_out(number, carry):
        rows = pl.ds(pl.multiple_of(number * tile, tile), tile)
        first = (
            r.s_row[rows, :].astype(jnp.float32)
            + dot_plain(r.s_context[rows, :], out_view[...])
            + r.s_vectors[2:3, :]
        )
        r.s_first[rows, :] = first
        normed = norm_rows(first, r.s_vectors[6:7, :], r.s_vectors[4:5, :])
        r.s_low[rows, :] = normed.astype(jnp.bfloat16)
        r.s_second[rows, :] = normed + r.s_vectors[3:4, :]
        return carry

    lax.fori_loop(0, 3, one_out, 0)
    store(r.s_first, r.first_sum, 5)
    store(r.s_low, r.first_low, 6)
    hidden_units = r.s_active.shape[1]
    in_view = r.h_in.reshape(width, hidden_units)
    chunk = r.s_slope.shape[2]
    unit = r.active_t.shape[1]

    def slope_copy(number, slot):
        return pltpu.make_async_copy(
            r.s_slope.at[slot],
            r.slope.at[:, pl.ds(pl.multiple_of(number * chunk, chunk), chunk)],
            r.slope_sem.at[slot],
        )

    def active_copy(number, slot):
        return pltpu.make_async_copy(
            r.s_active_t.at[slot],
            r.active_t.at[pl.ds(number * (chunk // unit), chunk // unit)],
            r.active_sem.at[slot],
        )

    def one_in(number, carry):
        columns = pl.ds(pl.multiple_of(number * chunk, chunk), chunk)
        slot = lax.rem(number, 2)

        @pl.when(number >= 2)
        def free():
            slope_copy(number - 2, slot).wait()
            active_copy(number - 2, slot).wait()

        hidden = dot_plain(r.s_low[...], in_view[:, columns]) + r.s_hidden[:, columns]
        active, slope = gelu_and_slope(hidden)
        active_low = active.astype(jnp.bfloat16)
        r.s_active[:, columns] = active_low
        r.s_active_t[slot] = active_low.T.reshape(chunk // unit, unit, length)
        active_copy(number, slot).start()
        r.s_slope[slot] = slope.astype(jnp.bfloat16)
        slope_copy(number, slot).start()
        return carry

    in_waves = [(w[3][-1], number) for number, w in enumerate(waves) if w[0] == 2]
    done = 0
    for edge, number in in_waves:
        arrived = starts[number][0] + starts[number][1] * (STEPS - 1)
        if arrived >= now:
            communicate(now, arrived + 1)
            now = arrived + 1
        lax.fori_loop(done, edge // chunk, one_in, 0)
        done = edge // chunk
    last = events[-1][0]
    down_view = r.h_down.reshape(hidden_units, width)
    for number, wave in enumerate(waves):
        if wave[0] == 3:
            arrived = starts[number][0] + starts[number][1] * (STEPS - 1)
            if arrived >= now:
                communicate(now, arrived + 1)
                now = arrived + 1
            columns = slice(wave[3][0], wave[3][-1])
            r.s_second[:, columns] = r.s_second[:, columns] + dot_plain(
                r.s_active[...], down_view[:, columns]
            )
    store(r.s_second, r.second_sum, 8)
    for pair_number in (pairs - 2, pairs - 1):
        probs_copy(pair_number, pair_number % 2).wait()
    chunks = hidden_units // chunk
    for number in (chunks - 2, chunks - 1):
        slope_copy(number, number % 2).wait()
        active_copy(number, number % 2).wait()
    for wave_steps in steps:
        wave_steps[STEPS]()
    for made in stores:
        made.wait()


def forward_all(shards, small, row_in, buckets, segments, validity, waves, starts, collective):
    length, width = row_in.shape
    padded = -(-length // LANES) * LANES
    hidden_units = shards[2].shape[1]
    unit = shards[3].shape[0]
    chunk = 256
    routes = len(GATHER_ORDERS)
    hops = 2 * hops_before(GATHER_ORDERS[0], 3) + 1
    low = jnp.bfloat16
    shape = jax.ShapeDtypeStruct
    anywhere = pl.BlockSpec(memory_space=pl.ANY)
    in_vmem = pl.BlockSpec(memory_space=pltpu.VMEM)
    whole = [shape(DIMS + (2,) + shard.shape, shard.dtype) for shard in shards + [small]]
    outs = whole[:4] + [
        shape((H, length, padded), low),
        shape((width, padded), low),
        shape((padded, width), low),
        shape((width, length), low),
        shape((length, width), low),
        shape((length, width), jnp.float32),
        shape((length, width), low),
        shape((hidden_units // unit, unit, length), low),
        shape((length, hidden_units), low),
        shape((length, width), jnp.float32),
        shape((8, width), jnp.float32),
        shape((padded // LANES, length, LANES), jnp.int32),
    ]
    scratch = [pltpu.VMEM(one.shape, one.dtype) for one in whole] + [
        pltpu.VMEM((length, width), low),
        pltpu.VMEM((3, length, length), jnp.int32),
        pltpu.VMEM((length, padded), jnp.int32),
        pltpu.VMEM((length, padded), jnp.float32),
        pltpu.VMEM((2, length, padded), jnp.float32),
        pltpu.VMEM((2, 2, length, padded), low),
        pltpu.VMEM((length, width), low),
        pltpu.VMEM((width, padded), low),
        pltpu.VMEM((padded, width), low),
        pltpu.VMEM((width, length), low),
        pltpu.VMEM((length, width), low),
        pltpu.VMEM((length, width), jnp.float32),
        pltpu.VMEM((length, width), low),
        pltpu.VMEM((length, hidden_units), low),
        pltpu.VMEM((2, length, chunk), low),
        pltpu.VMEM((2, chunk // unit, unit, length), low),
        pltpu.VMEM((length, width), jnp.float32),
        pltpu.VMEM((8, width), jnp.float32),
        pltpu.VMEM((1, hidden_units), jnp.float32),
        pltpu.VMEM((3, H // 2, 8, LANES), jnp.int32),
        pltpu.SemaphoreType.DMA((7,)),
        pltpu.SemaphoreType.DMA((len(waves), routes, hops)),
        pltpu.SemaphoreType.DMA((len(waves), routes, hops)),
        pltpu.SemaphoreType.DMA((len(waves),)),
        pltpu.SemaphoreType.DMA((2,)),
        pltpu.SemaphoreType.DMA((2,)),
        pltpu.SemaphoreType.DMA((2,)),
        pltpu.SemaphoreType.DMA((9 + padded // LANES,)),
    ]
    across = jnp.pad(segments, (0, padded - length))[None, :]
    marks = segments * 2 + (validity > 0).astype(jnp.int32)
    return pl.pallas_call(
        functools.partial(forward_kernel, waves, starts),
        in_specs=[anywhere] * 7 + [in_vmem] * 2,
        out_specs=[anywhere] * len(outs),
        out_shape=outs,
        scratch_shapes=scratch,
        compiler_params=pltpu.CompilerParams(
            collective_id=collective, has_side_effects=True, vmem_limit_bytes=VMEM_BYTES
        ),
    )(*shards, small, row_in, buckets, marks[:, None], across)


def small_block(device, vec_bias, norm_gain, bias_hidden, rel_tables):
    piece = vec_bias.shape[1]
    group = LANES // piece
    lane = jnp.arange(LANES)
    tiled = jnp.tile(jnp.concatenate([vec_bias, norm_gain], axis=0), (1, group))
    placed = jnp.where(lane // piece == device % group, tiled, jnp.zeros_like(tiled))
    hidden = jnp.pad(bias_hidden[None, :], ((0, 7), (0, 0)))
    heads_first = rel_tables.reshape(-1, H).T
    buckets_each = heads_first.shape[1]
    wanted = (lane - device * buckets_each) % NB
    choose = (wanted[None, :] == jnp.arange(buckets_each)[:, None]).astype(jnp.bfloat16)
    tables = dot_plain(jnp.concatenate([heads_first[0::2], heads_first[1::2]], axis=0), choose)
    return jnp.concatenate([placed, hidden, tables.astype(jnp.bfloat16)], axis=0)


def reduce_orders():
    return [tuple(reversed(order)) for order in GATHER_ORDERS]


def axes_left(order, phase):
    return [axis for axis in range(3) if axis not in order[: phase + 1]]


def scatter_scratch(waves, dtypes):
    shapes = []
    for array, row, rows, bounds in waves:
        dtype = dtypes[array]
        block = DIMS + (rows, bounds[-1] - bounds[0])
        shapes += [pltpu.VMEM(block, dtype), pltpu.VMEM(block, dtype)]
        for route, order in enumerate(reduce_orders()):
            width = bounds[route + 1] - bounds[route]
            for phase in range(3 if width else 0):
                left = tuple(DIMS[axis] for axis in axes_left(order, phase))
                shapes.append(
                    pltpu.VMEM((DIMS[order[phase]] - 1,) + left + (rows, width), dtype)
                )
    return shapes


def scatter_steps(wave, number, source, out, scratch, own_sem, send, recv, place, core):
    array, row, rows, bounds = wave
    base = bounds[0]
    total = next(scratch)
    other = next(scratch)
    orders = reduce_orders()
    routes = [r for r in range(len(orders)) if bounds[r + 1] > bounds[r]]
    landing = {}
    for route in routes:
        for phase in range(3):
            landing[route, phase] = next(scratch)
    core_slot = hops_before(orders[0], 3)
    every = slice(None)

    def own_copy():
        return pltpu.make_async_copy(source.at[:, :, :, core], total, own_sem.at[number])

    def core_copy():
        return pltpu.make_async_remote_copy(
            source.at[:, :, :, 1 - core], other,
            send.at[number, 0, core_slot], recv.at[number, 0, core_slot],
            device_id=device_at(place, 1 - core), device_id_type=MESH,
        )

    def hop(route, phase, distance):
        order = orders[route]
        axis = order[phase]
        index = [every] * 3
        for done in order[:phase]:
            index[done] = place[done]
        index[axis] = lax.rem(place[axis] + distance, DIMS[axis])
        slot = hops_before(order, phase) + distance - 1
        return pltpu.make_async_remote_copy(
            total.at[
                index[0], index[1], index[2], :,
                pl.ds(bounds[route] - base, bounds[route + 1] - bounds[route]),
            ],
            landing[route, phase].at[distance - 1],
            send.at[number, route, slot], recv.at[number, route, slot],
            device_id=device_at(shifted(place, axis, distance), core), device_id_type=MESH,
        )

    def launch(phase):
        for route in routes:
            for distance in range(1, DIMS[orders[route][phase]]):
                hop(route, phase, distance).start()

    def land(phase):
        for route in routes:
            order = orders[route]
            axis = order[phase]
            for distance in range(1, DIMS[axis]):
                hop(route, phase, distance).wait_recv()
            left = axes_left(order, phase)
            columns = slice(bounds[route] - base, bounds[route + 1] - base)
            for spot in itertools.product(*[range(DIMS[a]) for a in left]):
                index = list(place)
                for a, value in zip(left, spot):
                    index[a] = value
                at = (index[0], index[1], index[2], every, columns)
                added = total[at].astype(jnp.float32)
                for distance in range(1, DIMS[axis]):
                    added += landing[route, phase][(distance - 1,) + spot].astype(jnp.float32)
                if phase == 2:
                    out[pl.ds(row, rows), bounds[route] : bounds[route + 1]] = added
                else:
                    total[at] = added.astype(total.dtype)

    def first():
        own_copy().start()
        core_copy().start()

    def second():
        own_copy().wait()
        core_copy().wait()

        def one_plane(plane, carry):
            for y, x in itertools.product(range(DIMS[1]), range(DIMS[2])):
                total[plane, y, x] = total[plane, y, x] + other[plane, y, x]
            return carry

        lax.fori_loop(0, DIMS[0], one_plane, 0)
        launch(0)

    def third():
        land(0)
        launch(1)

    def fourth():
        land(1)
        launch(2)

    def fifth():
        land(2)
        for route in routes:
            for phase in range(3):
                for distance in range(1, DIMS[orders[route][phase]]):
                    hop(route, phase, distance).wait_send()

    return [first, second, third, fourth, fifth]


SCATTER_AFTER = (0, 1, 4, 7, 10)


def step_runner(steps, starts):
    events = sorted(
        (start + SCATTER_AFTER[step], number, step)
        for number, start in enumerate(starts)
        for step in range(STEPS)
    )

    def communicate(slot):
        for when, number, step in events:
            if when == slot:
                steps[number][step]()

    return communicate, events[-1][0]


def store_blocks(target, product, rows):
    planes = product.shape[0] // rows
    for block in range(planes):
        spot = (block // 8, (block // 4) % 2, (block // 2) % 2, block % 2)
        target[spot] = product[block * rows : (block + 1) * rows].astype(target.dtype)


def fold_rows(values):
    total = values[0:8]
    for start in range(8, values.shape[0], 8):
        total = total + values[start : start + 8]
    return total


def norm_rows_backward(inputs, gain_row, upstream):
    average = jnp.mean(inputs, axis=-1, keepdims=True)
    centered = inputs - average
    spread = lax.rsqrt(jnp.mean(centered * centered, axis=-1, keepdims=True) + EPSILON)
    normed = centered * spread
    scaled = upstream * gain_row
    grad = spread * (
        scaled
        - jnp.mean(scaled, axis=-1, keepdims=True)
        - normed * jnp.mean(scaled * normed, axis=-1, keepdims=True)
    )
    return grad, normed


def attention_pair_backward(refs):
    (
        value_ref, context_grad_t_ref, context_grad_ref, query_ref, key_t_ref, probs_ref,
        grads_ref, score_grad_ref, prob_grad_ref, low_ref,
    ) = refs
    length, pair = value_ref.shape
    padded = context_grad_t_ref.shape[1]
    half = pair // 2
    scale = half ** (-0.5)
    feature = lax.broadcasted_iota(jnp.int32, (pair, padded), 0)
    upstream = context_grad_t_ref[...]
    zero = jnp.zeros_like(upstream)
    prob_grad_ref[0] = dot_plain(value_ref[...], jnp.where(feature < half, upstream, zero))
    prob_grad_ref[1] = dot_plain(value_ref[...], jnp.where(feature < half, zero, upstream))
    for part in range(padded // LANES):
        lanes = slice(part * LANES, (part + 1) * LANES)
        for side in range(2):
            probs = probs_ref[side, :, lanes].astype(jnp.float32)
            prob_grad = prob_grad_ref[side, :, lanes]
            inner = jnp.sum(probs * prob_grad, axis=0, keepdims=True)
            score_grad = probs * (prob_grad - inner)
            score_grad_ref[part, side] = score_grad
            low_ref[side, :, lanes] = score_grad.astype(jnp.bfloat16)
    grad_query_t = jnp.concatenate(
        [
            dot_plain(key_t_ref[side * half : (side + 1) * half, :], low_ref[side])
            for side in range(2)
        ],
        axis=0,
    )
    grads_ref[0] = (grad_query_t * scale).astype(jnp.bfloat16).T[0:length]
    first_half = lax.broadcasted_iota(jnp.int32, (length, pair), 1) < half
    grad_key = [dot_plain(low_ref[side], query_ref[...]) for side in range(2)]
    grads_ref[1] = jnp.where(first_half, grad_key[0], grad_key[1]).astype(jnp.bfloat16)
    grad_value = [dot_plain(probs_ref[side], context_grad_ref[...]) for side in range(2)]
    grads_ref[2] = jnp.where(first_half, grad_value[0], grad_value[1]).astype(jnp.bfloat16)


class FeedInputs(typing.NamedTuple):
    full_in: typing.Any
    full_down: typing.Any
    full_out: typing.Any
    second_sum: typing.Any
    cotangent: typing.Any
    first_sum: typing.Any
    first_low: typing.Any
    active_t: typing.Any
    slope: typing.Any
    probs: typing.Any
    queries: typing.Any
    keys_t: typing.Any
    values: typing.Any
    vectors: typing.Any


class FeedOutputs(typing.NamedTuple):
    shard_in: typing.Any
    shard_down: typing.Any
    output: typing.Any
    grad_first_sum: typing.Any
    branch_grad: typing.Any
    grad_mixed: typing.Any
    score_grad: typing.Any
    sums: typing.Any
    hidden_sums: typing.Any


class FeedRefs(typing.NamedTuple):
    full_in: typing.Any
    full_down: typing.Any
    full_out: typing.Any
    second_sum: typing.Any
    cotangent: typing.Any
    first_sum: typing.Any
    first_low: typing.Any
    active_t: typing.Any
    slope: typing.Any
    probs: typing.Any
    queries: typing.Any
    keys_t: typing.Any
    values: typing.Any
    vectors: typing.Any
    shard_in: typing.Any
    shard_down: typing.Any
    output: typing.Any
    grad_first_sum: typing.Any
    branch_grad: typing.Any
    grad_mixed: typing.Any
    score_grad: typing.Any
    sums: typing.Any
    hidden_sums: typing.Any
    own_sem: typing.Any
    send: typing.Any
    recv: typing.Any
    load_sem: typing.Any
    store_sem: typing.Any
    chunk_sem: typing.Any
    probs_sem: typing.Any
    grads_sem: typing.Any
    score_sem: typing.Any
    s_stage: typing.Any
    s_in: typing.Any
    s_down: typing.Any
    s_grad: typing.Any
    s_low: typing.Any
    s_vectors: typing.Any
    s_sums: typing.Any
    s_hidden: typing.Any
    s_branch: typing.Any


def feed_backward_kernel(waves, *refs):
    r = FeedRefs(*refs[: len(FeedRefs._fields)])
    buffers = refs[len(FeedRefs._fields) :]
    place, core = coordinates()
    length, width = r.s_low.shape
    hidden_units = r.s_hidden.shape[1]
    padded = r.probs.shape[2]
    chunk = 512
    down_waves = sum(wave[0] == 1 for wave in waves)
    loads = {}

    def load(source, target, number):
        made = pltpu.make_async_copy(source, target, r.load_sem.at[number])
        made.start()
        loads[number] = made

    load(r.vectors, r.s_vectors, 0)
    greet(place, core)
    counts = [len(scatter_scratch([wave], [jnp.bfloat16] * 2)) for wave in waves]
    offsets = [sum(counts[:number]) for number in range(len(waves))]

    def steps_of(number, stage):
        mine = iter(buffers[offsets[number] : offsets[number] + counts[number]])
        return scatter_steps(
            waves[number], number, stage,
            r.s_down if waves[number][0] == 1 else r.s_in, mine,
            r.own_sem, r.send, r.recv, place, core,
        )

    steps = [None] * len(waves)
    for number in range(len(waves)):
        steps[number] = steps_of(number, r.s_stage.at[number % 2])
    communicate, last = step_runner(steps, list(range(len(waves))))
    stores = []

    def store(scratch, out, number):
        made = pltpu.make_async_copy(scratch, out, r.store_sem.at[number])
        made.start()
        stores.append(made)
        return made

    loads[0].wait()
    gains = [r.s_vectors[6:7, :], r.s_vectors[7:8, :]]
    tile = 32
    nothing = jnp.zeros((8, width), jnp.float32)

    def feed_phase(
        s_second, s_cot, s_out, s_active, s_low_rows, s_low_t, s_wd, s_wi, s_slope
    ):
        load(r.second_sum, s_second, 2)
        load(r.cotangent, s_cot, 3)
        load(r.active_t, s_active, 4)
        load(r.first_low, s_low_rows, 5)

        def chunk_copies(number, slot):
            columns = pl.ds(pl.multiple_of(number * chunk, chunk), chunk)
            return [
                pltpu.make_async_copy(
                    r.full_down.at[columns], s_wd.at[slot], r.chunk_sem.at[slot, 0]
                ),
                pltpu.make_async_copy(
                    r.full_in.at[:, columns], s_wi.at[slot], r.chunk_sem.at[slot, 1]
                ),
                pltpu.make_async_copy(
                    r.slope.at[:, columns], s_slope.at[slot], r.chunk_sem.at[slot, 2]
                ),
            ]

        for copy in chunk_copies(0, 0):
            copy.start()
        loads[2].wait()
        loads[3].wait()

        def one_norm(number, carry):
            rows = pl.ds(pl.multiple_of(number * tile, tile), tile)
            upstream = s_cot[rows, :].astype(jnp.float32)
            grad, normed = norm_rows_backward(s_second[rows, :], gains[1], upstream)
            s_out[rows, :] = (normed * gains[1] + r.s_vectors[5:6, :]).astype(jnp.bfloat16)
            r.s_grad[rows, :] = grad
            low = grad.astype(jnp.bfloat16)
            r.s_low[rows, :] = low
            return (
                carry[0] + fold_rows(low.astype(jnp.float32)),
                carry[1] + fold_rows(upstream),
                carry[2] + fold_rows(upstream * normed),
            )

        sums = lax.fori_loop(0, length // tile, one_norm, (nothing, nothing, nothing))
        for row, total in zip((3, 5, 7), sums):
            r.s_sums[row : row + 1, :] = jnp.sum(total, axis=0, keepdims=True)
        store(s_out, r.output, 0)
        loads[4].wait()
        rows_each = waves[0][2]
        spots = list(itertools.product(range(DIMS[1]), range(DIMS[2]), range(2)))

        def to_stage(stage, plane, product, rows, columns):
            for block, spot in enumerate(spots):
                stage[(plane,) + spot + (slice(None), columns)] = product[
                    block * rows : (block + 1) * rows
                ].astype(jnp.bfloat16)

        for number in range(down_waves):
            first_row = waves[number][1]

            def one_down(plane, carry, number=number, first_row=first_row):
                group = pl.ds(plane * len(spots), len(spots))
                units = s_active[group, first_row : first_row + rows_each, :]
                product = dot_plain(
                    units.reshape(len(spots) * rows_each, length), r.s_low[...]
                )
                to_stage(r.s_stage.at[number % 2], plane, product, rows_each, slice(None))
                return carry

            lax.fori_loop(0, DIMS[0], one_down, 0)
            communicate(number)
        loads[5].wait()
        s_low_t[...] = s_low_rows[...].T
        in_rows = waves[down_waves][2]
        per_wave = (waves[down_waves][3][-1] - waves[down_waves][3][0]) // chunk
        for number in range(down_waves, len(waves)):

            def one_piece(piece, carry, number=number):
                index = (number - down_waves) * per_wave + piece
                slot = lax.rem(index, 2)

                @pl.when(index + 1 < hidden_units // chunk)
                def fetch():
                    for copy in chunk_copies(index + 1, 1 - slot):
                        copy.start()

                for copy in chunk_copies(index, slot):
                    copy.wait()
                hidden_grad = dot_last(r.s_low[...], s_wd[slot]) * s_slope[slot].astype(
                    jnp.float32
                )
                low = hidden_grad.astype(jnp.bfloat16)
                here = pl.ds(pl.multiple_of(index * chunk, chunk), chunk)
                r.s_hidden[:, here] = jnp.sum(
                    low.astype(jnp.float32), axis=0, keepdims=True
                )
                there = pl.ds(pl.multiple_of(piece * chunk, chunk), chunk)
                size = len(spots) * in_rows
                for plane in range(DIMS[0]):
                    product = dot_plain(s_low_t[plane * size : (plane + 1) * size, :], low)
                    to_stage(r.s_stage.at[number % 2], plane, product, in_rows, there)
                r.s_grad[...] = r.s_grad[...] + dot_last(low, s_wi[slot])
                return carry

            lax.fori_loop(0, per_wave, one_piece, 0)
            communicate(number)
        stores[0].wait()

    bf, full32 = jnp.bfloat16, jnp.float32
    pl.run_scoped(
        feed_phase,
        pltpu.VMEM((length, width), full32),
        pltpu.VMEM((length, width), bf),
        pltpu.VMEM((length, width), bf),
        pltpu.VMEM(r.active_t.shape, bf),
        pltpu.VMEM((length, width), bf),
        pltpu.VMEM((width, length), bf),
        pltpu.VMEM((2, chunk, width), bf),
        pltpu.VMEM((2, width, chunk), bf),
        pltpu.VMEM((2, length, chunk), bf),
    )
    now = len(waves)
    pairs = H // 2
    pair = width // pairs

    def norm_phase(s_first):
        load(r.first_sum, s_first, 1)
        loads[1].wait()

        def one_norm(number, carry):
            rows = pl.ds(pl.multiple_of(number * tile, tile), tile)
            upstream = r.s_grad[rows, :]
            grad, normed = norm_rows_backward(s_first[rows, :], gains[0], upstream)
            r.s_grad[rows, :] = grad
            low = grad.astype(jnp.bfloat16)
            r.s_branch[rows, :] = low
            return (
                carry[0] + fold_rows(low.astype(jnp.float32)),
                carry[1] + fold_rows(upstream),
                carry[2] + fold_rows(upstream * normed),
            )

        sums = lax.fori_loop(0, length // tile, one_norm, (nothing, nothing, nothing))
        for row, total in zip((2, 4, 6), sums):
            r.s_sums[row : row + 1, :] = jnp.sum(total, axis=0, keepdims=True)

    pl.run_scoped(norm_phase, pltpu.VMEM((length, width), full32))
    store(r.s_grad, r.grad_first_sum, 1)
    store(r.s_branch, r.branch_grad, 2)
    communicate(now)

    def attention_phase(
        s_wout, s_context_grad, s_context_grad_t, s_query, s_key_t, s_value, s_probs, s_prob_grad,
        s_low, s_score, s_grads,
    ):
        load(r.full_out, s_wout, 6)
        load(r.queries, s_query, 7)
        load(r.keys_t, s_key_t, 8)
        load(r.values, s_value, 9)

        def probs_copy(number, slot):
            return pltpu.make_async_copy(
                r.probs.at[pl.ds(2 * number, 2)], s_probs.at[slot], r.probs_sem.at[slot]
            )

        def score_copy(number, slot):
            return pltpu.make_async_copy(
                s_score.at[slot], r.score_grad.at[:, pl.ds(2 * number, 2)],
                r.score_sem.at[slot],
            )

        def grads_copy(number, slot, part):
            columns = pl.ds(pl.multiple_of(part * width + number * pair, pair), pair)
            return pltpu.make_async_copy(
                s_grads.at[slot, part], r.grad_mixed.at[:, columns],
                r.grads_sem.at[slot, part],
            )

        probs_copy(0, 0).start()
        loads[6].wait()
        s_context_grad[length:, :] = jnp.zeros((padded - length, width), bf)
        s_context_grad[0:length, :] = dot_last(r.s_branch[...], s_wout[...]).astype(bf)
        s_context_grad_t[...] = s_context_grad[...].T
        communicate(now + 1)
        for number in (7, 8, 9):
            loads[number].wait()

        def one_pair(number, carry):
            slot = lax.rem(number, 2)
            probs_copy(number, slot).wait()

            @pl.when(number + 1 < pairs)
            def fetch():
                probs_copy(number + 1, 1 - slot).start()

            @pl.when(number >= 2)
            def free():
                score_copy(number - 2, slot).wait()
                for part in range(3):
                    grads_copy(number - 2, slot, part).wait()

            mine = pl.ds(pl.multiple_of(number * pair, pair), pair)
            attention_pair_backward(
                (
                    s_value.at[:, mine], s_context_grad_t.at[mine], s_context_grad.at[:, mine],
                    s_query.at[:, mine], s_key_t.at[mine], s_probs.at[slot], s_grads.at[slot],
                    s_score.at[slot], s_prob_grad, s_low,
                )
            )
            for row, part in ((0, 0), (1, 2)):
                r.s_sums[row : row + 1, mine] = jnp.sum(
                    s_grads[slot, part].astype(full32), axis=0, keepdims=True
                )
            score_copy(number, slot).start()
            for part in range(3):
                grads_copy(number, slot, part).start()
            for turn in range(pairs):
                if now + 2 + turn <= last:
                    @pl.when(number == turn)
                    def talk(turn=turn):
                        communicate(now + 2 + turn)

            return carry

        lax.fori_loop(0, pairs, one_pair, 0)
        for number in (pairs - 2, pairs - 1):
            score_copy(number, number % 2).wait()
            for part in range(3):
                grads_copy(number, number % 2, part).wait()

    pl.run_scoped(
        attention_phase,
        pltpu.VMEM((width, width), bf),
        pltpu.VMEM((padded, width), bf),
        pltpu.VMEM((width, padded), bf),
        pltpu.VMEM((padded, width), bf),
        pltpu.VMEM((width, length), bf),
        pltpu.VMEM((length, width), bf),
        pltpu.VMEM((2, 2, length, padded), bf),
        pltpu.VMEM((2, length, padded), full32),
        pltpu.VMEM((2, length, padded), bf),
        pltpu.VMEM((2, padded // LANES, 2, length, LANES), full32),
        pltpu.VMEM((2, 3, length, pair), bf),
    )
    for slot in range(now + 2 + pairs, last + 1):
        communicate(slot)
    store(r.s_sums, r.sums, 3)
    store(r.s_hidden, r.hidden_sums, 4)
    store(r.s_in, r.shard_in, 5)
    store(r.s_down, r.shard_down, 6)
    for made in stores[1:]:
        made.wait()


def feed_backward(inputs, in_shape, down_shape, collective):
    length, width = inputs.first_sum.shape
    hidden_units = inputs.slope.shape[1]
    padded = inputs.probs.shape[2]
    bf, full32 = jnp.bfloat16, jnp.float32
    shape = jax.ShapeDtypeStruct
    anywhere = pl.BlockSpec(memory_space=pl.ANY)
    waves = weight_waves(1, down_shape[0], down_shape[1], in_shape[0], 8)
    waves += weight_waves(0, in_shape[0], in_shape[1], in_shape[0], 8)
    outs = [
        shape(in_shape, full32),
        shape(down_shape, full32),
        shape((length, width), bf),
        shape((length, width), full32),
        shape((length, width), bf),
        shape((length, 3 * width), bf),
        shape((padded // LANES, H, length, LANES), full32),
        shape((8, width), full32),
        shape((1, hidden_units), full32),
    ]
    sems = (len(waves), len(GATHER_ORDERS), hops_before(GATHER_ORDERS[0], 3) + 1)
    dma = pltpu.SemaphoreType.DMA
    scratch = [
        dma((len(waves),)), dma(sems), dma(sems), dma((10,)), dma((7,)), dma((2, 3)), dma((2,)),
        dma((2, 3)), dma((2,)),
        pltpu.VMEM((2,) + DIMS + (2, in_shape[0], waves[-1][3][-1] - waves[-1][3][0]), bf),
        pltpu.VMEM(in_shape, full32),
        pltpu.VMEM(down_shape, full32),
        pltpu.VMEM((length, width), full32),
        pltpu.VMEM((length, width), bf),
        pltpu.VMEM((8, width), full32),
        pltpu.VMEM((8, width), full32),
        pltpu.VMEM((1, hidden_units), full32),
        pltpu.VMEM((length, width), bf),
    ] + scatter_scratch(waves, [bf, bf])
    results = pl.pallas_call(
        functools.partial(feed_backward_kernel, waves),
        in_specs=[anywhere] * len(inputs),
        out_specs=[anywhere] * len(outs),
        out_shape=outs,
        scratch_shapes=scratch,
        compiler_params=pltpu.CompilerParams(
            collective_id=collective, has_side_effects=True, vmem_limit_bytes=VMEM_BYTES
        ),
    )(*inputs)
    return FeedOutputs(*results)


class LastInputs(typing.NamedTuple):
    row_in: typing.Any
    grad_mixed: typing.Any
    full_qkv: typing.Any
    context_t: typing.Any
    branch_grad: typing.Any
    score_grad: typing.Any
    packed_t: typing.Any
    grad_first_sum: typing.Any
    sums: typing.Any
    hidden_sums: typing.Any
    starts: typing.Any


class LastOutputs(typing.NamedTuple):
    shard_qkv: typing.Any
    shard_out: typing.Any
    shard_small: typing.Any
    grad_input: typing.Any


class LastRefs(typing.NamedTuple):
    row_in: typing.Any
    grad_mixed: typing.Any
    full_qkv: typing.Any
    context_t: typing.Any
    branch_grad: typing.Any
    score_grad: typing.Any
    packed_t: typing.Any
    grad_first_sum: typing.Any
    sums: typing.Any
    hidden_sums: typing.Any
    starts: typing.Any
    shard_qkv: typing.Any
    shard_out: typing.Any
    shard_small: typing.Any
    grad_input: typing.Any
    own_sem: typing.Any
    send: typing.Any
    recv: typing.Any
    load_sem: typing.Any
    store_sem: typing.Any
    score_sem: typing.Any
    s_stage: typing.Any
    s_small: typing.Any
    s_out_qkv: typing.Any
    s_out_out: typing.Any
    s_out_small: typing.Any
    s_row: typing.Any
    s_row_t: typing.Any
    s_mixed: typing.Any
    s_qkv: typing.Any
    s_context_t: typing.Any
    s_branch: typing.Any
    s_packed: typing.Any
    s_input: typing.Any
    s_sums: typing.Any
    s_hidden: typing.Any
    s_score: typing.Any
    s_work: typing.Any
    s_product: typing.Any


def last_backward_kernel(waves, *refs):
    r = LastRefs(*refs[: len(LastRefs._fields)])
    buffers = iter(refs[len(LastRefs._fields) :])
    place, core = coordinates()
    length, width = r.s_row.shape
    padded = r.s_packed.shape[0] * LANES
    rows_each = waves[0][2]
    loads = {}
    for number, (source, target) in enumerate(
        (
            (r.row_in, r.s_row), (r.grad_mixed, r.s_mixed), (r.context_t, r.s_context_t),
            (r.branch_grad, r.s_branch), (r.packed_t, r.s_packed), (r.full_qkv, r.s_qkv),
            (r.grad_first_sum, r.s_input), (r.sums, r.s_sums), (r.hidden_sums, r.s_hidden),
        )
    ):
        loads[number] = pltpu.make_async_copy(source, target, r.load_sem.at[number])
        loads[number].start()

    def score_copy(block, slot):
        rows = pl.ds(pl.multiple_of(block * GRAD_TILE, GRAD_TILE), GRAD_TILE)
        return pltpu.make_async_copy(
            r.score_grad.at[:, :, rows], r.s_score.at[slot], r.score_sem.at[slot]
        )

    score_copy(0, 0).start()
    greet(place, core)
    results = [r.s_out_qkv, r.s_out_out, r.s_out_small]
    main = len(waves) - 1
    steps = [
        scatter_steps(
            wave, number, r.s_small if number == main else r.s_stage.at[number % 2],
            results[wave[0]], buffers, r.own_sem, r.send, r.recv, place, core,
        )
        for number, wave in enumerate(waves)
    ]
    communicate, last = step_runner(steps, list(range(main)))
    spots = list(itertools.product(range(DIMS[1]), range(DIMS[2]), range(2)))
    size = len(spots) * rows_each
    loads[0].wait()
    r.s_row_t[...] = r.s_row[...].T
    loads[1].wait()
    for number in range(main):
        array, row, rows, bounds = waves[number]
        columns = slice(bounds[0], bounds[-1])
        if array == 1:
            loads[2].wait()
            loads[3].wait()

        def one_plane(plane, carry, array=array, number=number, columns=columns):
            units = pl.ds(pl.multiple_of(plane * size, size), size)
            if array == 0:
                product = dot_plain(r.s_row_t[units, :], r.s_mixed[:, columns])
            else:
                product = dot_plain(
                    r.s_context_t[units, 0:length], r.s_branch[:, columns]
                )
            for block, spot in enumerate(spots):
                r.s_stage[(number % 2, plane) + spot] = product[
                    block * rows_each : (block + 1) * rows_each
                ].astype(jnp.bfloat16)
            return carry

        lax.fori_loop(0, DIMS[0], one_plane, 0)
        communicate(number)
    loads[5].wait()
    loads[6].wait()
    strip = 256
    for start in range(0, width, strip):
        r.s_input[:, start : start + strip] = r.s_input[:, start : start + strip] + dot_last(
            r.s_mixed[...], r.s_qkv[start : start + strip, :]
        )
    stored = pltpu.make_async_copy(r.s_input, r.grad_input, r.store_sem.at[0])
    stored.start()
    communicate(main)
    loads[4].wait()
    parts = padded // LANES
    span = WINDOW_TILES * LANES
    levels = lax.broadcasted_iota(jnp.int32, (LOW_PARTS, span), 0).astype(jnp.bfloat16)
    one = jnp.ones((LOW_PARTS, span), jnp.bfloat16)
    no_one = jnp.zeros((LOW_PARTS, span), jnp.bfloat16)
    nothing = jnp.zeros((H, span), jnp.bfloat16)

    def window(tiles, turn):
        rolled = [pltpu.roll(one_tile, (LANES - turn) & (LANES - 1), 1) for one_tile in tiles]
        kept = lax.broadcasted_iota(jnp.int32, tiles[0].shape, 1) < LANES - turn
        return jnp.concatenate(
            [jnp.where(kept, here, after) for here, after in zip(rolled[:-1], rolled[1:])],
            axis=1,
        )

    def spread_digit(digit, rows):
        as_float = digit.astype(jnp.float32)
        low = jnp.concatenate([as_float, as_float], axis=0).astype(jnp.bfloat16)
        return jnp.concatenate([low] * (rows // 16), axis=0)

    r.s_product[...] = jnp.zeros(r.s_product.shape, jnp.float32)
    blocks = length // GRAD_TILE

    def one_block(block, carry):
        slot = lax.rem(block, 2)

        @pl.when(block + 1 < blocks)
        def fetch():
            score_copy(block + 1, 1 - slot).start()

        score_copy(block, slot).wait()
        r.s_work[...] = r.s_score[slot]
        flat = r.s_work.reshape(parts * H * GRAD_TILE, LANES)

        def one_group(group, total):
            lefts = []
            rights = []
            for offset in range(ROWS_AT_ONCE):
                row = group * ROWS_AT_ONCE + offset
                begin = r.starts[block * GRAD_TILE + row]
                tile = begin // LANES
                turn = lax.rem(begin, LANES)
                grads_parts = []
                packed_parts = []
                for part in range(WINDOW_TILES + 1):
                    which = lax.rem(tile + part, parts)
                    grads_parts.append(
                        flat[pl.ds(which * H * GRAD_TILE + row, H, stride=GRAD_TILE), :]
                    )
                    packed_parts.append(
                        jnp.broadcast_to(
                            r.s_packed[which, pl.ds(block * GRAD_TILE + row, 1), :], (8, LANES)
                        )
                    )
                grads = window(grads_parts, turn).astype(jnp.bfloat16)
                packed = window(packed_parts, turn)
                masked = []
                onehot = []
                for table in range(3):
                    high = spread_digit((packed >> (7 * table + 5)) & (HIGH_PARTS - 1), H)
                    for part in range(HIGH_PARTS):
                        masked.append(jnp.where(high == jnp.bfloat16(part), grads, nothing))
                    low = spread_digit((packed >> (7 * table)) & (LOW_PARTS - 1), LOW_PARTS)
                    onehot.append(jnp.where(low == levels, one, no_one))
                lefts.append(jnp.concatenate(masked, axis=0))
                rights.append(jnp.concatenate(onehot, axis=0))
            return total + dot_last(
                jnp.concatenate(lefts, axis=1), jnp.concatenate(rights, axis=1)
            )

        total = lax.fori_loop(
            0, GRAD_TILE // ROWS_AT_ONCE, one_group, jnp.zeros(r.s_product.shape, jnp.float32)
        )
        r.s_product[...] = r.s_product[...] + total
        for turn in range(blocks):
            if main + 1 + turn <= last:
                @pl.when(block == turn)
                def talk(turn=turn):
                    communicate(main + 1 + turn)

        return carry

    lax.fori_loop(0, blocks, one_block, 0)
    for slot in range(main + 1 + blocks, last + 1):
        communicate(slot)
    loads[7].wait()
    loads[8].wait()
    lane = lax.broadcasted_iota(jnp.int32, (H, LANES), 1)
    product = jnp.concatenate(
        [
            r.s_product[...],
            jnp.zeros((3 * HIGH_PARTS * H, LANES - 3 * LOW_PARTS), jnp.float32),
        ],
        axis=1,
    )
    tables = []
    for table in range(3):
        whole = jnp.zeros((H, LANES), jnp.float32)
        for part in range(HIGH_PARTS):
            start = (table * HIGH_PARTS + part) * H
            turned = pltpu.roll(
                product[start : start + H], ((part - table) * LOW_PARTS) % LANES, 1
            )
            inside = (lane >= part * LOW_PARTS) & (lane < (part + 1) * LOW_PARTS)
            whole = jnp.where(inside, turned, whole)
        tables.append(whole)
    devices = DIMS[0] * DIMS[1] * DIMS[2] * 2
    group = LANES // (width // devices)
    buckets_each = 3 * NB // devices
    empty = jnp.zeros((7, LANES), jnp.float32)
    for device in range(devices):
        spot = (device // 8, (device // 4) % 2, (device // 2) % 2, device % 2)
        columns = slice(device // group * LANES, (device // group + 1) * LANES)
        low = device * buckets_each
        table = low // NB
        mine = tables[table]
        if (low + buckets_each - 1) // NB > table:
            mine = jnp.where(lane >= low - table * NB, mine, tables[table + 1])
        hidden = r.s_hidden[:, device * LANES : (device + 1) * LANES]
        r.s_small[spot] = jnp.concatenate(
            [r.s_sums[:, columns], hidden, empty, mine], axis=0
        )
    for step in steps[main]:
        step()
    stores = [stored]
    for number, (source, target) in enumerate(
        ((r.s_out_qkv, r.shard_qkv), (r.s_out_out, r.shard_out), (r.s_out_small, r.shard_small))
    ):
        stores.append(
            pltpu.make_async_copy(source, target, r.store_sem.at[number + 1])
        )
        stores[-1].start()
    for made in stores:
        made.wait()


def last_backward(inputs, qkv_shape, out_shape, collective):
    length, width = inputs.row_in.shape
    hidden_units = inputs.hidden_sums.shape[1]
    padded = inputs.packed_t.shape[0] * LANES
    bf, full32 = jnp.bfloat16, jnp.float32
    shape = jax.ShapeDtypeStruct
    anywhere = pl.BlockSpec(memory_space=pl.ANY)
    small_rows = 16 + H
    waves = weight_waves(0, qkv_shape[0], qkv_shape[1], qkv_shape[0], 8)
    waves += weight_waves(1, out_shape[0], out_shape[1], out_shape[0], 8)
    waves.append(wave_of(2, 0, small_rows, 0, 1, 0, 0))
    outs = [
        shape(qkv_shape, full32),
        shape(out_shape, full32),
        shape((small_rows, LANES), full32),
        shape((length, width), full32),
    ]
    sems = (len(waves), len(GATHER_ORDERS), hops_before(GATHER_ORDERS[0], 3) + 1)
    dma = pltpu.SemaphoreType.DMA
    scratch = [
        dma((len(waves),)), dma(sems), dma(sems), dma((9,)), dma((4,)), dma((2,)),
        pltpu.VMEM((2,) + DIMS + (2, qkv_shape[0], waves[0][3][-1] - waves[0][3][0]), bf),
        pltpu.VMEM(DIMS + (2, small_rows, LANES), full32),
        pltpu.VMEM(qkv_shape, full32),
        pltpu.VMEM(out_shape, full32),
        pltpu.VMEM((small_rows, LANES), full32),
        pltpu.VMEM((length, width), bf),
        pltpu.VMEM((width, length), bf),
        pltpu.VMEM((length, 3 * width), bf),
        pltpu.VMEM((width, 3 * width), bf),
        pltpu.VMEM((width, padded), bf),
        pltpu.VMEM((length, width), bf),
        pltpu.VMEM((padded // LANES, length, LANES), jnp.int32),
        pltpu.VMEM((length, width), full32),
        pltpu.VMEM((8, width), full32),
        pltpu.VMEM((1, hidden_units), full32),
        pltpu.VMEM((2, padded // LANES, H, GRAD_TILE, LANES), full32),
        pltpu.VMEM((padded // LANES, H, GRAD_TILE, LANES), full32),
        pltpu.VMEM((3 * HIGH_PARTS * H, 3 * LOW_PARTS), full32),
    ] + scatter_scratch(waves, [bf, bf, full32])
    results = pl.pallas_call(
        functools.partial(last_backward_kernel, waves),
        in_specs=[anywhere] * (len(inputs) - 1) + [pl.BlockSpec(memory_space=pltpu.SMEM)],
        out_specs=[anywhere] * len(outs),
        out_shape=outs,
        scratch_shapes=scratch,
        compiler_params=pltpu.CompilerParams(
            collective_id=collective, has_side_effects=True, vmem_limit_bytes=VMEM_BYTES
        ),
    )(*inputs)
    return LastOutputs(*results)


def even_waves(array, shape, tiles, parts):
    return [
        wave_of(array, 0, shape[0], tile * LANES, *parts)
        for tile in range(0, shape[1] // LANES, tiles)
    ]


def split_wave(array, row, rows, column, tiles, turn):
    edge = tiles // 8
    one = (tiles - edge + turn) // 2
    return wave_of(array, row, rows, column, one, tiles - edge - one, edge)


def forward_plan(weights, small):
    w_qkv, w_out, w_in, w_down = weights
    waves = [wave_of(4, 0, small.shape[0], 0, 1, 0, 0)]
    waves += weight_waves(0, w_qkv.shape[0], w_qkv.shape[1], w_qkv.shape[0], 8)
    early = len(waves)
    waves += weight_waves(1, w_out.shape[0], w_out.shape[1], w_out.shape[0], 8)
    waves += weight_waves(2, w_in.shape[0], w_in.shape[1], w_in.shape[0], 8)
    waves += even_waves(3, w_down.shape, 2, (1, 1, 0))
    starts = [(number, 1) if number < early else (number - 2, LAG) for number in range(len(waves))]
    return waves, starts


def weight_waves(array, rows, columns, row_step, tile_step):
    waves = []
    tiles = columns // LANES
    for row in range(0, rows, row_step):
        for tile in range(0, tiles, tile_step):
            size = min(tile_step, tiles - tile)
            waves.append(
                split_wave(array, row, row_step, tile * LANES, size, (len(waves) + array) % 2)
            )
    return waves


def attention_forward_kernel(
    key_ref, query_ref, value_ref, packed_ref, table_ref, mask_ref, probs_ref, context_ref,
    score_ref,
):
    length = key_ref.shape[0]
    padded = packed_ref.shape[1]
    pair = query_ref.shape[0]
    half = pair // 2
    feature = lax.broadcasted_iota(jnp.int32, (pair, padded), 0)
    queries = query_ref[...]
    zero = jnp.zeros_like(queries)
    score_ref[0] = dot_plain(key_ref[...], jnp.where(feature < half, queries, zero))
    score_ref[1] = dot_plain(key_ref[...], jnp.where(feature < half, zero, queries))
    for column in range(0, padded, LANES):
        lanes = slice(column, column + LANES)
        rows = [jnp.broadcast_to(table_ref[t, 0], (8, LANES)) for t in range(3)]
        tops = [jnp.full((8, LANES), 3.0 * MASK_FILL, jnp.float32) for side in range(2)]
        for start in range(0, length, 8):
            here = slice(start, start + 8)
            packed = packed_ref[here, lanes]
            sums = [None, None]
            for table in range(3):
                index = (packed >> (7 * table)) & (NB - 1)
                word = jnp.take_along_axis(rows[table], index, axis=1)
                for side, term in ((0, word >> 16), (1, (word << 16) >> 16)):
                    sums[side] = term if table == 0 else sums[side] + term
            mask = mask_ref[here, lanes]
            for side in range(2):
                scores = score_ref[side, here, lanes] + (
                    sums[side].astype(jnp.float32) * (1.0 / TABLE_STEP) + mask
                )
                score_ref[side, here, lanes] = scores
                tops[side] = jnp.maximum(tops[side], scores)
        for side in range(2):
            top = jnp.max(tops[side], axis=0, keepdims=True)
            exponent = jnp.exp(score_ref[side, :, lanes] - top)
            total = jnp.sum(exponent, axis=0, keepdims=True)
            probs_ref[side, :, lanes] = (exponent * (1.0 / total)).astype(jnp.bfloat16)
    for side in range(2):
        mine = slice(side * half, (side + 1) * half)
        context_ref[mine, :] = dot_plain(value_ref[mine, :], probs_ref[side]).astype(jnp.bfloat16)


def attention_forward(keys, queries_t, values_t, packed, tables, mask):
    length, width = keys.shape
    padded = packed.shape[1]
    pairs = H // 2
    pair = width // pairs
    whole = pl.BlockSpec((length, padded), lambda p: (0, 0))
    return pl.pallas_call(
        attention_forward_kernel,
        grid=(pairs,),
        in_specs=[
            pl.BlockSpec((length, pair), lambda p: (0, p)),
            pl.BlockSpec((pair, padded), lambda p: (p, 0)),
            pl.BlockSpec((pair, length), lambda p: (p, 0)),
            whole,
            pl.BlockSpec((3, 1, 1, NB), lambda p: (0, p, 0, 0)),
            whole,
        ],
        out_specs=[
            pl.BlockSpec((2, length, padded), lambda p: (p, 0, 0)),
            pl.BlockSpec((pair, padded), lambda p: (p, 0)),
        ],
        out_shape=[
            jax.ShapeDtypeStruct((H, length, padded), jnp.bfloat16),
            jax.ShapeDtypeStruct((width, padded), jnp.bfloat16),
        ],
        scratch_shapes=[pltpu.VMEM((2, length, padded), jnp.float32)],
        compiler_params=pltpu.CompilerParams(vmem_limit_bytes=VMEM_BYTES),
    )(keys, queries_t, values_t, packed, tables, mask)


def attention_backward_kernel(
    value_ref, context_grad_t_ref, context_grad_ref, query_ref, key_t_ref, probs_ref,
    grad_query_ref, grad_key_ref, grad_value_ref, score_grad_ref, prob_grad_ref, low_ref,
):
    length = value_ref.shape[0]
    pair, padded = context_grad_t_ref.shape
    half = pair // 2
    scale = half ** (-0.5)
    feature = lax.broadcasted_iota(jnp.int32, (pair, padded), 0)
    upstream = context_grad_t_ref[...]
    zero = jnp.zeros_like(upstream)
    prob_grad_ref[0] = dot_plain(value_ref[...], jnp.where(feature < half, upstream, zero))
    prob_grad_ref[1] = dot_plain(value_ref[...], jnp.where(feature < half, zero, upstream))
    for part in range(padded // LANES):
        lanes = slice(part * LANES, (part + 1) * LANES)
        for side in range(2):
            probs = probs_ref[side, :, lanes].astype(jnp.float32)
            prob_grad = prob_grad_ref[side, :, lanes]
            inner = jnp.sum(probs * prob_grad, axis=0, keepdims=True)
            score_grad = probs * (prob_grad - inner)
            score_grad_ref[part, side] = score_grad
            low_ref[side, :, lanes] = score_grad.astype(jnp.bfloat16)
    for side in range(2):
        mine = slice(side * half, (side + 1) * half)
        grad_query_ref[mine, :] = (dot_plain(key_t_ref[mine, :], low_ref[side]) * scale).astype(
            jnp.bfloat16
        )
    first_half = lax.broadcasted_iota(jnp.int32, (length, pair), 1) < half
    grad_key = [dot_plain(low_ref[side], query_ref[...]) for side in range(2)]
    grad_key_ref[...] = jnp.where(first_half, grad_key[0], grad_key[1]).astype(jnp.bfloat16)
    grad_value = [dot_plain(probs_ref[side], context_grad_ref[...]) for side in range(2)]
    grad_value_ref[...] = jnp.where(first_half, grad_value[0], grad_value[1]).astype(jnp.bfloat16)


def attention_backward(values, context_grad_t, context_grad, queries, keys_t, probs):
    length, width = values.shape
    padded = probs.shape[2]
    pairs = H // 2
    pair = width // pairs
    natural = pl.BlockSpec((length, pair), lambda p: (0, p))
    longer = pl.BlockSpec((padded, pair), lambda p: (0, p))
    flipped = pl.BlockSpec((pair, padded), lambda p: (p, 0))
    return pl.pallas_call(
        attention_backward_kernel,
        grid=(pairs,),
        in_specs=[
            natural,
            flipped,
            longer,
            longer,
            pl.BlockSpec((pair, length), lambda p: (p, 0)),
            pl.BlockSpec((2, length, padded), lambda p: (p, 0, 0)),
        ],
        out_specs=[
            flipped,
            natural,
            natural,
            pl.BlockSpec((padded // LANES, 2, length, LANES), lambda p: (0, p, 0, 0)),
        ],
        out_shape=[
            jax.ShapeDtypeStruct((width, padded), jnp.bfloat16),
            jax.ShapeDtypeStruct((length, width), jnp.bfloat16),
            jax.ShapeDtypeStruct((length, width), jnp.bfloat16),
            jax.ShapeDtypeStruct((padded // LANES, H, length, LANES), jnp.float32),
        ],
        scratch_shapes=[
            pltpu.VMEM((2, length, padded), jnp.float32),
            pltpu.VMEM((2, length, padded), jnp.bfloat16),
        ],
        compiler_params=pltpu.CompilerParams(vmem_limit_bytes=VMEM_BYTES),
    )(values, context_grad_t, context_grad, queries, keys_t, probs)


def table_grad_kernel(digit_ref, score_grad_ref, out_ref):
    padded = score_grad_ref.shape[0] * LANES

    @pl.when(pl.program_id(0) == 0)
    def start():
        out_ref[...] = jnp.zeros_like(out_ref)

    levels = lax.broadcasted_iota(jnp.int32, (LOW_PARTS, padded), 0).astype(jnp.bfloat16)
    one = jnp.ones((LOW_PARTS, padded), jnp.bfloat16)
    no_one = jnp.zeros((LOW_PARTS, padded), jnp.bfloat16)
    nothing = jnp.zeros((H, padded), jnp.bfloat16)
    flat_ref = score_grad_ref.reshape(padded // LANES * H * GRAD_TILE, LANES)

    def one_group(group, total):
        for offset in range(4):
            row = group * 4 + offset
            grads = jnp.concatenate(
                [
                    flat_ref[pl.ds(part * H * GRAD_TILE + row, H, stride=GRAD_TILE), :]
                    for part in range(padded // LANES)
                ],
                axis=1,
            ).astype(jnp.bfloat16)
            masked = []
            onehot = []
            for table in range(3):
                high = jnp.broadcast_to(digit_ref[row, table : table + 1, :], (H, padded))
                for part in range(HIGH_PARTS):
                    masked.append(jnp.where(high == jnp.bfloat16(part), grads, nothing))
                low = jnp.broadcast_to(digit_ref[row, 3 + table : 4 + table, :], (LOW_PARTS, padded))
                onehot.append(jnp.where(low == levels, one, no_one))
            total = total + dot_last(jnp.concatenate(masked, axis=0), jnp.concatenate(onehot, axis=0))
        return total

    out_ref[...] += lax.fori_loop(
        0, GRAD_TILE // 4, one_group, jnp.zeros(out_ref.shape, jnp.float32)
    )


def table_grads(digits, score_grad):
    length = score_grad.shape[2]
    padded = score_grad.shape[0] * LANES
    shape = (3 * HIGH_PARTS * H, 3 * LOW_PARTS)
    products = pl.pallas_call(
        table_grad_kernel,
        grid=(length // GRAD_TILE,),
        in_specs=[
            pl.BlockSpec((GRAD_TILE, 6, padded), lambda i: (i, 0, 0)),
            pl.BlockSpec((padded // LANES, H, GRAD_TILE, LANES), lambda i: (0, 0, i, 0)),
        ],
        out_specs=pl.BlockSpec(shape, lambda i: (0, 0)),
        out_shape=jax.ShapeDtypeStruct(shape, jnp.float32),
        compiler_params=pltpu.CompilerParams(vmem_limit_bytes=VMEM_BYTES),
    )(digits, score_grad)
    split = products.reshape(3, HIGH_PARTS, H, 3, LOW_PARTS)
    return jnp.stack(
        [jnp.transpose(split[t, :, :, t, :], (0, 2, 1)).reshape(NB, H) for t in range(3)]
    )


def norm_backward(inputs, gain_row, upstream):
    average = jnp.mean(inputs, axis=-1, keepdims=True)
    centered = inputs - average
    spread = lax.rsqrt(jnp.mean(centered * centered, axis=-1, keepdims=True) + EPSILON)
    normed = centered * spread
    scaled = upstream * gain_row
    grad = spread * (
        scaled
        - jnp.mean(scaled, axis=-1, keepdims=True)
        - normed * jnp.mean(scaled * normed, axis=-1, keepdims=True)
    )
    return grad, jnp.sum(upstream * normed, axis=0), jnp.sum(upstream, axis=0)


def spread_small(everything, vec_bias, norm_gain, bias_hidden):
    devices = everything.shape[0]
    vec_size, gain_size = vec_bias.size, norm_gain.size
    vectors, gains, hidden, tables = jnp.split(
        everything, [vec_size, vec_size + gain_size, vec_size + gain_size + bias_hidden.size], axis=1
    )
    vectors = jnp.transpose(vectors.reshape(devices, vec_bias.shape[0], -1), (1, 0, 2))
    gains = jnp.transpose(gains.reshape(devices, norm_gain.shape[0], -1), (1, 0, 2))
    rows = jnp.concatenate(
        [vectors.reshape(vec_bias.shape[0], -1), gains.reshape(norm_gain.shape[0], -1)], axis=0
    )
    return rows.astype(jnp.float32), hidden.reshape(-1).astype(jnp.float32), tables.reshape(3, NB, H)


def forward_by_ops(
    weights, row_in, buckets, segments, validity, vec_bias, norm_gain, bias_hidden, rel_tables
):
    length, width = row_in.shape
    padded = -(-length // LANES) * LANES
    scale = (width // H) ** (-0.5)
    full = [lax.all_gather(weight, BOTH, axis=0, tiled=True) for weight in weights]
    small = jnp.concatenate(
        [vec_bias.reshape(-1), norm_gain.reshape(-1), bias_hidden, rel_tables]
    )
    everything = lax.all_gather(small, BOTH, axis=0, tiled=False)
    vectors, hidden_bias, tables = spread_small(everything, vec_bias, norm_gain, bias_hidden)
    wide = ((0, 0), (0, padded - length))
    flipped = jnp.swapaxes(buckets, 1, 2)
    packed = jnp.pad(flipped[0] | (flipped[1] << 7) | (flipped[2] << 14), wide)
    position = jnp.arange(length)
    allowed = (segments[:, None] == segments[None, :]) & (
        (validity[:, None] > 0) | (position[:, None] == position[None, :])
    )
    mask = jnp.pad(jnp.where(allowed, 0.0, MASK_FILL), wide)
    fixed = jnp.round(tables.astype(jnp.float32) * TABLE_STEP).astype(jnp.int32)
    pair_tables = (fixed[:, :, 0::2] << 16) | (fixed[:, :, 1::2] & 0xFFFF)
    pair_tables = jnp.transpose(pair_tables, (0, 2, 1))[:, :, None, :]
    mixed = dot_plain(row_in, full[0])
    queries = (mixed[:, :width] + vectors[0]).astype(jnp.bfloat16) * jnp.bfloat16(scale)
    keys = mixed[:, width : 2 * width].astype(jnp.bfloat16)
    values = (mixed[:, 2 * width :] + vectors[1]).astype(jnp.bfloat16)
    queries = jnp.pad(queries, ((0, padded - length), (0, 0)))
    probs, context_t = attention_forward(keys, queries.T, values.T, packed, pair_tables, mask)
    branch = dot_first(context_t[:, :length], full[1])
    first_sum = row_in.astype(jnp.float32) + branch + vectors[2]
    normed_first = layer_norm(first_sum, vectors[6], vectors[4])
    first_low = normed_first.astype(jnp.bfloat16)
    hidden = dot_plain(first_low, full[2]) + hidden_bias
    active, slope = gelu_and_slope(hidden)
    active = active.astype(jnp.bfloat16)
    second_sum = normed_first + dot_plain(active, full[3]) + vectors[3]
    return full + [
        probs, context_t, queries, keys.T, values, first_sum, first_low, active, slope,
        second_sum, vectors, packed,
    ]


class Kept(typing.NamedTuple):
    full_qkv: typing.Any
    full_out: typing.Any
    full_in: typing.Any
    full_down: typing.Any
    probs: typing.Any
    context_t: typing.Any
    queries: typing.Any
    keys_t: typing.Any
    values: typing.Any
    first_sum: typing.Any
    first_low: typing.Any
    active_t: typing.Any
    slope: typing.Any
    second_sum: typing.Any
    vectors: typing.Any
    packed_t: typing.Any


def body(
    own_kernels, block_input, cotangent, seg_ids, slot_valid, rel_buckets, w_qkv, w_out, w_in,
    w_down, vec_bias, norm_gain, bias_hidden, rel_tables,
):
    row_in = block_input[0]
    row_cot = cotangent[0].astype(jnp.float32)
    length, width = row_in.shape
    devices = lax.axis_size(BOTH)
    weights = [w_qkv, w_out, w_in, w_down]
    if own_kernels:
        device = lax.axis_index("dp") * 2 + lax.axis_index("fsdp")
        small = small_block(device, vec_bias, norm_gain, bias_hidden, rel_tables)
        waves, starts = forward_plan(weights, small)
        forward = forward_all(
            weights, small, row_in, rel_buckets[0], seg_ids[0], slot_valid[0], waves, starts, 1
        )
        forward = [whole.reshape(-1, whole.shape[-1]) for whole in forward[:4]] + list(forward[4:])
    else:
        forward = forward_by_ops(
            weights, row_in, rel_buckets[0], seg_ids[0], slot_valid[0], vec_bias, norm_gain,
            bias_hidden, rel_tables,
        )
    if own_kernels:
        kept = Kept(*forward)
        fed = feed_backward(
            FeedInputs(
                kept.full_in, kept.full_down, kept.full_out, kept.second_sum, cotangent[0],
                kept.first_sum, kept.first_low, kept.active_t, kept.slope, kept.probs,
                kept.queries, kept.keys_t, kept.values, kept.vectors,
            ),
            w_in.shape, w_down.shape, 2,
        )
        segments = seg_ids[0]
        starts = jnp.sum(segments[None, :] < segments[:, None], axis=1, dtype=jnp.int32)
        done = last_backward(
            LastInputs(
                row_in, fed.grad_mixed, kept.full_qkv, kept.context_t, fed.branch_grad,
                fed.score_grad, kept.packed_t, fed.grad_first_sum, fed.sums, fed.hidden_sums,
                starts,
            ),
            w_qkv.shape, w_out.shape, 3,
        )
        small = done.shard_small
        piece = vec_bias.shape[1]
        vec_rows = vec_bias.shape[0]
        sums = lax.dynamic_slice(
            small, (0, device % (LANES // piece) * piece), (8, piece)
        )
        buckets_each = rel_tables.shape[0] // H
        twice = jnp.concatenate([small[16:], small[16:]], axis=1)
        tables = lax.dynamic_slice(twice, (0, device * buckets_each % NB), (H, buckets_each))
        return (
            fed.output[None],
            done.grad_input[None],
            done.shard_qkv,
            done.shard_out,
            fed.shard_in,
            fed.shard_down,
            sums[:vec_rows],
            sums[vec_rows:],
            small[8],
            tables.T.reshape(-1),
        )
    (
        full_qkv, full_out, full_in, full_down, probs, context_t, queries, keys_t, values,
        first_sum, first_low, active, slope, second_sum, vectors, packed,
    ) = forward
    padded = packed.shape[1]
    gains = vectors[6:8]
    taller = ((0, padded - length), (0, 0))
    context_t = context_t[:, :length]
    digits = jnp.stack(
        [
            (packed >> (7 * t + shift)) & mask
            for shift, mask in ((5, HIGH_PARTS - 1), (0, LOW_PARTS - 1))
            for t in range(3)
        ],
        axis=1,
    ).astype(jnp.bfloat16)
    output = layer_norm(second_sum, gains[1], vectors[5]).astype(jnp.bfloat16)

    grad_second, grad_gain_two, grad_shift_two = norm_backward(second_sum, gains[1], row_cot)
    down_grad = grad_second.astype(jnp.bfloat16)
    grad_w_down = dot_first(active, down_grad).astype(jnp.bfloat16)
    hidden_grad = (dot_last(down_grad, full_down) * slope.astype(jnp.float32)).astype(jnp.bfloat16)
    grad_w_in = dot_first(first_low, hidden_grad).astype(jnp.bfloat16)
    grad_first = dot_last(hidden_grad, full_in) + grad_second
    grad_first_sum, grad_gain_one, grad_shift_one = norm_backward(first_sum, gains[0], grad_first)
    branch_grad = grad_first_sum.astype(jnp.bfloat16)
    grad_w_out = dot_plain(context_t, branch_grad).astype(jnp.bfloat16)
    context_grad = jnp.pad(dot_last(branch_grad, full_out).astype(jnp.bfloat16), taller)
    grad_queries_t, grad_keys, grad_values, score_grad = attention_backward(
        values, context_grad.T, context_grad, queries, keys_t, probs
    )
    grad_queries = grad_queries_t[:, :length].T
    grad_mixed = jnp.concatenate([grad_queries, grad_keys, grad_values], axis=1)
    grad_w_qkv = dot_first(row_in, grad_mixed).astype(jnp.bfloat16)
    grad_input = grad_first_sum + dot_last(grad_mixed, full_qkv)
    grad_tables = table_grads(digits, score_grad)

    grad_vectors = jnp.stack(
        [
            jnp.sum(grad_queries.astype(jnp.float32), axis=0),
            jnp.sum(grad_values.astype(jnp.float32), axis=0),
            jnp.sum(branch_grad.astype(jnp.float32), axis=0),
            jnp.sum(down_grad.astype(jnp.float32), axis=0),
            grad_shift_one,
            grad_shift_two,
        ]
    )
    grad_gains = jnp.stack([grad_gain_one, grad_gain_two])
    grad_hidden_bias = jnp.sum(hidden_grad.astype(jnp.float32), axis=0)

    def by_device(matrix):
        return jnp.transpose(matrix.reshape(matrix.shape[0], devices, -1), (1, 0, 2)).reshape(
            devices, -1
        )

    small_grads = jnp.concatenate(
        [
            by_device(grad_vectors),
            by_device(grad_gains),
            grad_hidden_bias.reshape(devices, -1),
            grad_tables.reshape(devices, -1),
        ],
        axis=1,
    )
    weight_grads = [grad_w_qkv, grad_w_out, grad_w_in, grad_w_down]
    shards = [
        lax.psum_scatter(
            grad.astype(jnp.float32), BOTH, scatter_dimension=0, tiled=True
        )
        for grad in weight_grads
    ]
    small_shard = lax.psum_scatter(small_grads, BOTH, scatter_dimension=0, tiled=True)[0]
    shard_vectors, shard_gains, shard_hidden, shard_tables = jnp.split(
        small_shard,
        [
            vec_bias.size,
            vec_bias.size + norm_gain.size,
            vec_bias.size + norm_gain.size + bias_hidden.size,
        ],
    )
    return (
        output[None],
        grad_input[None],
        shards[0],
        shards[1],
        shards[2],
        shards[3],
        shard_vectors.reshape(vec_bias.shape),
        shard_gains.reshape(norm_gain.shape),
        shard_hidden,
        shard_tables,
    )


def solution(mesh):
    rows = P(BOTH)
    columns = P(None, BOTH)
    in_specs = (rows,) * 9 + (columns, columns, rows, rows)
    out_specs = (rows,) * 6 + (columns, columns, rows, rows)
    chips = DIMS[0] * DIMS[1] * DIMS[2]
    own_kernels = mesh.shape["dp"] == chips and mesh.shape["fsdp"] == 2
    return jax.shard_map(
        functools.partial(body, own_kernels),
        mesh=mesh,
        in_specs=in_specs,
        out_specs=out_specs,
        check_vma=False,
    )
```
